32 devices in a mesh: dp: 8 (over z, y), feat: 4 (over x, core).
Axes of the slice: x: 2, y: 2, z: 4, core: 2. Of those that a mesh axis runs over, the one named last changes fastest.
Arguments:
- first_view_outputs: bfloat16 [512, 8192], P('dp', 'feat'), may hold values from -120 to 120
- second_view_outputs: bfloat16 [512, 8192], P('feat', 'dp'), may hold values from -120 to 120
Outputs:
- first_view_gradient: bfloat16 [512, 8192], P('dp', 'feat')
- second_view_gradient: bfloat16 [512, 8192], P('feat', 'dp')
The draws below stay inside these ranges and needn't reach their ends.
All inputs are finite; a program needn't handle non-finite values.
Results may differ from the reference program's by a relative error of at most 0.033.
Values may be sent and summed in bfloat16 or wider, within the bound.
A program may use at most 64 MiB of HBM per device.

```python
import math
import jax
import jax.numpy as jnp
from jax import lax

D = 8192
PAIRS = 512
N_DP = 8
N_FEAT = 4


def shared_parts(key):
    sign_key, level_key, common_key = jax.random.split(key, 3)
    directions = D // 32
    sample_signs = (2 * jax.random.randint(sign_key, (PAIRS, directions), 0, 2) - 1).astype(jnp.float32)
    feature_levels = jax.random.randint(level_key, (directions, D), -3, 4).astype(jnp.float32)
    shared_sum = jnp.dot(sample_signs, feature_levels, precision=lax.Precision.HIGHEST)
    shared = jnp.clip(shared_sum * (1.0 / math.sqrt(4.0 * directions)), -5.0, 5.0)
    common = jnp.clip(jax.random.normal(common_key, (PAIRS, D), jnp.float32), -5.0, 5.0)
    return (shared, common)


def column_frame(key, low_scale, high_scale, offset):
    scale_key, shift_key = jax.random.split(key)
    scales = jnp.exp(jax.random.uniform(scale_key, (1, D), jnp.float32, math.log(low_scale), math.log(high_scale)))
    shifts = jax.random.uniform(shift_key, (1, D), jnp.float32, -offset, offset)
    return (scales, shifts)


def draw_first_view_outputs(key, part):
    shared, common = shared_parts(key)
    key = jax.random.fold_in(key, 11)
    scales, shifts = column_frame(key, 0.5, 4.0, 2.0)
    return (shifts + scales * (shared + common)).astype(jnp.bfloat16)


def draw_second_view_outputs(key, part):
    shared, common = shared_parts(key)
    key = jax.random.fold_in(key, 12)
    noise_key, frame_key = jax.random.split(key)
    noise_part = jnp.clip(jax.random.normal(noise_key, (PAIRS, D), jnp.float32), -5.0, 5.0)
    scales, shifts = column_frame(frame_key, 0.5, 4.0, 2.0)
    return (shifts + scales * (shared + 0.7 * common + 0.7 * noise_part)).astype(jnp.bfloat16)


def setup_inputs(seed: int = 0) -> dict:
    key_of = jax.random.split(jax.random.key(seed), 3)
    return {
        "first_view_outputs": draw_first_view_outputs(jax.random.fold_in(key_of[2], 71), 0),
        "second_view_outputs": draw_second_view_outputs(jax.random.fold_in(key_of[2], 71), 0),
    }


EPSILON = 1e-05
OFF_WEIGHT = 0.0051

def standardize_columns(values_in):
    values = values_in.astype(jnp.float32)
    center = lax.optimization_barrier(jnp.mean(values, axis=0))
    shifted = values - center
    spread = lax.optimization_barrier(jnp.mean(shifted * shifted, axis=0))
    inverse_scale = lax.rsqrt(spread + EPSILON)
    return (shifted * inverse_scale, inverse_scale)

def normalize_backward(normalized_gradient, standardized_values, inverse_scale):
    centering_term = lax.optimization_barrier(jnp.mean(normalized_gradient, axis=0))
    projection_term = lax.optimization_barrier(jnp.mean(normalized_gradient * standardized_values, axis=0))
    return ((normalized_gradient - centering_term - standardized_values * projection_term) * inverse_scale).astype(jnp.bfloat16)

def reference(first_view_outputs, second_view_outputs):
    standardized_first, inverse_deviation_first = standardize_columns(first_view_outputs)
    standardized_second, inverse_deviation_second = standardize_columns(second_view_outputs)
    normalized_first = standardized_first.astype(jnp.bfloat16)
    normalized_second = standardized_second.astype(jnp.bfloat16)
    row_width = D // N_FEAT
    col_width = D // N_DP

    def row_block(running, block_index):
        row_start = block_index * row_width
        left_cols = lax.dynamic_slice_in_dim(normalized_first, row_start, row_width, 1)
        correlation = lax.dot_general(left_cols, normalized_second, (((0,), (0,)), ((), ())), preferred_element_type=jnp.float32) / PAIRS
        row_ids = row_start + lax.broadcasted_iota(jnp.int32, (row_width, D), 0)
        col_ids = lax.broadcasted_iota(jnp.int32, (row_width, D), 1)
        grad_corr = jnp.where(row_ids == col_ids, 2.0 * (correlation - 1.0), 2.0 * OFF_WEIGHT * correlation).astype(jnp.bfloat16)

        def col_block(summed, column_index):
            col_start = column_index * col_width
            right_cols = lax.dynamic_slice_in_dim(normalized_second, col_start, col_width, 1)
            grad_tile = lax.dynamic_slice_in_dim(grad_corr, col_start, col_width, 1)
            partial_term = lax.dot_general(right_cols, grad_tile, (((1,), (1,)), ((), ())), preferred_element_type=jnp.float32)
            rounded = lax.optimization_barrier(partial_term.astype(jnp.bfloat16))
            return (summed + rounded.astype(jnp.float32), None)
        dnorm_block, _ = lax.scan(col_block, jnp.zeros((PAIRS, row_width), jnp.float32), jnp.arange(N_DP, dtype=jnp.int32))
        partial_b = jnp.dot(left_cols, grad_corr, preferred_element_type=jnp.float32)
        rounded_b = lax.optimization_barrier(partial_b.astype(jnp.bfloat16))
        return (running + rounded_b.astype(jnp.float32), dnorm_block)
    normalized_gradient_second, blocks = lax.scan(row_block, jnp.zeros((PAIRS, D), jnp.float32), jnp.arange(N_FEAT, dtype=jnp.int32))
    normalized_gradient_first = jnp.transpose(blocks, (1, 0, 2)).reshape(PAIRS, D)
    return (normalize_backward(normalized_gradient_first, standardized_first, inverse_deviation_first), normalize_backward(normalized_gradient_second, standardized_second, inverse_deviation_second))
```

```python
import functools
import jax
import jax.numpy as jnp
from jax import lax
from jax.experimental import pallas as pl
from jax.experimental.pallas import tpu as pltpu
from jax.sharding import PartitionSpec as P

EPSILON = 1e-05
OFF_WEIGHT = 0.0051
MESH = pl.DeviceIdType.MESH
BLK = 128
GROUP = 4


def normalize_backward(
    normalized_gradient, standardized_values, inverse_scale, column_sums, total_count
):
    centering_term = column_sums[0] / total_count
    projection_term = column_sums[1] / total_count
    return (
        (normalized_gradient - centering_term - standardized_values * projection_term)
        * inverse_scale
    ).astype(jnp.bfloat16)


def general_shards(first_view_outputs, second_view_outputs):
    rows_a, width_a = first_view_outputs.shape
    rows_b, width_b = second_view_outputs.shape
    total_count = rows_a * lax.axis_size("dp")

    def standardize(values, axis):
        local = values.astype(jnp.float32)
        center = lax.psum(jnp.sum(local, axis=0), axis) / total_count
        centered = local - center
        spread = lax.psum(jnp.sum(centered * centered, axis=0), axis) / total_count
        inverse = lax.rsqrt(spread + EPSILON)
        standardized = centered * inverse
        gathered = lax.all_gather(standardized.astype(jnp.bfloat16), axis, axis=0, tiled=True)
        return standardized, inverse, gathered

    standardized_first, inverse_first, normalized_first = standardize(first_view_outputs, "dp")
    standardized_second, inverse_second, normalized_second = standardize(
        second_view_outputs, "feat"
    )
    correlation = (
        lax.dot_general(
            normalized_first,
            normalized_second,
            (((0,), (0,)), ((), ())),
            preferred_element_type=jnp.float32,
        )
        / total_count
    )
    row_ids = lax.axis_index("feat") * width_a + lax.broadcasted_iota(
        jnp.int32, (width_a, width_b), 0
    )
    col_ids = lax.axis_index("dp") * width_b + lax.broadcasted_iota(
        jnp.int32, (width_a, width_b), 1
    )
    grad_tile = jnp.where(
        row_ids == col_ids, 2.0 * (correlation - 1.0), 2.0 * OFF_WEIGHT * correlation
    ).astype(jnp.bfloat16)

    def finish(partial, axis, standardized, inverse):
        gradient = lax.psum_scatter(
            partial.astype(jnp.bfloat16), axis, scatter_dimension=0, tiled=True
        ).astype(jnp.float32)
        sums = lax.psum(
            (jnp.sum(gradient, axis=0), jnp.sum(gradient * standardized, axis=0)), axis
        )
        return normalize_backward(gradient, standardized, inverse, sums, total_count)

    partial_first = lax.dot_general(
        normalized_second,
        grad_tile,
        (((1,), (1,)), ((), ())),
        preferred_element_type=jnp.float32,
    )
    partial_second = jnp.dot(normalized_first, grad_tile, preferred_element_type=jnp.float32)
    return (
        finish(partial_first, "dp", standardized_first, inverse_first),
        finish(partial_second, "feat", standardized_second, inverse_second),
    )


def kernel(
    features,
    chunk,
    a_ref,
    b_ref,
    ga_ref,
    gb_ref,
    raw,
    xhat,
    inv,
    norm,
    other,
    packed,
    r1,
    s1,
    r2,
    gathered,
    full_packed,
    gram,
    grad,
    in_send,
    in_recv,
    swap_send,
    swap_recv,
    rs1_send,
    rs1_recv,
    rs2_send,
    rs2_recv,
    ag1_send,
    ag1_recv,
    ag2_send,
    ag2_recv,
    out_send,
    out_recv,
):
    n_dp, n_feat = 8, 4
    n_dev = n_dp * n_feat
    p = lax.axis_index("dp")
    f = lax.axis_index("feat")
    z, y = p // 2, p % 2
    x, core = f // 2, f % 2
    g = 2 * y + x
    rows_a = a_ref.shape[0]
    rows_b = b_ref.shape[0]
    count, width = raw.shape
    n_chunks = width // chunk
    n_blk = count // BLK
    seg = packed.shape[0] // GROUP
    unit = seg // GROUP

    barrier = pltpu.get_barrier_semaphore()
    me = p * n_feat + f

    def greet(k, carry):
        t = (me + k) % n_dev
        pl.semaphore_signal(
            barrier, inc=1, device_id=(t // n_feat, t % n_feat), device_id_type=MESH
        )
        return carry

    lax.fori_loop(1, n_dev, greet, 0)
    pl.semaphore_wait(barrier, n_dev - 1)

    def start_or_local(src, dst, send_sem, recv_sem, device, is_self):
        cp = pltpu.make_async_remote_copy(
            src_ref=src,
            dst_ref=dst,
            send_sem=send_sem,
            recv_sem=recv_sem,
            device_id=device,
            device_id_type=MESH,
        )

        @pl.when(is_self)
        def _():
            pltpu.make_async_copy(src, dst, recv_sem).start()

        @pl.when(jnp.logical_not(is_self))
        def _():
            cp.start()

        return cp, is_self

    def wait_sent(item):
        cp, is_self = item

        @pl.when(jnp.logical_not(is_self))
        def _():
            cp.wait_send()

    sent = []
    for k in range(GROUP):
        q = (g + k) % GROUP
        dp_to = 2 * f + q // 2
        feat_to = 2 * (q % 2)
        sent.append(
            start_or_local(
                a_ref.at[:, pl.ds(pl.multiple_of(q * width, width), width)],
                raw.at[pl.ds(pl.multiple_of(p * rows_a, rows_a), rows_a), :],
                in_send.at[k],
                in_recv,
                (dp_to, feat_to),
                jnp.logical_and(dp_to == p, feat_to == f),
            )
        )
    for k in range(2):
        x_to = (x + 1 + k) % 2
        feat_to = 2 * x_to + 1
        sent.append(
            start_or_local(
                b_ref.at[:, pl.ds(pl.multiple_of(x_to * width, width), width)],
                raw.at[pl.ds(pl.multiple_of(f * rows_b, rows_b), rows_b), :],
                in_send.at[GROUP + k],
                in_recv,
                (p, feat_to),
                feat_to == f,
            )
        )
    pltpu.make_async_copy(raw, raw, in_recv).wait()

    for c in range(width // BLK):
        cols = slice(c * BLK, (c + 1) * BLK)
        values = raw[:, cols].astype(jnp.float32)
        center = jnp.sum(values, axis=0, keepdims=True) / count
        centered = values - center
        spread = jnp.sum(centered * centered, axis=0, keepdims=True) / count
        inverse = lax.rsqrt(spread + EPSILON)
        standardized = centered * inverse
        xhat[:, cols] = standardized
        norm[:, cols] = standardized.astype(jnp.bfloat16)
        inv[0:1, cols] = inverse

    swap = pltpu.make_async_remote_copy(
        src_ref=norm,
        dst_ref=other,
        send_sem=swap_send,
        recv_sem=swap_recv,
        device_id=(p, 2 * x + 1 - core),
        device_id_type=MESH,
    )

    eye = jnp.where(
        lax.broadcasted_iota(jnp.int32, (BLK, BLK), 0)
        == lax.broadcasted_iota(jnp.int32, (BLK, BLK), 1),
        jnp.float32(width),
        jnp.float32(0),
    )
    index = 0
    where = {}
    for bi in range(n_blk):
        share = lax.dot_general(
            norm[bi * BLK : (bi + 1) * BLK, :],
            norm[bi * BLK :, :],
            (((1,), (1,)), ((), ())),
            preferred_element_type=jnp.float32,
        )
        for bj in range(bi, n_blk):
            block = share[:, (bj - bi) * BLK : (bj - bi + 1) * BLK]
            if bi == bj:
                block = block - eye
            packed[index * BLK : (index + 1) * BLK, :] = block.astype(jnp.bfloat16)
            where[bi, bj] = index
            index += 1

    copies = []
    for k in range(1, GROUP):
        q = (g + k) % GROUP
        cp = pltpu.make_async_remote_copy(
            src_ref=packed.at[pl.ds(pl.multiple_of(q * seg, seg), seg), :],
            dst_ref=r1.at[k - 1],
            send_sem=rs1_send.at[k - 1],
            recv_sem=rs1_recv.at[k - 1],
            device_id=(2 * z + q // 2, 2 * (q % 2) + core),
            device_id_type=MESH,
        )
        cp.start()
        copies.append(cp)
    swap.start()
    total = packed[pl.ds(pl.multiple_of(g * seg, seg), seg), :].astype(jnp.float32)
    for k in range(1, GROUP):
        copies[k - 1].wait_recv()
        total = total + r1[k - 1].astype(jnp.float32)
    s1[...] = total.astype(jnp.bfloat16)
    for k in range(1, GROUP):
        zt = (z + k) % GROUP
        cp = pltpu.make_async_remote_copy(
            src_ref=s1.at[pl.ds(pl.multiple_of(zt * unit, unit), unit), :],
            dst_ref=r2.at[k - 1],
            send_sem=rs2_send.at[k - 1],
            recv_sem=rs2_recv.at[k - 1],
            device_id=(2 * zt + y, f),
            device_id_type=MESH,
        )
        cp.start()
        copies.append(cp)
    mine = pl.ds(pl.multiple_of(z * unit, unit), unit)
    total = s1[mine, :].astype(jnp.float32)
    for k in range(1, GROUP):
        copies[GROUP - 2 + k].wait_recv()
        total = total + r2[k - 1].astype(jnp.float32)
    gathered[mine, :] = total.astype(jnp.bfloat16)

    for k in range(1, GROUP):
        zt = (z + k) % GROUP
        cp = pltpu.make_async_remote_copy(
            src_ref=gathered.at[mine, :],
            dst_ref=gathered.at[mine, :],
            send_sem=ag1_send.at[k - 1],
            recv_sem=ag1_recv.at[k - 1],
            device_id=(2 * zt + y, f),
            device_id_type=MESH,
        )
        cp.start()
        copies.append(cp)
    for k in range(1, GROUP):
        copies[2 * GROUP - 3 + k].wait_recv()
    last = []
    for k in range(1, GROUP + 1):
        q = (g + k) % GROUP
        cp = pltpu.make_async_remote_copy(
            src_ref=gathered,
            dst_ref=full_packed.at[pl.ds(pl.multiple_of(g * seg, seg), seg), :],
            send_sem=ag2_send.at[k - 1],
            recv_sem=ag2_recv.at[k - 1],
            device_id=(2 * z + q // 2, 2 * (q % 2) + 1 - core),
            device_id_type=MESH,
        )
        cp.start()
        last.append(cp)

    swap.wait_recv()
    diagonals = []
    for c in range(n_chunks):
        cols = slice(c * chunk, (c + 1) * chunk)
        corr = (
            jnp.sum(
                norm[:, cols].astype(jnp.float32) * other[:, cols].astype(jnp.float32),
                axis=0,
                keepdims=True,
            )
            / count
        )
        diagonals.append(2.0 * (corr - 1.0) - 2.0 * OFF_WEIGHT * corr)
    for cp in last:
        cp.wait_recv()
    for (bi, bj), at in where.items():
        block = full_packed[at * BLK : (at + 1) * BLK, :]
        gram[bi * BLK : (bi + 1) * BLK, bj * BLK : (bj + 1) * BLK] = block
        if bi != bj:
            gram[bj * BLK : (bj + 1) * BLK, bi * BLK : (bi + 1) * BLK] = block.T

    scale = 2.0 * OFF_WEIGHT / count
    back = []
    for c in range(n_chunks):
        cols = slice(c * chunk, (c + 1) * chunk)
        own = norm[:, cols]
        dnorm = (
            lax.dot_general(
                gram[...], own, (((1,), (0,)), ((), ())), preferred_element_type=jnp.float32
            )
            + features * own.astype(jnp.float32)
        ) * scale + other[:, cols].astype(jnp.float32) * diagonals[c]
        standardized = xhat[:, cols]
        centering = jnp.sum(dnorm, axis=0, keepdims=True) / count
        projection = jnp.sum(dnorm * standardized, axis=0, keepdims=True) / count
        grad[:, cols] = (
            (dnorm - centering - standardized * projection) * inv[0:1, cols]
        ).astype(jnp.bfloat16)

        @pl.when(core == 0)
        def _():
            place = pl.ds(pl.multiple_of(g * width + c * chunk, chunk), chunk)
            for k in range(1, n_dp + 1):
                to = (p + k) % n_dp
                start_or_local(
                    grad.at[pl.ds(pl.multiple_of(to * rows_a, rows_a), rows_a), cols],
                    ga_ref.at[:, place],
                    out_send.at[c, k - 1],
                    out_recv.at[0],
                    (to, z),
                    jnp.logical_and(to == p, z == f),
                )

        @pl.when(core == 1)
        def _():
            place = pl.ds(pl.multiple_of(x * width + c * chunk, chunk), chunk)
            for k in range(1, n_feat + 1):
                to = (f + k) % n_feat
                src = grad.at[pl.ds(pl.multiple_of(to * rows_b, rows_b), rows_b), cols]
                if k == n_feat:
                    pltpu.make_async_copy(src, gb_ref.at[:, place], out_recv.at[1]).start()
                else:
                    pltpu.make_async_remote_copy(
                        src_ref=src,
                        dst_ref=gb_ref.at[:, place],
                        send_sem=out_send.at[c, k - 1],
                        recv_sem=out_recv.at[1],
                        device_id=(p, to),
                        device_id_type=MESH,
                    ).start()

    for item in sent:
        wait_sent(item)
    swap.wait_send()
    for cp in copies + last:
        cp.wait_send()

    @pl.when(core == 0)
    def _():
        for c in range(n_chunks):
            for k in range(1, n_dp + 1):
                to = (p + k) % n_dp
                piece = grad.at[0:rows_a, 0:chunk]

                @pl.when(jnp.logical_not(jnp.logical_and(to == p, z == f)))
                def _():
                    pltpu.make_async_copy(piece, piece, out_send.at[c, k - 1]).wait()

    @pl.when(core == 1)
    def _():
        for c in range(n_chunks):
            for k in range(1, n_feat):
                piece = grad.at[0:rows_b, 0:chunk]
                pltpu.make_async_copy(piece, piece, out_send.at[c, k - 1]).wait()

    pltpu.make_async_copy(ga_ref, ga_ref, out_recv.at[0]).wait()
    pltpu.make_async_copy(gb_ref, gb_ref, out_recv.at[1]).wait()


def owned_shards(first_view_outputs, second_view_outputs):
    count = first_view_outputs.shape[0] * lax.axis_size("dp")
    features = first_view_outputs.shape[1] * lax.axis_size("feat")
    width = first_view_outputs.shape[1] // GROUP
    chunk = 256 if width % 256 == 0 else 128
    n_blk = count // BLK
    packed_rows = n_blk * (n_blk + 1) // 2 * BLK
    seg = packed_rows // GROUP
    unit = seg // GROUP
    bf16, f32 = jnp.bfloat16, jnp.float32
    dma = pltpu.SemaphoreType.DMA
    any_spec = pl.BlockSpec(memory_space=pl.ANY)
    return pl.pallas_call(
        functools.partial(kernel, float(features), chunk),
        out_shape=[
            jax.ShapeDtypeStruct(first_view_outputs.shape, bf16),
            jax.ShapeDtypeStruct(second_view_outputs.shape, bf16),
        ],
        in_specs=[any_spec] * 2,
        out_specs=[any_spec] * 2,
        scratch_shapes=[
            pltpu.VMEM((count, width), bf16),
            pltpu.VMEM((count, width), f32),
            pltpu.VMEM((8, width), f32),
            pltpu.VMEM((count, width), bf16),
            pltpu.VMEM((count, width), bf16),
            pltpu.VMEM((packed_rows, BLK), bf16),
            pltpu.VMEM((GROUP - 1, seg, BLK), bf16),
            pltpu.VMEM((seg, BLK), bf16),
            pltpu.VMEM((GROUP - 1, unit, BLK), bf16),
            pltpu.VMEM((seg, BLK), bf16),
            pltpu.VMEM((packed_rows, BLK), bf16),
            pltpu.VMEM((count, count), bf16),
            pltpu.VMEM((count, width), bf16),
            dma((GROUP + 2,)),
            dma,
            dma,
            dma,
            dma((GROUP - 1,)),
            dma((GROUP - 1,)),
            dma((GROUP - 1,)),
            dma((GROUP - 1,)),
            dma((GROUP - 1,)),
            dma((GROUP - 1,)),
            dma((GROUP,)),
            dma((GROUP,)),
            dma((width // chunk, 8)),
            dma((2,)),
        ],
        compiler_params=pltpu.CompilerParams(
            collective_id=0, has_side_effects=True, vmem_limit_bytes=40 * 1024 * 1024
        ),
        name="owned_columns",
    )(first_view_outputs, second_view_outputs)


def shards(first_view_outputs, second_view_outputs):
    rows_a, width_a = first_view_outputs.shape
    rows_b, width_b = second_view_outputs.shape
    fits = (
        lax.axis_size("dp") == 8
        and lax.axis_size("feat") == 4
        and rows_a % 16 == 0
        and rows_b == 2 * rows_a
        and width_a == 2 * width_b
        and width_a % (GROUP * BLK) == 0
        and (8 * rows_a) % (4 * BLK) == 0
        and 8 * rows_a <= 1024
    )
    plan = owned_shards if fits else general_shards
    return plan(first_view_outputs, second_view_outputs)


def solution(mesh):
    placed = (P("dp", "feat"), P("feat", "dp"))
    return jax.shard_map(
        shards,
        mesh=mesh,
        in_specs=placed,
        out_specs=(P("dp", "feat"), P("feat", "dp")),
        check_vma=False,
    )
```

```python
import functools
import jax
import jax.numpy as jnp
from jax import lax
from jax.experimental import pallas as pl
from jax.experimental.pallas import tpu as pltpu
from jax.sharding import PartitionSpec as P

EPSILON = 1e-05
OFF_WEIGHT = 0.0051
MESH = pl.DeviceIdType.MESH
BLK = 128
GROUP = 4


def normalize_backward(
    normalized_gradient, standardized_values, inverse_scale, column_sums, total_count
):
    centering_term = column_sums[0] / total_count
    projection_term = column_sums[1] / total_count
    return (
        (normalized_gradient - centering_term - standardized_values * projection_term)
        * inverse_scale
    ).astype(jnp.bfloat16)


def general_shards(first_view_outputs, second_view_outputs):
    rows_a, width_a = first_view_outputs.shape
    rows_b, width_b = second_view_outputs.shape
    total_count = rows_a * lax.axis_size("dp")

    def standardize(values, axis):
        local = values.astype(jnp.float32)
        center = lax.psum(jnp.sum(local, axis=0), axis) / total_count
        centered = local - center
        spread = lax.psum(jnp.sum(centered * centered, axis=0), axis) / total_count
        inverse = lax.rsqrt(spread + EPSILON)
        standardized = centered * inverse
        gathered = lax.all_gather(standardized.astype(jnp.bfloat16), axis, axis=0, tiled=True)
        return standardized, inverse, gathered

    standardized_first, inverse_first, normalized_first = standardize(first_view_outputs, "dp")
    standardized_second, inverse_second, normalized_second = standardize(
        second_view_outputs, "feat"
    )
    correlation = (
        lax.dot_general(
            normalized_first,
            normalized_second,
            (((0,), (0,)), ((), ())),
            preferred_element_type=jnp.float32,
        )
        / total_count
    )
    row_ids = lax.axis_index("feat") * width_a + lax.broadcasted_iota(
        jnp.int32, (width_a, width_b), 0
    )
    col_ids = lax.axis_index("dp") * width_b + lax.broadcasted_iota(
        jnp.int32, (width_a, width_b), 1
    )
    grad_tile = jnp.where(
        row_ids == col_ids, 2.0 * (correlation - 1.0), 2.0 * OFF_WEIGHT * correlation
    ).astype(jnp.bfloat16)

    def finish(partial, axis, standardized, inverse):
        gradient = lax.psum_scatter(
            partial.astype(jnp.bfloat16), axis, scatter_dimension=0, tiled=True
        ).astype(jnp.float32)
        sums = lax.psum(
            (jnp.sum(gradient, axis=0), jnp.sum(gradient * standardized, axis=0)), axis
        )
        return normalize_backward(gradient, standardized, inverse, sums, total_count)

    partial_first = lax.dot_general(
        normalized_second,
        grad_tile,
        (((1,), (1,)), ((), ())),
        preferred_element_type=jnp.float32,
    )
    partial_second = jnp.dot(normalized_first, grad_tile, preferred_element_type=jnp.float32)
    return (
        finish(partial_first, "dp", standardized_first, inverse_first),
        finish(partial_second, "feat", standardized_second, inverse_second),
    )


def kernel(
    features,
    chunk,
    a_ref,
    b_ref,
    ga_ref,
    gb_ref,
    raw,
    xhat,
    inv,
    norm,
    other,
    base,
    running,
    packed,
    r1,
    s1,
    r2,
    gathered,
    full_packed,
    gram,
    grad,
    in_send,
    in_recv,
    swap_send,
    swap_recv,
    rs1_send,
    rs1_recv,
    rs2_send,
    rs2_recv,
    ag1_send,
    ag1_recv,
    ag2_send,
    ag2_recv,
    out_send,
    out_recv,
):
    n_dp, n_feat = 8, 4
    n_dev = n_dp * n_feat
    p = lax.axis_index("dp")
    f = lax.axis_index("feat")
    z, y = p // 2, p % 2
    x, core = f // 2, f % 2
    g = 2 * y + x
    rows_a = a_ref.shape[0]
    rows_b = b_ref.shape[0]
    count, width = raw.shape
    n_chunks = width // chunk
    n_blk = count // BLK
    seg = packed.shape[0] // GROUP
    unit = seg // GROUP

    barrier = pltpu.get_barrier_semaphore()
    me = p * n_feat + f

    def greet(k, carry):
        t = (me + k) % n_dev
        pl.semaphore_signal(
            barrier, inc=1, device_id=(t // n_feat, t % n_feat), device_id_type=MESH
        )
        return carry

    lax.fori_loop(1, n_dev, greet, 0)
    pl.semaphore_wait(barrier, n_dev - 1)

    def start_or_local(src, dst, send_sem, recv_sem, device, is_self):
        cp = pltpu.make_async_remote_copy(
            src_ref=src,
            dst_ref=dst,
            send_sem=send_sem,
            recv_sem=recv_sem,
            device_id=device,
            device_id_type=MESH,
        )

        @pl.when(is_self)
        def _():
            pltpu.make_async_copy(src, dst, recv_sem).start()

        @pl.when(jnp.logical_not(is_self))
        def _():
            cp.start()

        return cp, is_self

    def wait_sent(item):
        cp, is_self = item

        @pl.when(jnp.logical_not(is_self))
        def _():
            cp.wait_send()

    sent = []
    for c in range(n_chunks):
        for k in range(GROUP):
            q = (g + k) % GROUP
            dp_to = 2 * f + q // 2
            feat_to = 2 * (q % 2)
            sent.append(
                start_or_local(
                    a_ref.at[:, pl.ds(pl.multiple_of(q * width + c * chunk, chunk), chunk)],
                    raw.at[
                        pl.ds(pl.multiple_of(p * rows_a, rows_a), rows_a),
                        pl.ds(c * chunk, chunk),
                    ],
                    in_send.at[c, k],
                    in_recv.at[c],
                    (dp_to, feat_to),
                    jnp.logical_and(dp_to == p, feat_to == f),
                )
            )
        for k in range(2):
            x_to = (x + 1 + k) % 2
            feat_to = 2 * x_to + 1
            sent.append(
                start_or_local(
                    b_ref.at[:, pl.ds(pl.multiple_of(x_to * width + c * chunk, chunk), chunk)],
                    raw.at[
                        pl.ds(pl.multiple_of(f * rows_b, rows_b), rows_b),
                        pl.ds(c * chunk, chunk),
                    ],
                    in_send.at[c, GROUP + k],
                    in_recv.at[c],
                    (p, feat_to),
                    feat_to == f,
                )
            )

    eye = jnp.where(
        lax.broadcasted_iota(jnp.int32, (BLK, BLK), 0)
        == lax.broadcasted_iota(jnp.int32, (BLK, BLK), 1),
        jnp.float32(width),
        jnp.float32(0),
    )
    where = {}
    for bi in range(n_blk):
        for bj in range(bi, n_blk):
            where[bi, bj] = len(where)
    swaps = []
    for c in range(n_chunks):
        part = raw.at[:, pl.ds(c * chunk, chunk)]
        pltpu.make_async_copy(part, part, in_recv.at[c]).wait()
        for h in range(c * chunk, (c + 1) * chunk, BLK):
            cols = slice(h, h + BLK)
            values = raw[:, cols].astype(jnp.float32)
            center = jnp.sum(values, axis=0, keepdims=True) / count
            centered = values - center
            spread = jnp.sum(centered * centered, axis=0, keepdims=True) / count
            inverse = lax.rsqrt(spread + EPSILON)
            standardized = centered * inverse
            xhat[:, cols] = standardized
            norm[:, cols] = standardized.astype(jnp.bfloat16)
            inv[0:1, cols] = inverse
        cols = slice(c * chunk, (c + 1) * chunk)
        for bi in range(n_blk):
            share = lax.dot_general(
                norm[bi * BLK : (bi + 1) * BLK, cols],
                norm[bi * BLK :, cols],
                (((1,), (1,)), ((), ())),
                preferred_element_type=jnp.float32,
            )
            for bj in range(bi, n_blk):
                at = slice(where[bi, bj] * BLK, (where[bi, bj] + 1) * BLK)
                block = share[:, (bj - bi) * BLK : (bj - bi + 1) * BLK]
                if bi == bj and c == 0:
                    block = block - eye
                if c > 0:
                    block = block + running[at, :]
                if c < n_chunks - 1:
                    running[at, :] = block
                else:
                    packed[at, :] = block.astype(jnp.bfloat16)
        swap = pltpu.make_async_remote_copy(
            src_ref=norm.at[:, pl.ds(c * chunk, chunk)],
            dst_ref=other.at[:, pl.ds(c * chunk, chunk)],
            send_sem=swap_send.at[c],
            recv_sem=swap_recv.at[c],
            device_id=(p, 2 * x + 1 - core),
            device_id_type=MESH,
        )
        swaps.append(swap)
        if c < n_chunks - 1:
            swap.start()

    copies = []
    arriving = {}
    for kz in range(1, GROUP + 1):
        zt = (z + kz) % GROUP
        for k in range(1, GROUP):
            q = (g + k) % GROUP
            cp = pltpu.make_async_remote_copy(
                src_ref=packed.at[pl.ds(pl.multiple_of(q * seg + zt * unit, unit), unit), :],
                dst_ref=r1.at[kz - 1, k - 1],
                send_sem=rs1_send.at[kz - 1, k - 1],
                recv_sem=rs1_recv.at[kz - 1, k - 1],
                device_id=(2 * z + q // 2, 2 * (q % 2) + core),
                device_id_type=MESH,
            )
            cp.start()
            arriving[kz, k] = cp
            copies.append(cp)
    swaps[-1].start()
    coming = []
    for kz in range(1, GROUP + 1):
        zt = (z + kz) % GROUP
        total = packed[pl.ds(pl.multiple_of(g * seg + zt * unit, unit), unit), :].astype(
            jnp.float32
        )
        for k in range(1, GROUP):
            arriving[kz, k].wait_recv()
            total = total + r1[kz - 1, k - 1].astype(jnp.float32)
        if kz < GROUP:
            s1[kz - 1] = total.astype(jnp.bfloat16)
            cp = pltpu.make_async_remote_copy(
                src_ref=s1.at[kz - 1],
                dst_ref=r2.at[kz - 1],
                send_sem=rs2_send.at[kz - 1],
                recv_sem=rs2_recv.at[kz - 1],
                device_id=(2 * zt + y, f),
                device_id_type=MESH,
            )
            cp.start()
            coming.append(cp)
    for kz in range(1, GROUP):
        coming[kz - 1].wait_recv()
        total = total + r2[kz - 1].astype(jnp.float32)
    copies += coming
    mine = pl.ds(pl.multiple_of(z * unit, unit), unit)
    gathered[mine, :] = total.astype(jnp.bfloat16)

    coming = []
    for kz in range(1, GROUP):
        zt = (z + kz) % GROUP
        cp = pltpu.make_async_remote_copy(
            src_ref=gathered.at[mine, :],
            dst_ref=gathered.at[mine, :],
            send_sem=ag1_send.at[kz - 1],
            recv_sem=ag1_recv.at[kz - 1],
            device_id=(2 * zt + y, f),
            device_id_type=MESH,
        )
        cp.start()
        coming.append(cp)
    last = []
    for kz in range(GROUP):
        if kz > 0:
            coming[kz - 1].wait_recv()
        zs = (z + GROUP - kz) % GROUP
        for k in range(1, GROUP + 1):
            q = (g + k) % GROUP
            cp = pltpu.make_async_remote_copy(
                src_ref=gathered.at[pl.ds(pl.multiple_of(zs * unit, unit), unit), :],
                dst_ref=full_packed.at[
                    pl.ds(pl.multiple_of(g * seg + zs * unit, unit), unit), :
                ],
                send_sem=ag2_send.at[kz, k - 1],
                recv_sem=ag2_recv.at[kz, k - 1],
                device_id=(2 * z + q // 2, 2 * (q % 2) + 1 - core),
                device_id_type=MESH,
            )
            cp.start()
            last.append(cp)
    copies += coming

    scale = 2.0 * OFF_WEIGHT / count
    for c in range(n_chunks):
        swaps[c].wait_recv()
        cols = slice(c * chunk, (c + 1) * chunk)
        own = norm[:, cols].astype(jnp.float32)
        paired = other[:, cols].astype(jnp.float32)
        corr = jnp.sum(own * paired, axis=0, keepdims=True) / count
        diagonal = 2.0 * (corr - 1.0) - 2.0 * OFF_WEIGHT * corr
        base[:, cols] = own * (scale * features) + paired * diagonal
    for cp in last:
        cp.wait_recv()
    for (bi, bj), at in where.items():
        block = full_packed[at * BLK : (at + 1) * BLK, :]
        gram[bi * BLK : (bi + 1) * BLK, bj * BLK : (bj + 1) * BLK] = block
        if bi != bj:
            gram[bj * BLK : (bj + 1) * BLK, bi * BLK : (bi + 1) * BLK] = block.T

    for c in range(n_chunks):
        cols = slice(c * chunk, (c + 1) * chunk)
        dnorm = base[:, cols] + scale * lax.dot_general(
            gram[...], norm[:, cols], (((1,), (0,)), ((), ())), preferred_element_type=jnp.float32
        )
        standardized = xhat[:, cols]
        centering = jnp.sum(dnorm, axis=0, keepdims=True) / count
        projection = jnp.sum(dnorm * standardized, axis=0, keepdims=True) / count
        grad[:, cols] = (
            (dnorm - centering - standardized * projection) * inv[0:1, cols]
        ).astype(jnp.bfloat16)

        @pl.when(core == 0)
        def _():
            place = pl.ds(pl.multiple_of(g * width + c * chunk, chunk), chunk)
            for k in range(1, n_dp + 1):
                to = (p + k) % n_dp
                start_or_local(
                    grad.at[pl.ds(pl.multiple_of(to * rows_a, rows_a), rows_a), cols],
                    ga_ref.at[:, place],
                    out_send.at[c, k - 1],
                    out_recv.at[0],
                    (to, z),
                    jnp.logical_and(to == p, z == f),
                )

        @pl.when(core == 1)
        def _():
            place = pl.ds(pl.multiple_of(x * width + c * chunk, chunk), chunk)
            for k in range(1, n_feat + 1):
                to = (f + k) % n_feat
                src = grad.at[pl.ds(pl.multiple_of(to * rows_b, rows_b), rows_b), cols]
                if k == n_feat:
                    pltpu.make_async_copy(src, gb_ref.at[:, place], out_recv.at[1]).start()
                else:
                    pltpu.make_async_remote_copy(
                        src_ref=src,
                        dst_ref=gb_ref.at[:, place],
                        send_sem=out_send.at[c, k - 1],
                        recv_sem=out_recv.at[1],
                        device_id=(p, to),
                        device_id_type=MESH,
                    ).start()

    for item in sent:
        wait_sent(item)
    for cp in swaps + copies + last:
        cp.wait_send()

    @pl.when(core == 0)
    def _():
        for c in range(n_chunks):
            for k in range(1, n_dp + 1):
                to = (p + k) % n_dp
                piece = grad.at[0:rows_a, 0:chunk]

                @pl.when(jnp.logical_not(jnp.logical_and(to == p, z == f)))
                def _():
                    pltpu.make_async_copy(piece, piece, out_send.at[c, k - 1]).wait()

    @pl.when(core == 1)
    def _():
        for c in range(n_chunks):
            for k in range(1, n_feat):
                piece = grad.at[0:rows_b, 0:chunk]
                pltpu.make_async_copy(piece, piece, out_send.at[c, k - 1]).wait()

    pltpu.make_async_copy(ga_ref, ga_ref, out_recv.at[0]).wait()
    pltpu.make_async_copy(gb_ref, gb_ref, out_recv.at[1]).wait()


def owned_shards(first_view_outputs, second_view_outputs):
    count = first_view_outputs.shape[0] * lax.axis_size("dp")
    features = first_view_outputs.shape[1] * lax.axis_size("feat")
    width = first_view_outputs.shape[1] // GROUP
    chunk = 256 if width % 256 == 0 else 128
    chunks = width // chunk
    n_blk = count // BLK
    packed_rows = n_blk * (n_blk + 1) // 2 * BLK
    seg = packed_rows // GROUP
    unit = seg // GROUP
    bf16, f32 = jnp.bfloat16, jnp.float32
    dma = pltpu.SemaphoreType.DMA
    any_spec = pl.BlockSpec(memory_space=pl.ANY)
    return pl.pallas_call(
        functools.partial(kernel, float(features), chunk),
        out_shape=[
            jax.ShapeDtypeStruct(first_view_outputs.shape, bf16),
            jax.ShapeDtypeStruct(second_view_outputs.shape, bf16),
        ],
        in_specs=[any_spec] * 2,
        out_specs=[any_spec] * 2,
        scratch_shapes=[
            pltpu.VMEM((count, width), bf16),
            pltpu.VMEM((count, width), f32),
            pltpu.VMEM((8, width), f32),
            pltpu.VMEM((count, width), bf16),
            pltpu.VMEM((count, width), bf16),
            pltpu.VMEM((count, width), f32),
            pltpu.VMEM((packed_rows, BLK), f32),
            pltpu.VMEM((packed_rows, BLK), bf16),
            pltpu.VMEM((GROUP, GROUP - 1, unit, BLK), bf16),
            pltpu.VMEM((GROUP - 1, unit, BLK), bf16),
            pltpu.VMEM((GROUP - 1, unit, BLK), bf16),
            pltpu.VMEM((seg, BLK), bf16),
            pltpu.VMEM((packed_rows, BLK), bf16),
            pltpu.VMEM((count, count), bf16),
            pltpu.VMEM((count, width), bf16),
            dma((chunks, GROUP + 2)),
            dma((chunks,)),
            dma((chunks,)),
            dma((chunks,)),
            dma((GROUP, GROUP - 1)),
            dma((GROUP, GROUP - 1)),
            dma((GROUP - 1,)),
            dma((GROUP - 1,)),
            dma((GROUP - 1,)),
            dma((GROUP - 1,)),
            dma((GROUP, GROUP)),
            dma((GROUP, GROUP)),
            dma((chunks, 8)),
            dma((2,)),
        ],
        compiler_params=pltpu.CompilerParams(
            collective_id=0, has_side_effects=True, vmem_limit_bytes=60 * 1024 * 1024
        ),
        name="owned_columns",
    )(first_view_outputs, second_view_outputs)


def shards(first_view_outputs, second_view_outputs):
    rows_a, width_a = first_view_outputs.shape
    rows_b, width_b = second_view_outputs.shape
    fits = (
        lax.axis_size("dp") == 8
        and lax.axis_size("feat") == 4
        and rows_a % 16 == 0
        and rows_b == 2 * rows_a
        and width_a == 2 * width_b
        and width_a % (GROUP * BLK) == 0
        and (8 * rows_a) % (4 * BLK) == 0
        and 8 * rows_a <= 1024
    )
    plan = owned_shards if fits else general_shards
    return plan(first_view_outputs, second_view_outputs)


def solution(mesh):
    placed = (P("dp", "feat"), P("feat", "dp"))
    return jax.shard_map(
        shards,
        mesh=mesh,
        in_specs=placed,
        out_specs=(P("dp", "feat"), P("feat", "dp")),
        check_vma=False,
    )
```

```python
import functools
import jax
import jax.numpy as jnp
from jax import lax
from jax.experimental import pallas as pl
from jax.experimental.pallas import tpu as pltpu
from jax.sharding import PartitionSpec as P

EPSILON = 1e-05
OFF_WEIGHT = 0.0051
MESH = pl.DeviceIdType.MESH
BLK = 128
PARTS = 4
GROUP = 4


def normalize_backward(
    normalized_gradient, standardized_values, inverse_scale, column_sums, total_count
):
    centering_term = column_sums[0] / total_count
    projection_term = column_sums[1] / total_count
    return (
        (normalized_gradient - centering_term - standardized_values * projection_term)
        * inverse_scale
    ).astype(jnp.bfloat16)


def general_shards(first_view_outputs, second_view_outputs):
    rows_a, width_a = first_view_outputs.shape
    rows_b, width_b = second_view_outputs.shape
    total_count = rows_a * lax.axis_size("dp")

    def standardize(values, axis):
        local = values.astype(jnp.float32)
        center = lax.psum(jnp.sum(local, axis=0), axis) / total_count
        centered = local - center
        spread = lax.psum(jnp.sum(centered * centered, axis=0), axis) / total_count
        inverse = lax.rsqrt(spread + EPSILON)
        standardized = centered * inverse
        gathered = lax.all_gather(standardized.astype(jnp.bfloat16), axis, axis=0, tiled=True)
        return standardized, inverse, gathered

    standardized_first, inverse_first, normalized_first = standardize(first_view_outputs, "dp")
    standardized_second, inverse_second, normalized_second = standardize(
        second_view_outputs, "feat"
    )
    correlation = (
        lax.dot_general(
            normalized_first,
            normalized_second,
            (((0,), (0,)), ((), ())),
            preferred_element_type=jnp.float32,
        )
        / total_count
    )
    row_ids = lax.axis_index("feat") * width_a + lax.broadcasted_iota(
        jnp.int32, (width_a, width_b), 0
    )
    col_ids = lax.axis_index("dp") * width_b + lax.broadcasted_iota(
        jnp.int32, (width_a, width_b), 1
    )
    grad_tile = jnp.where(
        row_ids == col_ids, 2.0 * (correlation - 1.0), 2.0 * OFF_WEIGHT * correlation
    ).astype(jnp.bfloat16)

    def finish(partial, axis, standardized, inverse):
        gradient = lax.psum_scatter(
            partial.astype(jnp.bfloat16), axis, scatter_dimension=0, tiled=True
        ).astype(jnp.float32)
        sums = lax.psum(
            (jnp.sum(gradient, axis=0), jnp.sum(gradient * standardized, axis=0)), axis
        )
        return normalize_backward(gradient, standardized, inverse, sums, total_count)

    partial_first = lax.dot_general(
        normalized_second,
        grad_tile,
        (((1,), (1,)), ((), ())),
        preferred_element_type=jnp.float32,
    )
    partial_second = jnp.dot(normalized_first, grad_tile, preferred_element_type=jnp.float32)
    return (
        finish(partial_first, "dp", standardized_first, inverse_first),
        finish(partial_second, "feat", standardized_second, inverse_second),
    )


def kernel(
    features,
    chunk,
    a_ref,
    b_ref,
    ga_ref,
    gb_ref,
    raw,
    xhat,
    inv,
    norm,
    other,
    base,
    running,
    packed,
    r1,
    s1,
    r2,
    gathered,
    full_packed,
    gram,
    grad,
    in_send,
    in_recv,
    swap_send,
    swap_recv,
    rs1_send,
    rs1_recv,
    rs2_send,
    rs2_recv,
    ag1_send,
    ag1_recv,
    ag2_send,
    ag2_recv,
    out_send,
    out_recv,
):
    n_dp, n_feat = 8, 4
    n_dev = n_dp * n_feat
    p = lax.axis_index("dp")
    f = lax.axis_index("feat")
    z, y = p // 2, p % 2
    x, core = f // 2, f % 2
    g = 2 * y + x
    rows_a = a_ref.shape[0]
    rows_b = b_ref.shape[0]
    count, width = raw.shape
    n_chunks = width // chunk
    n_blk = count // BLK
    seg = packed.shape[0] // GROUP
    unit = seg // GROUP

    barrier = pltpu.get_barrier_semaphore()
    me = p * n_feat + f

    def greet(k, carry):
        t = (me + k) % n_dev
        pl.semaphore_signal(
            barrier, inc=1, device_id=(t // n_feat, t % n_feat), device_id_type=MESH
        )
        return carry

    lax.fori_loop(1, n_dev, greet, 0)
    pl.semaphore_wait(barrier, n_dev - 1)

    def start_or_local(src, dst, send_sem, recv_sem, device, is_self):
        cp = pltpu.make_async_remote_copy(
            src_ref=src,
            dst_ref=dst,
            send_sem=send_sem,
            recv_sem=recv_sem,
            device_id=device,
            device_id_type=MESH,
        )

        @pl.when(is_self)
        def _():
            pltpu.make_async_copy(src, dst, recv_sem).start()

        @pl.when(jnp.logical_not(is_self))
        def _():
            cp.start()

        return cp, is_self

    def wait_sent(item):
        cp, is_self = item

        @pl.when(jnp.logical_not(is_self))
        def _():
            cp.wait_send()

    sent = []
    for c in range(n_chunks):
        for k in range(GROUP):
            q = (g + k) % GROUP
            dp_to = 2 * f + q // 2
            feat_to = 2 * (q % 2)
            sent.append(
                start_or_local(
                    a_ref.at[:, pl.ds(pl.multiple_of(q * width + c * chunk, chunk), chunk)],
                    raw.at[
                        pl.ds(pl.multiple_of(p * rows_a, rows_a), rows_a),
                        pl.ds(c * chunk, chunk),
                    ],
                    in_send.at[c, k],
                    in_recv.at[c],
                    (dp_to, feat_to),
                    jnp.logical_and(dp_to == p, feat_to == f),
                )
            )
        for k in range(2):
            x_to = (x + 1 + k) % 2
            feat_to = 2 * x_to + 1
            sent.append(
                start_or_local(
                    b_ref.at[:, pl.ds(pl.multiple_of(x_to * width + c * chunk, chunk), chunk)],
                    raw.at[
                        pl.ds(pl.multiple_of(f * rows_b, rows_b), rows_b),
                        pl.ds(c * chunk, chunk),
                    ],
                    in_send.at[c, GROUP + k],
                    in_recv.at[c],
                    (p, feat_to),
                    feat_to == f,
                )
            )

    eye = jnp.where(
        lax.broadcasted_iota(jnp.int32, (BLK, BLK), 0)
        == lax.broadcasted_iota(jnp.int32, (BLK, BLK), 1),
        jnp.float32(width),
        jnp.float32(0),
    )
    where = {}
    for bi in range(n_blk):
        for bj in range(bi, n_blk):
            where[bi, bj] = len(where)
    swaps = []
    for c in range(n_chunks):
        part = raw.at[:, pl.ds(c * chunk, chunk)]
        pltpu.make_async_copy(part, part, in_recv.at[c]).wait()
        for h in range(c * chunk, (c + 1) * chunk, BLK):
            cols = slice(h, h + BLK)
            values = raw[:, cols].astype(jnp.float32)
            center = jnp.sum(values, axis=0, keepdims=True) / count
            centered = values - center
            spread = jnp.sum(centered * centered, axis=0, keepdims=True) / count
            inverse = lax.rsqrt(spread + EPSILON)
            standardized = centered * inverse
            xhat[:, cols] = standardized
            norm[:, cols] = standardized.astype(jnp.bfloat16)
            inv[0:1, cols] = inverse
        cols = slice(c * chunk, (c + 1) * chunk)
        for bi in range(n_blk):
            share = lax.dot_general(
                norm[bi * BLK : (bi + 1) * BLK, cols],
                norm[bi * BLK :, cols],
                (((1,), (1,)), ((), ())),
                preferred_element_type=jnp.float32,
            )
            for bj in range(bi, n_blk):
                at = slice(where[bi, bj] * BLK, (where[bi, bj] + 1) * BLK)
                block = share[:, (bj - bi) * BLK : (bj - bi + 1) * BLK]
                if bi == bj and c == 0:
                    block = block - eye
                if c > 0:
                    block = block + running[at, :]
                if c < n_chunks - 1:
                    running[at, :] = block
                else:
                    packed[at, :] = block.astype(jnp.bfloat16)
        swap = pltpu.make_async_remote_copy(
            src_ref=norm.at[:, pl.ds(c * chunk, chunk)],
            dst_ref=other.at[:, pl.ds(c * chunk, chunk)],
            send_sem=swap_send.at[c],
            recv_sem=swap_recv.at[c],
            device_id=(p, 2 * x + 1 - core),
            device_id_type=MESH,
        )
        swaps.append(swap)
        if c < n_chunks - 1:
            swap.start()

    copies = []
    arriving = {}
    for kz in range(1, GROUP + 1):
        zt = (z + kz) % GROUP
        for k in range(1, GROUP):
            q = (g + k) % GROUP
            cp = pltpu.make_async_remote_copy(
                src_ref=packed.at[pl.ds(pl.multiple_of(q * seg + zt * unit, unit), unit), :],
                dst_ref=r1.at[kz - 1, k - 1],
                send_sem=rs1_send.at[kz - 1, k - 1],
                recv_sem=rs1_recv.at[kz - 1, k - 1],
                device_id=(2 * z + q // 2, 2 * (q % 2) + core),
                device_id_type=MESH,
            )
            cp.start()
            arriving[kz, k] = cp
            copies.append(cp)
    swaps[-1].start()
    coming = []
    for kz in range(1, GROUP + 1):
        zt = (z + kz) % GROUP
        total = packed[pl.ds(pl.multiple_of(g * seg + zt * unit, unit), unit), :].astype(
            jnp.float32
        )
        for k in range(1, GROUP):
            arriving[kz, k].wait_recv()
            total = total + r1[kz - 1, k - 1].astype(jnp.float32)
        if kz < GROUP:
            s1[kz - 1] = total.astype(jnp.bfloat16)
            cp = pltpu.make_async_remote_copy(
                src_ref=s1.at[kz - 1],
                dst_ref=r2.at[kz - 1],
                send_sem=rs2_send.at[kz - 1],
                recv_sem=rs2_recv.at[kz - 1],
                device_id=(2 * zt + y, f),
                device_id_type=MESH,
            )
            cp.start()
            coming.append(cp)
    for kz in range(1, GROUP):
        coming[kz - 1].wait_recv()
        total = total + r2[kz - 1].astype(jnp.float32)
    copies += coming
    mine = pl.ds(pl.multiple_of(z * unit, unit), unit)
    gathered[mine, :] = total.astype(jnp.bfloat16)

    coming = []
    for kz in range(1, GROUP):
        zt = (z + kz) % GROUP
        cp = pltpu.make_async_remote_copy(
            src_ref=gathered.at[mine, :],
            dst_ref=gathered.at[mine, :],
            send_sem=ag1_send.at[kz - 1],
            recv_sem=ag1_recv.at[kz - 1],
            device_id=(2 * zt + y, f),
            device_id_type=MESH,
        )
        cp.start()
        coming.append(cp)
    last = []
    for kz in range(GROUP):
        if kz > 0:
            coming[kz - 1].wait_recv()
        zs = (z + GROUP - kz) % GROUP
        for k in range(1, GROUP + 1):
            q = (g + k) % GROUP
            cp = pltpu.make_async_remote_copy(
                src_ref=gathered.at[pl.ds(pl.multiple_of(zs * unit, unit), unit), :],
                dst_ref=full_packed.at[
                    pl.ds(pl.multiple_of(g * seg + zs * unit, unit), unit), :
                ],
                send_sem=ag2_send.at[kz, k - 1],
                recv_sem=ag2_recv.at[kz, k - 1],
                device_id=(2 * z + q // 2, 2 * (q % 2) + 1 - core),
                device_id_type=MESH,
            )
            cp.start()
            last.append(cp)
    copies += coming

    scale = 2.0 * OFF_WEIGHT / count
    for c in range(n_chunks):
        swaps[c].wait_recv()
        cols = slice(c * chunk, (c + 1) * chunk)
        own = norm[:, cols].astype(jnp.float32)
        paired = other[:, cols].astype(jnp.float32)
        corr = jnp.sum(own * paired, axis=0, keepdims=True) / count
        diagonal = 2.0 * (corr - 1.0) - 2.0 * OFF_WEIGHT * corr
        base[:, cols] = own * (scale * features) + paired * diagonal
    for cp in last:
        cp.wait_recv()
    for (bi, bj), at in where.items():
        block = full_packed[at * BLK : (at + 1) * BLK, :]
        gram[bi * BLK : (bi + 1) * BLK, bj * BLK : (bj + 1) * BLK] = block
        if bi != bj:
            gram[bj * BLK : (bj + 1) * BLK, bi * BLK : (bi + 1) * BLK] = block.T

    for c in range(n_chunks):
        cols = slice(c * chunk, (c + 1) * chunk)
        dnorm = base[:, cols] + scale * lax.dot_general(
            gram[...], norm[:, cols], (((1,), (0,)), ((), ())), preferred_element_type=jnp.float32
        )
        standardized = xhat[:, cols]
        centering = jnp.sum(dnorm, axis=0, keepdims=True) / count
        projection = jnp.sum(dnorm * standardized, axis=0, keepdims=True) / count
        grad[:, cols] = (
            (dnorm - centering - standardized * projection) * inv[0:1, cols]
        ).astype(jnp.bfloat16)

        @pl.when(core == 0)
        def _():
            place = pl.ds(pl.multiple_of(g * width + c * chunk, chunk), chunk)
            for k in range(1, n_dp + 1):
                to = (p + k) % n_dp
                start_or_local(
                    grad.at[pl.ds(pl.multiple_of(to * rows_a, rows_a), rows_a), cols],
                    ga_ref.at[:, place],
                    out_send.at[c, k - 1],
                    out_recv.at[0],
                    (to, z),
                    jnp.logical_and(to == p, z == f),
                )

        @pl.when(core == 1)
        def _():
            place = pl.ds(pl.multiple_of(x * width + c * chunk, chunk), chunk)
            for k in range(1, n_feat + 1):
                to = (f + k) % n_feat
                src = grad.at[pl.ds(pl.multiple_of(to * rows_b, rows_b), rows_b), cols]
                if k == n_feat:
                    pltpu.make_async_copy(src, gb_ref.at[:, place], out_recv.at[1]).start()
                else:
                    pltpu.make_async_remote_copy(
                        src_ref=src,
                        dst_ref=gb_ref.at[:, place],
                        send_sem=out_send.at[c, k - 1],
                        recv_sem=out_recv.at[1],
                        device_id=(p, to),
                        device_id_type=MESH,
                    ).start()

    for item in sent:
        wait_sent(item)
    for cp in swaps + copies + last:
        cp.wait_send()

    @pl.when(core == 0)
    def _():
        for c in range(n_chunks):
            for k in range(1, n_dp + 1):
                to = (p + k) % n_dp
                piece = grad.at[0:rows_a, 0:chunk]

                @pl.when(jnp.logical_not(jnp.logical_and(to == p, z == f)))
                def _():
                    pltpu.make_async_copy(piece, piece, out_send.at[c, k - 1]).wait()

    @pl.when(core == 1)
    def _():
        for c in range(n_chunks):
            for k in range(1, n_feat):
                piece = grad.at[0:rows_b, 0:chunk]
                pltpu.make_async_copy(piece, piece, out_send.at[c, k - 1]).wait()

    pltpu.make_async_copy(ga_ref, ga_ref, out_recv.at[0]).wait()
    pltpu.make_async_copy(gb_ref, gb_ref, out_recv.at[1]).wait()


def hand_out(landed_a, landed_b, ga_ref, gb_ref, sems):
    copies = []
    for landed, out in ((landed_a, ga_ref), (landed_b, gb_ref)):
        part = landed.shape[0] // PARTS
        for i in range(PARTS):
            rows = pl.ds(i * part, part)
            copies.append(
                pltpu.make_async_copy(landed.at[rows, :], out.at[rows, :], sems.at[len(copies)])
            )
    for cp in copies:
        cp.start()
    for cp in copies:
        cp.wait()


def owned_shards(first_view_outputs, second_view_outputs):
    count = first_view_outputs.shape[0] * lax.axis_size("dp")
    features = first_view_outputs.shape[1] * lax.axis_size("feat")
    width = first_view_outputs.shape[1] // GROUP
    chunk = 256 if width % 256 == 0 else 128
    chunks = width // chunk
    n_blk = count // BLK
    packed_rows = n_blk * (n_blk + 1) // 2 * BLK
    seg = packed_rows // GROUP
    unit = seg // GROUP
    bf16, f32 = jnp.bfloat16, jnp.float32
    dma = pltpu.SemaphoreType.DMA
    any_spec = pl.BlockSpec(memory_space=pl.ANY)
    landed = pl.pallas_call(
        functools.partial(kernel, float(features), chunk),
        out_shape=[
            jax.ShapeDtypeStruct(first_view_outputs.shape, bf16),
            jax.ShapeDtypeStruct(second_view_outputs.shape, bf16),
        ],
        in_specs=[any_spec] * 2,
        out_specs=[any_spec] * 2,
        scratch_shapes=[
            pltpu.VMEM((count, width), bf16),
            pltpu.VMEM((count, width), f32),
            pltpu.VMEM((8, width), f32),
            pltpu.VMEM((count, width), bf16),
            pltpu.VMEM((count, width), bf16),
            pltpu.VMEM((count, width), f32),
            pltpu.VMEM((packed_rows, BLK), f32),
            pltpu.VMEM((packed_rows, BLK), bf16),
            pltpu.VMEM((GROUP, GROUP - 1, unit, BLK), bf16),
            pltpu.VMEM((GROUP - 1, unit, BLK), bf16),
            pltpu.VMEM((GROUP - 1, unit, BLK), bf16),
            pltpu.VMEM((seg, BLK), bf16),
            pltpu.VMEM((packed_rows, BLK), bf16),
            pltpu.VMEM((count, count), bf16),
            pltpu.VMEM((count, width), bf16),
            dma((chunks, GROUP + 2)),
            dma((chunks,)),
            dma((chunks,)),
            dma((chunks,)),
            dma((GROUP, GROUP - 1)),
            dma((GROUP, GROUP - 1)),
            dma((GROUP - 1,)),
            dma((GROUP - 1,)),
            dma((GROUP - 1,)),
            dma((GROUP - 1,)),
            dma((GROUP, GROUP)),
            dma((GROUP, GROUP)),
            dma((chunks, 8)),
            dma((2,)),
        ],
        compiler_params=pltpu.CompilerParams(
            collective_id=0, has_side_effects=True, vmem_limit_bytes=60 * 1024 * 1024
        ),
        name="owned_columns",
    )(first_view_outputs, second_view_outputs)
    return pl.pallas_call(
        hand_out,
        out_shape=[
            jax.ShapeDtypeStruct(first_view_outputs.shape, bf16),
            jax.ShapeDtypeStruct(second_view_outputs.shape, bf16),
        ],
        in_specs=[any_spec] * 2,
        out_specs=[any_spec] * 2,
        scratch_shapes=[dma((2 * PARTS,))],
        name="hand_out",
    )(*landed)


def shards(first_view_outputs, second_view_outputs):
    rows_a, width_a = first_view_outputs.shape
    rows_b, width_b = second_view_outputs.shape
    fits = (
        lax.axis_size("dp") == 8
        and lax.axis_size("feat") == 4
        and rows_a % 16 == 0
        and rows_b == 2 * rows_a
        and width_a == 2 * width_b
        and width_a % (GROUP * BLK) == 0
        and (8 * rows_a) % (4 * BLK) == 0
        and 8 * rows_a <= 1024
    )
    plan = owned_shards if fits else general_shards
    return plan(first_view_outputs, second_view_outputs)


def solution(mesh):
    placed = (P("dp", "feat"), P("feat", "dp"))
    return jax.shard_map(
        shards,
        mesh=mesh,
        in_specs=placed,
        out_specs=(P("dp", "feat"), P("feat", "dp")),
        check_vma=False,
    )
```

```python
import functools
import jax
import jax.numpy as jnp
from jax import lax
from jax.experimental import pallas as pl
from jax.experimental.pallas import tpu as pltpu
from jax.sharding import PartitionSpec as P

EPSILON = 1e-05
OFF_WEIGHT = 0.0051
MESH = pl.DeviceIdType.MESH
BLK = 128
GROUP = 4


def normalize_backward(
    normalized_gradient, standardized_values, inverse_scale, column_sums, total_count
):
    centering_term = column_sums[0] / total_count
    projection_term = column_sums[1] / total_count
    return (
        (normalized_gradient - centering_term - standardized_values * projection_term)
        * inverse_scale
    ).astype(jnp.bfloat16)


def general_shards(first_view_outputs, second_view_outputs):
    rows_a, width_a = first_view_outputs.shape
    rows_b, width_b = second_view_outputs.shape
    total_count = rows_a * lax.axis_size("dp")

    def standardize(values, axis):
        local = values.astype(jnp.float32)
        center = lax.psum(jnp.sum(local, axis=0), axis) / total_count
        centered = local - center
        spread = lax.psum(jnp.sum(centered * centered, axis=0), axis) / total_count
        inverse = lax.rsqrt(spread + EPSILON)
        standardized = centered * inverse
        gathered = lax.all_gather(standardized.astype(jnp.bfloat16), axis, axis=0, tiled=True)
        return standardized, inverse, gathered

    standardized_first, inverse_first, normalized_first = standardize(first_view_outputs, "dp")
    standardized_second, inverse_second, normalized_second = standardize(
        second_view_outputs, "feat"
    )
    correlation = (
        lax.dot_general(
            normalized_first,
            normalized_second,
            (((0,), (0,)), ((), ())),
            preferred_element_type=jnp.float32,
        )
        / total_count
    )
    row_ids = lax.axis_index("feat") * width_a + lax.broadcasted_iota(
        jnp.int32, (width_a, width_b), 0
    )
    col_ids = lax.axis_index("dp") * width_b + lax.broadcasted_iota(
        jnp.int32, (width_a, width_b), 1
    )
    grad_tile = jnp.where(
        row_ids == col_ids, 2.0 * (correlation - 1.0), 2.0 * OFF_WEIGHT * correlation
    ).astype(jnp.bfloat16)

    def finish(partial, axis, standardized, inverse):
        gradient = lax.psum_scatter(
            partial.astype(jnp.bfloat16), axis, scatter_dimension=0, tiled=True
        ).astype(jnp.float32)
        sums = lax.psum(
            (jnp.sum(gradient, axis=0), jnp.sum(gradient * standardized, axis=0)), axis
        )
        return normalize_backward(gradient, standardized, inverse, sums, total_count)

    partial_first = lax.dot_general(
        normalized_second,
        grad_tile,
        (((1,), (1,)), ((), ())),
        preferred_element_type=jnp.float32,
    )
    partial_second = jnp.dot(normalized_first, grad_tile, preferred_element_type=jnp.float32)
    return (
        finish(partial_first, "dp", standardized_first, inverse_first),
        finish(partial_second, "feat", standardized_second, inverse_second),
    )


def kernel(
    features,
    chunk,
    a_ref,
    b_ref,
    ga_ref,
    gb_ref,
    raw,
    xhat,
    inv,
    norm,
    other,
    base,
    running,
    packed,
    r1,
    s1,
    r2,
    gathered,
    full_packed,
    gram,
    grad,
    relay,
    in_send,
    in_recv,
    swap_send,
    swap_recv,
    rs1_send,
    rs1_recv,
    rs2_send,
    rs2_recv,
    ag1_send,
    ag1_recv,
    ag2_send,
    ag2_recv,
    out_send,
    out_recv,
    relay_send,
    relay_recv,
):
    n_dp, n_feat = 8, 4
    n_dev = n_dp * n_feat
    p = lax.axis_index("dp")
    f = lax.axis_index("feat")
    z, y = p // 2, p % 2
    x, core = f // 2, f % 2
    g = 2 * y + x
    rows_a = a_ref.shape[0]
    rows_b = b_ref.shape[0]
    count, width = raw.shape
    n_chunks = width // chunk
    n_blk = count // BLK
    seg = packed.shape[0] // GROUP
    unit = seg // GROUP

    barrier = pltpu.get_barrier_semaphore()
    me = p * n_feat + f

    def greet(k, carry):
        t = (me + k) % n_dev
        pl.semaphore_signal(
            barrier, inc=1, device_id=(t // n_feat, t % n_feat), device_id_type=MESH
        )
        return carry

    lax.fori_loop(1, n_dev, greet, 0)
    pl.semaphore_wait(barrier, n_dev - 1)

    def start_or_local(src, dst, send_sem, recv_sem, device, is_self):
        cp = pltpu.make_async_remote_copy(
            src_ref=src,
            dst_ref=dst,
            send_sem=send_sem,
            recv_sem=recv_sem,
            device_id=device,
            device_id_type=MESH,
        )

        @pl.when(is_self)
        def _():
            pltpu.make_async_copy(src, dst, recv_sem).start()

        @pl.when(jnp.logical_not(is_self))
        def _():
            cp.start()

        return cp, is_self

    def wait_sent(item):
        cp, is_self = item

        @pl.when(jnp.logical_not(is_self))
        def _():
            cp.wait_send()

    sent = []
    for c in range(n_chunks):
        for k in range(GROUP):
            q = (g + k) % GROUP
            dp_to = 2 * f + q // 2
            feat_to = 2 * (q % 2)
            sent.append(
                start_or_local(
                    a_ref.at[:, pl.ds(pl.multiple_of(q * width + c * chunk, chunk), chunk)],
                    raw.at[
                        pl.ds(pl.multiple_of(p * rows_a, rows_a), rows_a),
                        pl.ds(c * chunk, chunk),
                    ],
                    in_send.at[c, k],
                    in_recv.at[c],
                    (dp_to, feat_to),
                    jnp.logical_and(dp_to == p, feat_to == f),
                )
            )
        for k in range(2):
            x_to = (x + 1 + k) % 2
            feat_to = 2 * x_to + 1
            sent.append(
                start_or_local(
                    b_ref.at[:, pl.ds(pl.multiple_of(x_to * width + c * chunk, chunk), chunk)],
                    raw.at[
                        pl.ds(pl.multiple_of(f * rows_b, rows_b), rows_b),
                        pl.ds(c * chunk, chunk),
                    ],
                    in_send.at[c, GROUP + k],
                    in_recv.at[c],
                    (p, feat_to),
                    feat_to == f,
                )
            )

    eye = jnp.where(
        lax.broadcasted_iota(jnp.int32, (BLK, BLK), 0)
        == lax.broadcasted_iota(jnp.int32, (BLK, BLK), 1),
        jnp.float32(width),
        jnp.float32(0),
    )
    where = {}
    for bi in range(n_blk):
        for bj in range(bi, n_blk):
            where[bi, bj] = len(where)
    swaps = []
    for c in range(n_chunks):
        part = raw.at[:, pl.ds(c * chunk, chunk)]
        pltpu.make_async_copy(part, part, in_recv.at[c]).wait()
        for h in range(c * chunk, (c + 1) * chunk, BLK):
            cols = slice(h, h + BLK)
            values = raw[:, cols].astype(jnp.float32)
            center = jnp.sum(values, axis=0, keepdims=True) / count
            centered = values - center
            spread = jnp.sum(centered * centered, axis=0, keepdims=True) / count
            inverse = lax.rsqrt(spread + EPSILON)
            standardized = centered * inverse
            xhat[:, cols] = standardized
            norm[:, cols] = standardized.astype(jnp.bfloat16)
            inv[0:1, cols] = inverse
        cols = slice(c * chunk, (c + 1) * chunk)
        for bi in range(n_blk):
            share = lax.dot_general(
                norm[bi * BLK : (bi + 1) * BLK, cols],
                norm[bi * BLK :, cols],
                (((1,), (1,)), ((), ())),
                preferred_element_type=jnp.float32,
            )
            for bj in range(bi, n_blk):
                at = slice(where[bi, bj] * BLK, (where[bi, bj] + 1) * BLK)
                block = share[:, (bj - bi) * BLK : (bj - bi + 1) * BLK]
                if bi == bj and c == 0:
                    block = block - eye
                if c > 0:
                    block = block + running[at, :]
                if c < n_chunks - 1:
                    running[at, :] = block
                else:
                    packed[at, :] = block.astype(jnp.bfloat16)
        swap = pltpu.make_async_remote_copy(
            src_ref=norm.at[:, pl.ds(c * chunk, chunk)],
            dst_ref=other.at[:, pl.ds(c * chunk, chunk)],
            send_sem=swap_send.at[c],
            recv_sem=swap_recv.at[c],
            device_id=(p, 2 * x + 1 - core),
            device_id_type=MESH,
        )
        swaps.append(swap)
        if c < n_chunks - 1:
            swap.start()

    copies = []
    arriving = {}
    for kz in range(1, GROUP + 1):
        zt = (z + kz) % GROUP
        for k in range(1, GROUP):
            q = (g + k) % GROUP
            cp = pltpu.make_async_remote_copy(
                src_ref=packed.at[pl.ds(pl.multiple_of(q * seg + zt * unit, unit), unit), :],
                dst_ref=r1.at[kz - 1, k - 1],
                send_sem=rs1_send.at[kz - 1, k - 1],
                recv_sem=rs1_recv.at[kz - 1, k - 1],
                device_id=(2 * z + q // 2, 2 * (q % 2) + core),
                device_id_type=MESH,
            )
            cp.start()
            arriving[kz, k] = cp
            copies.append(cp)
    swaps[-1].start()
    coming = []
    for kz in range(1, GROUP + 1):
        zt = (z + kz) % GROUP
        total = packed[pl.ds(pl.multiple_of(g * seg + zt * unit, unit), unit), :].astype(
            jnp.float32
        )
        for k in range(1, GROUP):
            arriving[kz, k].wait_recv()
            total = total + r1[kz - 1, k - 1].astype(jnp.float32)
        if kz < GROUP:
            s1[kz - 1] = total.astype(jnp.bfloat16)
            cp = pltpu.make_async_remote_copy(
                src_ref=s1.at[kz - 1],
                dst_ref=r2.at[kz - 1],
                send_sem=rs2_send.at[kz - 1],
                recv_sem=rs2_recv.at[kz - 1],
                device_id=(2 * zt + y, f),
                device_id_type=MESH,
            )
            cp.start()
            coming.append(cp)
    for kz in range(1, GROUP):
        coming[kz - 1].wait_recv()
        total = total + r2[kz - 1].astype(jnp.float32)
    copies += coming
    mine = pl.ds(pl.multiple_of(z * unit, unit), unit)
    gathered[mine, :] = total.astype(jnp.bfloat16)

    coming = []
    for kz in range(1, GROUP):
        zt = (z + kz) % GROUP
        cp = pltpu.make_async_remote_copy(
            src_ref=gathered.at[mine, :],
            dst_ref=gathered.at[mine, :],
            send_sem=ag1_send.at[kz - 1],
            recv_sem=ag1_recv.at[kz - 1],
            device_id=(2 * zt + y, f),
            device_id_type=MESH,
        )
        cp.start()
        coming.append(cp)
    last = []
    for kz in range(GROUP):
        if kz > 0:
            coming[kz - 1].wait_recv()
        zs = (z + GROUP - kz) % GROUP
        for k in range(1, GROUP + 1):
            q = (g + k) % GROUP
            cp = pltpu.make_async_remote_copy(
                src_ref=gathered.at[pl.ds(pl.multiple_of(zs * unit, unit), unit), :],
                dst_ref=full_packed.at[
                    pl.ds(pl.multiple_of(g * seg + zs * unit, unit), unit), :
                ],
                send_sem=ag2_send.at[kz, k - 1],
                recv_sem=ag2_recv.at[kz, k - 1],
                device_id=(2 * z + q // 2, 2 * (q % 2) + 1 - core),
                device_id_type=MESH,
            )
            cp.start()
            last.append(cp)
    copies += coming

    scale = 2.0 * OFF_WEIGHT / count
    for c in range(n_chunks):
        swaps[c].wait_recv()
        cols = slice(c * chunk, (c + 1) * chunk)
        own = norm[:, cols].astype(jnp.float32)
        paired = other[:, cols].astype(jnp.float32)
        corr = jnp.sum(own * paired, axis=0, keepdims=True) / count
        diagonal = 2.0 * (corr - 1.0) - 2.0 * OFF_WEIGHT * corr
        base[:, cols] = own * (scale * features) + paired * diagonal
    for cp in last:
        cp.wait_recv()
    for (bi, bj), at in where.items():
        block = full_packed[at * BLK : (at + 1) * BLK, :]
        gram[bi * BLK : (bi + 1) * BLK, bj * BLK : (bj + 1) * BLK] = block
        if bi != bj:
            gram[bj * BLK : (bj + 1) * BLK, bi * BLK : (bi + 1) * BLK] = block.T

    home = z // 2 == x
    for c in range(n_chunks):
        cols = slice(c * chunk, (c + 1) * chunk)
        dnorm = base[:, cols] + scale * lax.dot_general(
            gram[...], norm[:, cols], (((1,), (0,)), ((), ())), preferred_element_type=jnp.float32
        )
        standardized = xhat[:, cols]
        centering = jnp.sum(dnorm, axis=0, keepdims=True) / count
        projection = jnp.sum(dnorm * standardized, axis=0, keepdims=True) / count
        grad[:, cols] = (
            (dnorm - centering - standardized * projection) * inv[0:1, cols]
        ).astype(jnp.bfloat16)

        @pl.when(core == 0)
        def _():
            place = pl.ds(pl.multiple_of(g * width + c * chunk, chunk), chunk)
            for k in range(1, n_dp + 1):
                to = (p + k) % n_dp
                feat_to = 2 * x + z % 2
                is_self = jnp.logical_and(to == p, feat_to == f)
                src = grad.at[pl.ds(pl.multiple_of(to * rows_a, rows_a), rows_a), cols]

                @pl.when(home)
                def _():
                    start_or_local(
                        src,
                        ga_ref.at[:, place],
                        out_send.at[c, k - 1],
                        out_recv.at[0],
                        (to, feat_to),
                        is_self,
                    )

                @pl.when(jnp.logical_not(home))
                def _():
                    start_or_local(
                        src,
                        relay.at[c, y],
                        out_send.at[c, k - 1],
                        relay_recv.at[c],
                        (to, feat_to),
                        is_self,
                    )

        @pl.when(core == 1)
        def _():
            place = pl.ds(pl.multiple_of(x * width + c * chunk, chunk), chunk)
            for k in range(1, n_feat + 1):
                to = (f + k) % n_feat
                src = grad.at[pl.ds(pl.multiple_of(to * rows_b, rows_b), rows_b), cols]
                if k == n_feat:
                    pltpu.make_async_copy(src, gb_ref.at[:, place], out_recv.at[1]).start()
                else:
                    pltpu.make_async_remote_copy(
                        src_ref=src,
                        dst_ref=gb_ref.at[:, place],
                        send_sem=out_send.at[c, k - 1],
                        recv_sem=out_recv.at[1],
                        device_id=(p, to),
                        device_id_type=MESH,
                    ).start()

    forwarded = []
    for c in range(n_chunks):
        pltpu.make_async_copy(relay.at[c], relay.at[c], relay_recv.at[c]).wait()
        for ys in range(2):
            place = pl.ds(
                pl.multiple_of((2 * ys + x) * width + c * chunk, chunk), chunk
            )
            cp = pltpu.make_async_remote_copy(
                src_ref=relay.at[c, ys],
                dst_ref=ga_ref.at[:, place],
                send_sem=relay_send.at[c, ys],
                recv_sem=out_recv.at[0],
                device_id=(p, 2 * (1 - x) + core),
                device_id_type=MESH,
            )
            cp.start()
            forwarded.append(cp)

    for item in sent:
        wait_sent(item)
    for cp in swaps + copies + last + forwarded:
        cp.wait_send()

    @pl.when(core == 0)
    def _():
        for c in range(n_chunks):
            for k in range(1, n_dp + 1):
                to = (p + k) % n_dp
                piece = grad.at[0:rows_a, 0:chunk]

                @pl.when(jnp.logical_not(jnp.logical_and(to == p, core == z % 2)))
                def _():
                    pltpu.make_async_copy(piece, piece, out_send.at[c, k - 1]).wait()

    @pl.when(core == 1)
    def _():
        for c in range(n_chunks):
            for k in range(1, n_feat):
                piece = grad.at[0:rows_b, 0:chunk]
                pltpu.make_async_copy(piece, piece, out_send.at[c, k - 1]).wait()

    pltpu.make_async_copy(ga_ref, ga_ref, out_recv.at[0]).wait()
    pltpu.make_async_copy(gb_ref, gb_ref, out_recv.at[1]).wait()


def hand_out(landed_a, landed_b, ga_ref, gb_ref, held_a, held_b, loads, stores):
    moves = ((landed_a, held_a, ga_ref), (landed_b, held_b, gb_ref))
    fetched = [
        pltpu.make_async_copy(src, held, loads.at[i]) for i, (src, held, _) in enumerate(moves)
    ]
    written = [
        pltpu.make_async_copy(held, dst, stores.at[i]) for i, (_, held, dst) in enumerate(moves)
    ]
    for cp in fetched:
        cp.start()
    for first, second in zip(fetched, written):
        first.wait()
        second.start()
    for cp in written:
        cp.wait()


def owned_shards(first_view_outputs, second_view_outputs):
    count = first_view_outputs.shape[0] * lax.axis_size("dp")
    features = first_view_outputs.shape[1] * lax.axis_size("feat")
    width = first_view_outputs.shape[1] // GROUP
    chunk = 256 if width % 256 == 0 else 128
    chunks = width // chunk
    n_blk = count // BLK
    packed_rows = n_blk * (n_blk + 1) // 2 * BLK
    seg = packed_rows // GROUP
    unit = seg // GROUP
    bf16, f32 = jnp.bfloat16, jnp.float32
    dma = pltpu.SemaphoreType.DMA
    any_spec = pl.BlockSpec(memory_space=pl.ANY)
    landed = pl.pallas_call(
        functools.partial(kernel, float(features), chunk),
        out_shape=[
            jax.ShapeDtypeStruct(first_view_outputs.shape, bf16),
            jax.ShapeDtypeStruct(second_view_outputs.shape, bf16),
        ],
        in_specs=[any_spec] * 2,
        out_specs=[any_spec] * 2,
        scratch_shapes=[
            pltpu.VMEM((count, width), bf16),
            pltpu.VMEM((count, width), f32),
            pltpu.VMEM((8, width), f32),
            pltpu.VMEM((count, width), bf16),
            pltpu.VMEM((count, width), bf16),
            pltpu.VMEM((count, width), f32),
            pltpu.VMEM((packed_rows, BLK), f32),
            pltpu.VMEM((packed_rows, BLK), bf16),
            pltpu.VMEM((GROUP, GROUP - 1, unit, BLK), bf16),
            pltpu.VMEM((GROUP - 1, unit, BLK), bf16),
            pltpu.VMEM((GROUP - 1, unit, BLK), bf16),
            pltpu.VMEM((seg, BLK), bf16),
            pltpu.VMEM((packed_rows, BLK), bf16),
            pltpu.VMEM((count, count), bf16),
            pltpu.VMEM((count, width), bf16),
            pltpu.VMEM((chunks, 2, first_view_outputs.shape[0], chunk), bf16),
            dma((chunks, GROUP + 2)),
            dma((chunks,)),
            dma((chunks,)),
            dma((chunks,)),
            dma((GROUP, GROUP - 1)),
            dma((GROUP, GROUP - 1)),
            dma((GROUP - 1,)),
            dma((GROUP - 1,)),
            dma((GROUP - 1,)),
            dma((GROUP - 1,)),
            dma((GROUP, GROUP)),
            dma((GROUP, GROUP)),
            dma((chunks, 8)),
            dma((2,)),
            dma((chunks, 2)),
            dma((chunks,)),
        ],
        compiler_params=pltpu.CompilerParams(
            collective_id=0, has_side_effects=True, vmem_limit_bytes=60 * 1024 * 1024
        ),
        name="owned_columns",
    )(first_view_outputs, second_view_outputs)
    return pl.pallas_call(
        hand_out,
        out_shape=[
            jax.ShapeDtypeStruct(first_view_outputs.shape, bf16),
            jax.ShapeDtypeStruct(second_view_outputs.shape, bf16),
        ],
        in_specs=[any_spec] * 2,
        out_specs=[any_spec] * 2,
        scratch_shapes=[
            pltpu.VMEM(first_view_outputs.shape, bf16),
            pltpu.VMEM(second_view_outputs.shape, bf16),
            dma((2,)),
            dma((2,)),
        ],
        name="hand_out",
    )(*landed)


def shards(first_view_outputs, second_view_outputs):
    rows_a, width_a = first_view_outputs.shape
    rows_b, width_b = second_view_outputs.shape
    fits = (
        lax.axis_size("dp") == 8
        and lax.axis_size("feat") == 4
        and rows_a % 16 == 0
        and rows_b == 2 * rows_a
        and width_a == 2 * width_b
        and width_a % (GROUP * BLK) == 0
        and (8 * rows_a) % (4 * BLK) == 0
        and 8 * rows_a <= 1024
    )
    plan = owned_shards if fits else general_shards
    return plan(first_view_outputs, second_view_outputs)


def solution(mesh):
    placed = (P("dp", "feat"), P("feat", "dp"))
    return jax.shard_map(
        shards,
        mesh=mesh,
        in_specs=placed,
        out_specs=(P("dp", "feat"), P("feat", "dp")),
        check_vma=False,
    )
```

```python
import functools
import jax
import jax.numpy as jnp
from jax import lax
from jax.experimental import pallas as pl
from jax.experimental.pallas import tpu as pltpu
from jax.sharding import PartitionSpec as P

EPSILON = 1e-05
OFF_WEIGHT = 0.0051
MESH = pl.DeviceIdType.MESH
BLK = 128
GROUP = 4


def normalize_backward(
    normalized_gradient, standardized_values, inverse_scale, column_sums, total_count
):
    centering_term = column_sums[0] / total_count
    projection_term = column_sums[1] / total_count
    return (
        (normalized_gradient - centering_term - standardized_values * projection_term)
        * inverse_scale
    ).astype(jnp.bfloat16)


def general_shards(first_view_outputs, second_view_outputs):
    rows_a, width_a = first_view_outputs.shape
    rows_b, width_b = second_view_outputs.shape
    total_count = rows_a * lax.axis_size("dp")

    def standardize(values, axis):
        local = values.astype(jnp.float32)
        center = lax.psum(jnp.sum(local, axis=0), axis) / total_count
        centered = local - center
        spread = lax.psum(jnp.sum(centered * centered, axis=0), axis) / total_count
        inverse = lax.rsqrt(spread + EPSILON)
        standardized = centered * inverse
        gathered = lax.all_gather(standardized.astype(jnp.bfloat16), axis, axis=0, tiled=True)
        return standardized, inverse, gathered

    standardized_first, inverse_first, normalized_first = standardize(first_view_outputs, "dp")
    standardized_second, inverse_second, normalized_second = standardize(
        second_view_outputs, "feat"
    )
    correlation = (
        lax.dot_general(
            normalized_first,
            normalized_second,
            (((0,), (0,)), ((), ())),
            preferred_element_type=jnp.float32,
        )
        / total_count
    )
    row_ids = lax.axis_index("feat") * width_a + lax.broadcasted_iota(
        jnp.int32, (width_a, width_b), 0
    )
    col_ids = lax.axis_index("dp") * width_b + lax.broadcasted_iota(
        jnp.int32, (width_a, width_b), 1
    )
    grad_tile = jnp.where(
        row_ids == col_ids, 2.0 * (correlation - 1.0), 2.0 * OFF_WEIGHT * correlation
    ).astype(jnp.bfloat16)

    def finish(partial, axis, standardized, inverse):
        gradient = lax.psum_scatter(
            partial.astype(jnp.bfloat16), axis, scatter_dimension=0, tiled=True
        ).astype(jnp.float32)
        sums = lax.psum(
            (jnp.sum(gradient, axis=0), jnp.sum(gradient * standardized, axis=0)), axis
        )
        return normalize_backward(gradient, standardized, inverse, sums, total_count)

    partial_first = lax.dot_general(
        normalized_second,
        grad_tile,
        (((1,), (1,)), ((), ())),
        preferred_element_type=jnp.float32,
    )
    partial_second = jnp.dot(normalized_first, grad_tile, preferred_element_type=jnp.float32)
    return (
        finish(partial_first, "dp", standardized_first, inverse_first),
        finish(partial_second, "feat", standardized_second, inverse_second),
    )


def kernel(
    features,
    chunk,
    a_ref,
    b_ref,
    ga_ref,
    gb_ref,
    raw,
    xhat,
    inv,
    norm,
    other,
    base,
    running,
    packed,
    r1,
    s1,
    r2,
    gathered,
    full_packed,
    gram,
    grad,
    relay,
    in_send,
    in_recv,
    swap_send,
    swap_recv,
    rs1_send,
    rs1_recv,
    rs2_send,
    rs2_recv,
    ag1_send,
    ag1_recv,
    ag2_send,
    ag2_recv,
    out_send,
    out_recv,
    relay_send,
    relay_recv,
):
    n_dp, n_feat = 8, 4
    n_dev = n_dp * n_feat
    p = lax.axis_index("dp")
    f = lax.axis_index("feat")
    z, y = p // 2, p % 2
    x, core = f // 2, f % 2
    g = 2 * y + x
    rows_a = a_ref.shape[0]
    rows_b = b_ref.shape[0]
    count, width = raw.shape
    n_chunks = width // chunk
    n_blk = count // BLK
    seg = packed.shape[0] // GROUP
    unit = seg // GROUP

    barrier = pltpu.get_barrier_semaphore()
    me = p * n_feat + f

    def greet(k, carry):
        t = (me + k) % n_dev
        pl.semaphore_signal(
            barrier, inc=1, device_id=(t // n_feat, t % n_feat), device_id_type=MESH
        )
        return carry

    lax.fori_loop(1, n_dev, greet, 0)
    pl.semaphore_wait(barrier, n_dev - 1)

    def start_or_local(src, dst, send_sem, recv_sem, device, is_self):
        cp = pltpu.make_async_remote_copy(
            src_ref=src,
            dst_ref=dst,
            send_sem=send_sem,
            recv_sem=recv_sem,
            device_id=device,
            device_id_type=MESH,
        )

        @pl.when(is_self)
        def _():
            pltpu.make_async_copy(src, dst, recv_sem).start()

        @pl.when(jnp.logical_not(is_self))
        def _():
            cp.start()

        return cp, is_self

    def wait_sent(item):
        cp, is_self = item

        @pl.when(jnp.logical_not(is_self))
        def _():
            cp.wait_send()

    def piece_of_a(c, q):
        return a_ref.at[:, pl.ds(pl.multiple_of(q * width + c * chunk, chunk), chunk)]

    def rows_for_a(c):
        return raw.at[
            pl.ds(pl.multiple_of(p * rows_a, rows_a), rows_a), pl.ds(c * chunk, chunk)
        ]

    sent = []
    crossing = []
    for c in range(n_chunks):
        for ys in range(2):
            cp = pltpu.make_async_remote_copy(
                src_ref=piece_of_a(c, 2 * ys + 1 - x),
                dst_ref=relay.at[c, ys],
                send_sem=relay_send.at[c, ys],
                recv_sem=relay_recv.at[c, ys],
                device_id=(p, 2 * (1 - x) + core),
                device_id_type=MESH,
            )
            cp.start()
            crossing.append(cp)
        for k in range(2):
            y_to = (y + 1 + k) % 2
            dp_to = 2 * f + y_to
            sent.append(
                start_or_local(
                    piece_of_a(c, 2 * y_to + x),
                    rows_for_a(c),
                    in_send.at[c, k],
                    in_recv.at[c],
                    (dp_to, 2 * x),
                    jnp.logical_and(dp_to == p, core == 0),
                )
            )
    for c in range(n_chunks):
        for k in range(2):
            x_to = (x + 1 + k) % 2
            feat_to = 2 * x_to + 1
            sent.append(
                start_or_local(
                    b_ref.at[:, pl.ds(pl.multiple_of(x_to * width + c * chunk, chunk), chunk)],
                    raw.at[
                        pl.ds(pl.multiple_of(f * rows_b, rows_b), rows_b),
                        pl.ds(c * chunk, chunk),
                    ],
                    in_send.at[c, GROUP + k],
                    in_recv.at[c],
                    (p, feat_to),
                    feat_to == f,
                )
            )
    for c in range(n_chunks):
        for ys in range(2):
            crossing[2 * c + ys].wait_recv()
            dp_to = 2 * (2 * (1 - x) + core) + ys
            sent.append(
                start_or_local(
                    relay.at[c, ys],
                    rows_for_a(c),
                    in_send.at[c, 2 + ys],
                    in_recv.at[c],
                    (dp_to, 2 * x),
                    jnp.logical_and(dp_to == p, core == 0),
                )
            )

    eye = jnp.where(
        lax.broadcasted_iota(jnp.int32, (BLK, BLK), 0)
        == lax.broadcasted_iota(jnp.int32, (BLK, BLK), 1),
        jnp.float32(width),
        jnp.float32(0),
    )
    where = {}
    for bi in range(n_blk):
        for bj in range(bi, n_blk):
            where[bi, bj] = len(where)
    swaps = []
    for c in range(n_chunks):
        part = raw.at[:, pl.ds(c * chunk, chunk)]
        pltpu.make_async_copy(part, part, in_recv.at[c]).wait()
        for h in range(c * chunk, (c + 1) * chunk, BLK):
            cols = slice(h, h + BLK)
            values = raw[:, cols].astype(jnp.float32)
            center = jnp.sum(values, axis=0, keepdims=True) / count
            centered = values - center
            spread = jnp.sum(centered * centered, axis=0, keepdims=True) / count
            inverse = lax.rsqrt(spread + EPSILON)
            standardized = centered * inverse
            xhat[:, cols] = standardized
            norm[:, cols] = standardized.astype(jnp.bfloat16)
            inv[0:1, cols] = inverse
        cols = slice(c * chunk, (c + 1) * chunk)
        for bi in range(n_blk):
            share = lax.dot_general(
                norm[bi * BLK : (bi + 1) * BLK, cols],
                norm[bi * BLK :, cols],
                (((1,), (1,)), ((), ())),
                preferred_element_type=jnp.float32,
            )
            for bj in range(bi, n_blk):
                at = slice(where[bi, bj] * BLK, (where[bi, bj] + 1) * BLK)
                block = share[:, (bj - bi) * BLK : (bj - bi + 1) * BLK]
                if bi == bj and c == 0:
                    block = block - eye
                if c > 0:
                    block = block + running[at, :]
                if c < n_chunks - 1:
                    running[at, :] = block
                else:
                    packed[at, :] = block.astype(jnp.bfloat16)
        swap = pltpu.make_async_remote_copy(
            src_ref=norm.at[:, pl.ds(c * chunk, chunk)],
            dst_ref=other.at[:, pl.ds(c * chunk, chunk)],
            send_sem=swap_send.at[c],
            recv_sem=swap_recv.at[c],
            device_id=(p, 2 * x + 1 - core),
            device_id_type=MESH,
        )
        swaps.append(swap)
        if c < n_chunks - 1:
            swap.start()

    copies = []
    arriving = {}
    for kz in range(1, GROUP + 1):
        zt = (z + kz) % GROUP
        for k in range(1, GROUP):
            q = (g + k) % GROUP
            cp = pltpu.make_async_remote_copy(
                src_ref=packed.at[pl.ds(pl.multiple_of(q * seg + zt * unit, unit), unit), :],
                dst_ref=r1.at[kz - 1, k - 1],
                send_sem=rs1_send.at[kz - 1, k - 1],
                recv_sem=rs1_recv.at[kz - 1, k - 1],
                device_id=(2 * z + q // 2, 2 * (q % 2) + core),
                device_id_type=MESH,
            )
            cp.start()
            arriving[kz, k] = cp
            copies.append(cp)
    swaps[-1].start()
    coming = []
    for kz in range(1, GROUP + 1):
        zt = (z + kz) % GROUP
        total = packed[pl.ds(pl.multiple_of(g * seg + zt * unit, unit), unit), :].astype(
            jnp.float32
        )
        for k in range(1, GROUP):
            arriving[kz, k].wait_recv()
            total = total + r1[kz - 1, k - 1].astype(jnp.float32)
        if kz < GROUP:
            s1[kz - 1] = total.astype(jnp.bfloat16)
            cp = pltpu.make_async_remote_copy(
                src_ref=s1.at[kz - 1],
                dst_ref=r2.at[kz - 1],
                send_sem=rs2_send.at[kz - 1],
                recv_sem=rs2_recv.at[kz - 1],
                device_id=(2 * zt + y, f),
                device_id_type=MESH,
            )
            cp.start()
            coming.append(cp)
    for kz in range(1, GROUP):
        coming[kz - 1].wait_recv()
        total = total + r2[kz - 1].astype(jnp.float32)
    copies += coming
    mine = pl.ds(pl.multiple_of(z * unit, unit), unit)
    gathered[mine, :] = total.astype(jnp.bfloat16)

    coming = []
    for kz in range(1, GROUP):
        zt = (z + kz) % GROUP
        cp = pltpu.make_async_remote_copy(
            src_ref=gathered.at[mine, :],
            dst_ref=gathered.at[mine, :],
            send_sem=ag1_send.at[kz - 1],
            recv_sem=ag1_recv.at[kz - 1],
            device_id=(2 * zt + y, f),
            device_id_type=MESH,
        )
        cp.start()
        coming.append(cp)
    last = []
    for kz in range(GROUP):
        if kz > 0:
            coming[kz - 1].wait_recv()
        zs = (z + GROUP - kz) % GROUP
        for k in range(1, GROUP + 1):
            q = (g + k) % GROUP
            cp = pltpu.make_async_remote_copy(
                src_ref=gathered.at[pl.ds(pl.multiple_of(zs * unit, unit), unit), :],
                dst_ref=full_packed.at[
                    pl.ds(pl.multiple_of(g * seg + zs * unit, unit), unit), :
                ],
                send_sem=ag2_send.at[kz, k - 1],
                recv_sem=ag2_recv.at[kz, k - 1],
                device_id=(2 * z + q // 2, 2 * (q % 2) + 1 - core),
                device_id_type=MESH,
            )
            cp.start()
            last.append(cp)
    copies += coming

    scale = 2.0 * OFF_WEIGHT / count
    for c in range(n_chunks):
        swaps[c].wait_recv()
        cols = slice(c * chunk, (c + 1) * chunk)
        own = norm[:, cols].astype(jnp.float32)
        paired = other[:, cols].astype(jnp.float32)
        corr = jnp.sum(own * paired, axis=0, keepdims=True) / count
        diagonal = 2.0 * (corr - 1.0) - 2.0 * OFF_WEIGHT * corr
        base[:, cols] = own * (scale * features) + paired * diagonal
    for cp in last:
        cp.wait_recv()
    for (bi, bj), at in where.items():
        block = full_packed[at * BLK : (at + 1) * BLK, :]
        gram[bi * BLK : (bi + 1) * BLK, bj * BLK : (bj + 1) * BLK] = block
        if bi != bj:
            gram[bj * BLK : (bj + 1) * BLK, bi * BLK : (bi + 1) * BLK] = block.T

    for c in range(n_chunks):
        cols = slice(c * chunk, (c + 1) * chunk)
        dnorm = base[:, cols] + scale * lax.dot_general(
            gram[...], norm[:, cols], (((1,), (0,)), ((), ())), preferred_element_type=jnp.float32
        )
        standardized = xhat[:, cols]
        centering = jnp.sum(dnorm, axis=0, keepdims=True) / count
        projection = jnp.sum(dnorm * standardized, axis=0, keepdims=True) / count
        grad[:, cols] = (
            (dnorm - centering - standardized * projection) * inv[0:1, cols]
        ).astype(jnp.bfloat16)

        @pl.when(core == 0)
        def _():
            place = pl.ds(pl.multiple_of(g * width + c * chunk, chunk), chunk)
            for k in range(1, n_dp + 1):
                to = (p + k) % n_dp
                is_self = jnp.logical_and(to == p, z == f)
                src = grad.at[pl.ds(pl.multiple_of(to * rows_a, rows_a), rows_a), cols]

                start_or_local(
                    src,
                    ga_ref.at[:, place],
                    out_send.at[c, k - 1],
                    out_recv.at[0],
                    (to, z),
                    is_self,
                )

        @pl.when(core == 1)
        def _():
            place = pl.ds(pl.multiple_of(x * width + c * chunk, chunk), chunk)
            for k in range(1, n_feat + 1):
                to = (f + k) % n_feat
                src = grad.at[pl.ds(pl.multiple_of(to * rows_b, rows_b), rows_b), cols]
                if k == n_feat:
                    pltpu.make_async_copy(src, gb_ref.at[:, place], out_recv.at[1]).start()
                else:
                    pltpu.make_async_remote_copy(
                        src_ref=src,
                        dst_ref=gb_ref.at[:, place],
                        send_sem=out_send.at[c, k - 1],
                        recv_sem=out_recv.at[1],
                        device_id=(p, to),
                        device_id_type=MESH,
                    ).start()

    for item in sent:
        wait_sent(item)
    for cp in crossing + swaps + copies + last:
        cp.wait_send()

    @pl.when(core == 0)
    def _():
        for c in range(n_chunks):
            for k in range(1, n_dp + 1):
                to = (p + k) % n_dp
                piece = grad.at[0:rows_a, 0:chunk]

                @pl.when(jnp.logical_not(jnp.logical_and(to == p, z == f)))
                def _():
                    pltpu.make_async_copy(piece, piece, out_send.at[c, k - 1]).wait()

    @pl.when(core == 1)
    def _():
        for c in range(n_chunks):
            for k in range(1, n_feat):
                piece = grad.at[0:rows_b, 0:chunk]
                pltpu.make_async_copy(piece, piece, out_send.at[c, k - 1]).wait()

    pltpu.make_async_copy(ga_ref, ga_ref, out_recv.at[0]).wait()
    pltpu.make_async_copy(gb_ref, gb_ref, out_recv.at[1]).wait()


def hand_out(landed_a, landed_b, ga_ref, gb_ref, held_a, held_b, loads, stores):
    moves = ((landed_a, held_a, ga_ref), (landed_b, held_b, gb_ref))
    fetched = [
        pltpu.make_async_copy(src, held, loads.at[i]) for i, (src, held, _) in enumerate(moves)
    ]
    written = [
        pltpu.make_async_copy(held, dst, stores.at[i]) for i, (_, held, dst) in enumerate(moves)
    ]
    for cp in fetched:
        cp.start()
    for first, second in zip(fetched, written):
        first.wait()
        second.start()
    for cp in written:
        cp.wait()


def owned_shards(first_view_outputs, second_view_outputs):
    count = first_view_outputs.shape[0] * lax.axis_size("dp")
    features = first_view_outputs.shape[1] * lax.axis_size("feat")
    width = first_view_outputs.shape[1] // GROUP
    chunk = 256 if width % 256 == 0 else 128
    chunks = width // chunk
    n_blk = count // BLK
    packed_rows = n_blk * (n_blk + 1) // 2 * BLK
    seg = packed_rows // GROUP
    unit = seg // GROUP
    bf16, f32 = jnp.bfloat16, jnp.float32
    dma = pltpu.SemaphoreType.DMA
    any_spec = pl.BlockSpec(memory_space=pl.ANY)
    landed = pl.pallas_call(
        functools.partial(kernel, float(features), chunk),
        out_shape=[
            jax.ShapeDtypeStruct(first_view_outputs.shape, bf16),
            jax.ShapeDtypeStruct(second_view_outputs.shape, bf16),
        ],
        in_specs=[any_spec] * 2,
        out_specs=[any_spec] * 2,
        scratch_shapes=[
            pltpu.VMEM((count, width), bf16),
            pltpu.VMEM((count, width), f32),
            pltpu.VMEM((8, width), f32),
            pltpu.VMEM((count, width), bf16),
            pltpu.VMEM((count, width), bf16),
            pltpu.VMEM((count, width), f32),
            pltpu.VMEM((packed_rows, BLK), f32),
            pltpu.VMEM((packed_rows, BLK), bf16),
            pltpu.VMEM((GROUP, GROUP - 1, unit, BLK), bf16),
            pltpu.VMEM((GROUP - 1, unit, BLK), bf16),
            pltpu.VMEM((GROUP - 1, unit, BLK), bf16),
            pltpu.VMEM((seg, BLK), bf16),
            pltpu.VMEM((packed_rows, BLK), bf16),
            pltpu.VMEM((count, count), bf16),
            pltpu.VMEM((count, width), bf16),
            pltpu.VMEM((chunks, 2, first_view_outputs.shape[0], chunk), bf16),
            dma((chunks, GROUP + 2)),
            dma((chunks,)),
            dma((chunks,)),
            dma((chunks,)),
            dma((GROUP, GROUP - 1)),
            dma((GROUP, GROUP - 1)),
            dma((GROUP - 1,)),
            dma((GROUP - 1,)),
            dma((GROUP - 1,)),
            dma((GROUP - 1,)),
            dma((GROUP, GROUP)),
            dma((GROUP, GROUP)),
            dma((chunks, 8)),
            dma((2,)),
            dma((chunks, 2)),
            dma((chunks, 2)),
        ],
        compiler_params=pltpu.CompilerParams(
            collective_id=0, has_side_effects=True, vmem_limit_bytes=60 * 1024 * 1024
        ),
        name="owned_columns",
    )(first_view_outputs, second_view_outputs)
    return pl.pallas_call(
        hand_out,
        out_shape=[
            jax.ShapeDtypeStruct(first_view_outputs.shape, bf16),
            jax.ShapeDtypeStruct(second_view_outputs.shape, bf16),
        ],
        in_specs=[any_spec] * 2,
        out_specs=[any_spec] * 2,
        scratch_shapes=[
            pltpu.VMEM(first_view_outputs.shape, bf16),
            pltpu.VMEM(second_view_outputs.shape, bf16),
            dma((2,)),
            dma((2,)),
        ],
        name="hand_out",
    )(*landed)


def shards(first_view_outputs, second_view_outputs):
    rows_a, width_a = first_view_outputs.shape
    rows_b, width_b = second_view_outputs.shape
    fits = (
        lax.axis_size("dp") == 8
        and lax.axis_size("feat") == 4
        and rows_a % 16 == 0
        and rows_b == 2 * rows_a
        and width_a == 2 * width_b
        and width_a % (GROUP * BLK) == 0
        and (8 * rows_a) % (4 * BLK) == 0
        and 8 * rows_a <= 1024
    )
    plan = owned_shards if fits else general_shards
    return plan(first_view_outputs, second_view_outputs)


def solution(mesh):
    placed = (P("dp", "feat"), P("feat", "dp"))
    return jax.shard_map(
        shards,
        mesh=mesh,
        in_specs=placed,
        out_specs=(P("dp", "feat"), P("feat", "dp")),
        check_vma=False,
    )
```

```python
import functools
import jax
import jax.numpy as jnp
from jax import lax
from jax.experimental import pallas as pl
from jax.experimental.pallas import tpu as pltpu
from jax.sharding import PartitionSpec as P

EPSILON = 1e-05
OFF_WEIGHT = 0.0051
MESH = pl.DeviceIdType.MESH
BLK = 128
GROUP = 4


def normalize_backward(
    normalized_gradient, standardized_values, inverse_scale, column_sums, total_count
):
    centering_term = column_sums[0] / total_count
    projection_term = column_sums[1] / total_count
    return (
        (normalized_gradient - centering_term - standardized_values * projection_term)
        * inverse_scale
    ).astype(jnp.bfloat16)


def general_shards(first_view_outputs, second_view_outputs):
    rows_a, width_a = first_view_outputs.shape
    rows_b, width_b = second_view_outputs.shape
    total_count = rows_a * lax.axis_size("dp")

    def standardize(values, axis):
        local = values.astype(jnp.float32)
        center = lax.psum(jnp.sum(local, axis=0), axis) / total_count
        centered = local - center
        spread = lax.psum(jnp.sum(centered * centered, axis=0), axis) / total_count
        inverse = lax.rsqrt(spread + EPSILON)
        standardized = centered * inverse
        gathered = lax.all_gather(standardized.astype(jnp.bfloat16), axis, axis=0, tiled=True)
        return standardized, inverse, gathered

    standardized_first, inverse_first, normalized_first = standardize(first_view_outputs, "dp")
    standardized_second, inverse_second, normalized_second = standardize(
        second_view_outputs, "feat"
    )
    correlation = (
        lax.dot_general(
            normalized_first,
            normalized_second,
            (((0,), (0,)), ((), ())),
            preferred_element_type=jnp.float32,
        )
        / total_count
    )
    row_ids = lax.axis_index("feat") * width_a + lax.broadcasted_iota(
        jnp.int32, (width_a, width_b), 0
    )
    col_ids = lax.axis_index("dp") * width_b + lax.broadcasted_iota(
        jnp.int32, (width_a, width_b), 1
    )
    grad_tile = jnp.where(
        row_ids == col_ids, 2.0 * (correlation - 1.0), 2.0 * OFF_WEIGHT * correlation
    ).astype(jnp.bfloat16)

    def finish(partial, axis, standardized, inverse):
        gradient = lax.psum_scatter(
            partial.astype(jnp.bfloat16), axis, scatter_dimension=0, tiled=True
        ).astype(jnp.float32)
        sums = lax.psum(
            (jnp.sum(gradient, axis=0), jnp.sum(gradient * standardized, axis=0)), axis
        )
        return normalize_backward(gradient, standardized, inverse, sums, total_count)

    partial_first = lax.dot_general(
        normalized_second,
        grad_tile,
        (((1,), (1,)), ((), ())),
        preferred_element_type=jnp.float32,
    )
    partial_second = jnp.dot(normalized_first, grad_tile, preferred_element_type=jnp.float32)
    return (
        finish(partial_first, "dp", standardized_first, inverse_first),
        finish(partial_second, "feat", standardized_second, inverse_second),
    )


def kernel(
    features,
    chunk,
    a_ref,
    b_ref,
    ga_ref,
    gb_ref,
    raw,
    xhat,
    inv,
    norm,
    other,
    base,
    running,
    packed,
    r1,
    s1,
    r2,
    gathered,
    full_packed,
    gram,
    grad,
    relay,
    in_send,
    in_recv,
    swap_send,
    swap_recv,
    rs1_send,
    rs1_recv,
    rs2_send,
    rs2_recv,
    ag1_send,
    ag1_recv,
    ag2_send,
    ag2_recv,
    out_send,
    out_recv,
    relay_send,
    relay_recv,
):
    n_dp, n_feat = 8, 4
    n_dev = n_dp * n_feat
    p = lax.axis_index("dp")
    f = lax.axis_index("feat")
    z, y = p // 2, p % 2
    x, core = f // 2, f % 2
    g = 2 * y + x
    rows_a = a_ref.shape[0]
    rows_b = b_ref.shape[0]
    count, width = raw.shape
    n_chunks = width // chunk
    n_blk = count // BLK
    seg = packed.shape[0] // GROUP
    unit = seg // GROUP

    barrier = pltpu.get_barrier_semaphore()
    for dp_to in reversed(range(n_dp)):
        for feat_to in range(n_feat):

            @pl.when(jnp.logical_or(p != dp_to, f != feat_to))
            def _():
                pl.semaphore_signal(
                    barrier, inc=1, device_id=(dp_to, feat_to), device_id_type=MESH
                )

    pl.semaphore_wait(barrier, n_dev - 1)

    def start_or_local(src, dst, send_sem, recv_sem, device, is_self):
        cp = pltpu.make_async_remote_copy(
            src_ref=src,
            dst_ref=dst,
            send_sem=send_sem,
            recv_sem=recv_sem,
            device_id=device,
            device_id_type=MESH,
        )

        @pl.when(is_self)
        def _():
            pltpu.make_async_copy(src, dst, recv_sem).start()

        @pl.when(jnp.logical_not(is_self))
        def _():
            cp.start()

        return cp, is_self

    def wait_sent(item):
        cp, is_self = item

        @pl.when(jnp.logical_not(is_self))
        def _():
            cp.wait_send()

    def piece_of_a(c, q):
        return a_ref.at[:, pl.ds(pl.multiple_of(q * width + c * chunk, chunk), chunk)]

    def rows_for_a(c):
        return raw.at[
            pl.ds(pl.multiple_of(p * rows_a, rows_a), rows_a), pl.ds(c * chunk, chunk)
        ]

    sent = []
    crossing = []
    for c in range(n_chunks):
        for ys in range(2):
            cp = pltpu.make_async_remote_copy(
                src_ref=piece_of_a(c, 2 * ys + 1 - x),
                dst_ref=relay.at[c, ys],
                send_sem=relay_send.at[c, ys],
                recv_sem=relay_recv.at[c, ys],
                device_id=(p, 2 * (1 - x) + core),
                device_id_type=MESH,
            )
            cp.start()
            crossing.append(cp)
        for k in range(2):
            y_to = (y + 1 + k) % 2
            dp_to = 2 * f + y_to
            sent.append(
                start_or_local(
                    piece_of_a(c, 2 * y_to + x),
                    rows_for_a(c),
                    in_send.at[c, k],
                    in_recv.at[c],
                    (dp_to, 2 * x),
                    jnp.logical_and(dp_to == p, core == 0),
                )
            )
    for c in range(n_chunks):
        for k in range(2):
            x_to = (x + 1 + k) % 2
            feat_to = 2 * x_to + 1
            sent.append(
                start_or_local(
                    b_ref.at[:, pl.ds(pl.multiple_of(x_to * width + c * chunk, chunk), chunk)],
                    raw.at[
                        pl.ds(pl.multiple_of(f * rows_b, rows_b), rows_b),
                        pl.ds(c * chunk, chunk),
                    ],
                    in_send.at[c, GROUP + k],
                    in_recv.at[c],
                    (p, feat_to),
                    feat_to == f,
                )
            )
    for c in range(n_chunks):
        for ys in range(2):
            crossing[2 * c + ys].wait_recv()
            dp_to = 2 * (2 * (1 - x) + core) + ys
            sent.append(
                start_or_local(
                    relay.at[c, ys],
                    rows_for_a(c),
                    in_send.at[c, 2 + ys],
                    in_recv.at[c],
                    (dp_to, 2 * x),
                    jnp.logical_and(dp_to == p, core == 0),
                )
            )

    eye = jnp.where(
        lax.broadcasted_iota(jnp.int32, (BLK, BLK), 0)
        == lax.broadcasted_iota(jnp.int32, (BLK, BLK), 1),
        jnp.float32(width),
        jnp.float32(0),
    )
    where = {}
    for bi in range(n_blk):
        for bj in range(bi, n_blk):
            where[bi, bj] = len(where)
    swaps = []
    for c in range(n_chunks):
        part = raw.at[:, pl.ds(c * chunk, chunk)]
        pltpu.make_async_copy(part, part, in_recv.at[c]).wait()
        for h in range(c * chunk, (c + 1) * chunk, BLK):
            cols = slice(h, h + BLK)
            values = raw[:, cols].astype(jnp.float32)
            center = jnp.sum(values, axis=0, keepdims=True) / count
            centered = values - center
            spread = jnp.sum(centered * centered, axis=0, keepdims=True) / count
            inverse = lax.rsqrt(spread + EPSILON)
            standardized = centered * inverse
            xhat[:, cols] = standardized
            norm[:, cols] = standardized.astype(jnp.bfloat16)
            inv[0:1, cols] = inverse
        cols = slice(c * chunk, (c + 1) * chunk)
        for bi in range(n_blk):
            share = lax.dot_general(
                norm[bi * BLK : (bi + 1) * BLK, cols],
                norm[bi * BLK :, cols],
                (((1,), (1,)), ((), ())),
                preferred_element_type=jnp.float32,
            )
            for bj in range(bi, n_blk):
                at = slice(where[bi, bj] * BLK, (where[bi, bj] + 1) * BLK)
                block = share[:, (bj - bi) * BLK : (bj - bi + 1) * BLK]
                if bi == bj and c == 0:
                    block = block - eye
                if c > 0:
                    block = block + running[at, :]
                if c < n_chunks - 1:
                    running[at, :] = block
                else:
                    packed[at, :] = block.astype(jnp.bfloat16)
        swap = pltpu.make_async_remote_copy(
            src_ref=norm.at[:, pl.ds(c * chunk, chunk)],
            dst_ref=other.at[:, pl.ds(c * chunk, chunk)],
            send_sem=swap_send.at[c],
            recv_sem=swap_recv.at[c],
            device_id=(p, 2 * x + 1 - core),
            device_id_type=MESH,
        )
        swaps.append(swap)
        if c < n_chunks - 1:
            swap.start()

    copies = []
    arriving = {}
    for kz in range(1, GROUP + 1):
        zt = (z + kz) % GROUP
        for k in range(1, GROUP):
            q = (g + k) % GROUP
            cp = pltpu.make_async_remote_copy(
                src_ref=packed.at[pl.ds(pl.multiple_of(q * seg + zt * unit, unit), unit), :],
                dst_ref=r1.at[kz - 1, k - 1],
                send_sem=rs1_send.at[kz - 1, k - 1],
                recv_sem=rs1_recv.at[kz - 1, k - 1],
                device_id=(2 * z + q // 2, 2 * (q % 2) + core),
                device_id_type=MESH,
            )
            cp.start()
            arriving[kz, k] = cp
            copies.append(cp)
    swaps[-1].start()
    coming = []
    for kz in range(1, GROUP + 1):
        zt = (z + kz) % GROUP
        total = packed[pl.ds(pl.multiple_of(g * seg + zt * unit, unit), unit), :].astype(
            jnp.float32
        )
        for k in range(1, GROUP):
            arriving[kz, k].wait_recv()
            total = total + r1[kz - 1, k - 1].astype(jnp.float32)
        if kz < GROUP:
            s1[kz - 1] = total.astype(jnp.bfloat16)
            cp = pltpu.make_async_remote_copy(
                src_ref=s1.at[kz - 1],
                dst_ref=r2.at[kz - 1],
                send_sem=rs2_send.at[kz - 1],
                recv_sem=rs2_recv.at[kz - 1],
                device_id=(2 * zt + y, f),
                device_id_type=MESH,
            )
            cp.start()
            coming.append(cp)
    for kz in range(1, GROUP):
        coming[kz - 1].wait_recv()
        total = total + r2[kz - 1].astype(jnp.float32)
    copies += coming
    mine = pl.ds(pl.multiple_of(z * unit, unit), unit)
    gathered[mine, :] = total.astype(jnp.bfloat16)

    coming = []
    for kz in range(1, GROUP):
        zt = (z + kz) % GROUP
        cp = pltpu.make_async_remote_copy(
            src_ref=gathered.at[mine, :],
            dst_ref=gathered.at[mine, :],
            send_sem=ag1_send.at[kz - 1],
            recv_sem=ag1_recv.at[kz - 1],
            device_id=(2 * zt + y, f),
            device_id_type=MESH,
        )
        cp.start()
        coming.append(cp)
    last = []
    for kz in range(GROUP):
        if kz > 0:
            coming[kz - 1].wait_recv()
        zs = (z + GROUP - kz) % GROUP
        for k in range(1, GROUP + 1):
            q = (g + k) % GROUP
            cp = pltpu.make_async_remote_copy(
                src_ref=gathered.at[pl.ds(pl.multiple_of(zs * unit, unit), unit), :],
                dst_ref=full_packed.at[
                    pl.ds(pl.multiple_of(g * seg + zs * unit, unit), unit), :
                ],
                send_sem=ag2_send.at[kz, k - 1],
                recv_sem=ag2_recv.at[kz, k - 1],
                device_id=(2 * z + q // 2, 2 * (q % 2) + 1 - core),
                device_id_type=MESH,
            )
            cp.start()
            last.append(cp)
    copies += coming

    scale = 2.0 * OFF_WEIGHT / count
    for c in range(n_chunks):
        swaps[c].wait_recv()
        cols = slice(c * chunk, (c + 1) * chunk)
        own = norm[:, cols].astype(jnp.float32)
        paired = other[:, cols].astype(jnp.float32)
        corr = jnp.sum(own * paired, axis=0, keepdims=True) / count
        diagonal = 2.0 * (corr - 1.0) - 2.0 * OFF_WEIGHT * corr
        base[:, cols] = own * (scale * features) + paired * diagonal
    for cp in last:
        cp.wait_recv()
    for (bi, bj), at in where.items():
        block = full_packed[at * BLK : (at + 1) * BLK, :]
        gram[bi * BLK : (bi + 1) * BLK, bj * BLK : (bj + 1) * BLK] = block
        if bi != bj:
            gram[bj * BLK : (bj + 1) * BLK, bi * BLK : (bi + 1) * BLK] = block.T

    for c in range(n_chunks):
        cols = slice(c * chunk, (c + 1) * chunk)
        dnorm = base[:, cols] + scale * lax.dot_general(
            gram[...], norm[:, cols], (((1,), (0,)), ((), ())), preferred_element_type=jnp.float32
        )
        standardized = xhat[:, cols]
        centering = jnp.sum(dnorm, axis=0, keepdims=True) / count
        projection = jnp.sum(dnorm * standardized, axis=0, keepdims=True) / count
        grad[:, cols] = (
            (dnorm - centering - standardized * projection) * inv[0:1, cols]
        ).astype(jnp.bfloat16)

        @pl.when(core == 0)
        def _():
            place = pl.ds(pl.multiple_of(g * width + c * chunk, chunk), chunk)
            for k in range(1, n_dp + 1):
                to = (p + k) % n_dp
                is_self = jnp.logical_and(to == p, z == f)
                src = grad.at[pl.ds(pl.multiple_of(to * rows_a, rows_a), rows_a), cols]

                start_or_local(
                    src,
                    ga_ref.at[:, place],
                    out_send.at[c, k - 1],
                    out_recv.at[0],
                    (to, z),
                    is_self,
                )

        @pl.when(core == 1)
        def _():
            place = pl.ds(pl.multiple_of(x * width + c * chunk, chunk), chunk)
            for k in range(1, n_feat + 1):
                to = (f + k) % n_feat
                src = grad.at[pl.ds(pl.multiple_of(to * rows_b, rows_b), rows_b), cols]
                if k == n_feat:
                    pltpu.make_async_copy(src, gb_ref.at[:, place], out_recv.at[1]).start()
                else:
                    pltpu.make_async_remote_copy(
                        src_ref=src,
                        dst_ref=gb_ref.at[:, place],
                        send_sem=out_send.at[c, k - 1],
                        recv_sem=out_recv.at[1],
                        device_id=(p, to),
                        device_id_type=MESH,
                    ).start()

    for item in sent:
        wait_sent(item)
    for cp in crossing + swaps + copies + last:
        cp.wait_send()

    @pl.when(core == 0)
    def _():
        for c in range(n_chunks):
            for k in range(1, n_dp + 1):
                to = (p + k) % n_dp
                piece = grad.at[0:rows_a, 0:chunk]

                @pl.when(jnp.logical_not(jnp.logical_and(to == p, z == f)))
                def _():
                    pltpu.make_async_copy(piece, piece, out_send.at[c, k - 1]).wait()

    @pl.when(core == 1)
    def _():
        for c in range(n_chunks):
            for k in range(1, n_feat):
                piece = grad.at[0:rows_b, 0:chunk]
                pltpu.make_async_copy(piece, piece, out_send.at[c, k - 1]).wait()

    pltpu.make_async_copy(ga_ref, ga_ref, out_recv.at[0]).wait()
    pltpu.make_async_copy(gb_ref, gb_ref, out_recv.at[1]).wait()


def hand_out(landed_a, landed_b, ga_ref, gb_ref, held_a, held_b, loads, stores):
    moves = ((landed_a, held_a, ga_ref), (landed_b, held_b, gb_ref))
    fetched = [
        pltpu.make_async_copy(src, held, loads.at[i]) for i, (src, held, _) in enumerate(moves)
    ]
    written = [
        pltpu.make_async_copy(held, dst, stores.at[i]) for i, (_, held, dst) in enumerate(moves)
    ]
    for cp in fetched:
        cp.start()
    for first, second in zip(fetched, written):
        first.wait()
        second.start()
    for cp in written:
        cp.wait()


def owned_shards(first_view_outputs, second_view_outputs):
    count = first_view_outputs.shape[0] * lax.axis_size("dp")
    features = first_view_outputs.shape[1] * lax.axis_size("feat")
    width = first_view_outputs.shape[1] // GROUP
    chunk = 256 if width % 256 == 0 else 128
    chunks = width // chunk
    n_blk = count // BLK
    packed_rows = n_blk * (n_blk + 1) // 2 * BLK
    seg = packed_rows // GROUP
    unit = seg // GROUP
    bf16, f32 = jnp.bfloat16, jnp.float32
    dma = pltpu.SemaphoreType.DMA
    any_spec = pl.BlockSpec(memory_space=pl.ANY)
    landed = pl.pallas_call(
        functools.partial(kernel, float(features), chunk),
        out_shape=[
            pltpu.VMEM(first_view_outputs.shape, bf16),
            pltpu.VMEM(second_view_outputs.shape, bf16),
        ],
        in_specs=[any_spec] * 2,
        out_specs=[pl.BlockSpec(memory_space=pltpu.VMEM)] * 2,
        scratch_shapes=[
            pltpu.VMEM((count, width), bf16),
            pltpu.VMEM((count, width), f32),
            pltpu.VMEM((8, width), f32),
            pltpu.VMEM((count, width), bf16),
            pltpu.VMEM((count, width), bf16),
            pltpu.VMEM((count, width), f32),
            pltpu.VMEM((packed_rows, BLK), f32),
            pltpu.VMEM((packed_rows, BLK), bf16),
            pltpu.VMEM((GROUP, GROUP - 1, unit, BLK), bf16),
            pltpu.VMEM((GROUP - 1, unit, BLK), bf16),
            pltpu.VMEM((GROUP - 1, unit, BLK), bf16),
            pltpu.VMEM((seg, BLK), bf16),
            pltpu.VMEM((packed_rows, BLK), bf16),
            pltpu.VMEM((count, count), bf16),
            pltpu.VMEM((count, width), bf16),
            pltpu.VMEM((chunks, 2, first_view_outputs.shape[0], chunk), bf16),
            dma((chunks, GROUP + 2)),
            dma((chunks,)),
            dma((chunks,)),
            dma((chunks,)),
            dma((GROUP, GROUP - 1)),
            dma((GROUP, GROUP - 1)),
            dma((GROUP - 1,)),
            dma((GROUP - 1,)),
            dma((GROUP - 1,)),
            dma((GROUP - 1,)),
            dma((GROUP, GROUP)),
            dma((GROUP, GROUP)),
            dma((chunks, 8)),
            dma((2,)),
            dma((chunks, 2)),
            dma((chunks, 2)),
        ],
        compiler_params=pltpu.CompilerParams(
            collective_id=0, has_side_effects=True, vmem_limit_bytes=60 * 1024 * 1024
        ),
        name="owned_columns",
    )(first_view_outputs, second_view_outputs)
    return pl.pallas_call(
        hand_out,
        out_shape=[
            jax.ShapeDtypeStruct(first_view_outputs.shape, bf16),
            jax.ShapeDtypeStruct(second_view_outputs.shape, bf16),
        ],
        in_specs=[any_spec] * 2,
        out_specs=[any_spec] * 2,
        scratch_shapes=[
            pltpu.VMEM(first_view_outputs.shape, bf16),
            pltpu.VMEM(second_view_outputs.shape, bf16),
            dma((2,)),
            dma((2,)),
        ],
        name="hand_out",
    )(*landed)


def shards(first_view_outputs, second_view_outputs):
    rows_a, width_a = first_view_outputs.shape
    rows_b, width_b = second_view_outputs.shape
    fits = (
        lax.axis_size("dp") == 8
        and lax.axis_size("feat") == 4
        and rows_a % 16 == 0
        and rows_b == 2 * rows_a
        and width_a == 2 * width_b
        and width_a % (GROUP * BLK) == 0
        and (8 * rows_a) % (4 * BLK) == 0
        and 8 * rows_a <= 1024
    )
    plan = owned_shards if fits else general_shards
    return plan(first_view_outputs, second_view_outputs)


def solution(mesh):
    placed = (P("dp", "feat"), P("feat", "dp"))
    return jax.shard_map(
        shards,
        mesh=mesh,
        in_specs=placed,
        out_specs=(P("dp", "feat"), P("feat", "dp")),
        check_vma=False,
    )
```

```python
import functools
import jax
import jax.numpy as jnp
from jax import lax
from jax.experimental import pallas as pl
from jax.experimental.pallas import tpu as pltpu
from jax.sharding import PartitionSpec as P

EPSILON = 1e-05
OFF_WEIGHT = 0.0051
MESH = pl.DeviceIdType.MESH
BLK = 128
GROUP = 4


def normalize_backward(
    normalized_gradient, standardized_values, inverse_scale, column_sums, total_count
):
    centering_term = column_sums[0] / total_count
    projection_term = column_sums[1] / total_count
    return (
        (normalized_gradient - centering_term - standardized_values * projection_term)
        * inverse_scale
    ).astype(jnp.bfloat16)


def general_shards(first_view_outputs, second_view_outputs):
    rows_a, width_a = first_view_outputs.shape
    rows_b, width_b = second_view_outputs.shape
    total_count = rows_a * lax.axis_size("dp")

    def standardize(values, axis):
        local = values.astype(jnp.float32)
        center = lax.psum(jnp.sum(local, axis=0), axis) / total_count
        centered = local - center
        spread = lax.psum(jnp.sum(centered * centered, axis=0), axis) / total_count
        inverse = lax.rsqrt(spread + EPSILON)
        standardized = centered * inverse
        gathered = lax.all_gather(standardized.astype(jnp.bfloat16), axis, axis=0, tiled=True)
        return standardized, inverse, gathered

    standardized_first, inverse_first, normalized_first = standardize(first_view_outputs, "dp")
    standardized_second, inverse_second, normalized_second = standardize(
        second_view_outputs, "feat"
    )
    correlation = (
        lax.dot_general(
            normalized_first,
            normalized_second,
            (((0,), (0,)), ((), ())),
            preferred_element_type=jnp.float32,
        )
        / total_count
    )
    row_ids = lax.axis_index("feat") * width_a + lax.broadcasted_iota(
        jnp.int32, (width_a, width_b), 0
    )
    col_ids = lax.axis_index("dp") * width_b + lax.broadcasted_iota(
        jnp.int32, (width_a, width_b), 1
    )
    grad_tile = jnp.where(
        row_ids == col_ids, 2.0 * (correlation - 1.0), 2.0 * OFF_WEIGHT * correlation
    ).astype(jnp.bfloat16)

    def finish(partial, axis, standardized, inverse):
        gradient = lax.psum_scatter(
            partial.astype(jnp.bfloat16), axis, scatter_dimension=0, tiled=True
        ).astype(jnp.float32)
        sums = lax.psum(
            (jnp.sum(gradient, axis=0), jnp.sum(gradient * standardized, axis=0)), axis
        )
        return normalize_backward(gradient, standardized, inverse, sums, total_count)

    partial_first = lax.dot_general(
        normalized_second,
        grad_tile,
        (((1,), (1,)), ((), ())),
        preferred_element_type=jnp.float32,
    )
    partial_second = jnp.dot(normalized_first, grad_tile, preferred_element_type=jnp.float32)
    return (
        finish(partial_first, "dp", standardized_first, inverse_first),
        finish(partial_second, "feat", standardized_second, inverse_second),
    )


def kernel(
    features,
    chunk,
    a_ref,
    b_ref,
    ga_ref,
    gb_ref,
    raw,
    xhat,
    inv,
    norm,
    other,
    base,
    running,
    packed,
    r1,
    s1,
    r2,
    gathered,
    full_packed,
    gram,
    grad,
    relay,
    in_send,
    in_recv,
    swap_send,
    swap_recv,
    rs1_send,
    rs1_recv,
    rs2_send,
    rs2_recv,
    ag1_send,
    ag1_recv,
    ag2_send,
    ag2_recv,
    out_send,
    out_recv,
    relay_send,
    relay_recv,
):
    n_dp, n_feat = 8, 4
    n_dev = n_dp * n_feat
    p = lax.axis_index("dp")
    f = lax.axis_index("feat")
    z, y = p // 2, p % 2
    x, core = f // 2, f % 2
    g = 2 * y + x
    rows_a = a_ref.shape[0]
    rows_b = b_ref.shape[0]
    count, width = raw.shape
    n_chunks = width // chunk
    n_blk = count // BLK
    seg = packed.shape[0] // GROUP
    unit = seg // GROUP

    barrier = pltpu.get_barrier_semaphore()
    for dp_to in reversed(range(n_dp)):
        for feat_to in range(n_feat):

            @pl.when(jnp.logical_or(p != dp_to, f != feat_to))
            def _():
                pl.semaphore_signal(
                    barrier, inc=1, device_id=(dp_to, feat_to), device_id_type=MESH
                )

    pl.semaphore_wait(barrier, n_dev - 1)

    def start_or_local(src, dst, send_sem, recv_sem, device, is_self):
        cp = pltpu.make_async_remote_copy(
            src_ref=src,
            dst_ref=dst,
            send_sem=send_sem,
            recv_sem=recv_sem,
            device_id=device,
            device_id_type=MESH,
        )

        @pl.when(is_self)
        def _():
            pltpu.make_async_copy(src, dst, recv_sem).start()

        @pl.when(jnp.logical_not(is_self))
        def _():
            cp.start()

        return cp, is_self

    def wait_sent(item):
        cp, is_self = item

        @pl.when(jnp.logical_not(is_self))
        def _():
            cp.wait_send()

    def piece_of_a(c, q):
        return a_ref.at[:, pl.ds(pl.multiple_of(q * width + c * chunk, chunk), chunk)]

    def rows_for_a(c):
        return raw.at[
            pl.ds(pl.multiple_of(p * rows_a, rows_a), rows_a), pl.ds(c * chunk, chunk)
        ]

    sent = []
    crossing = []
    for c in range(n_chunks):
        for ys in range(2):
            cp = pltpu.make_async_remote_copy(
                src_ref=piece_of_a(c, 2 * ys + 1 - x),
                dst_ref=relay.at[c, ys],
                send_sem=relay_send.at[c, ys],
                recv_sem=relay_recv.at[c, ys],
                device_id=(p, 2 * (1 - x) + core),
                device_id_type=MESH,
            )
            cp.start()
            crossing.append(cp)
        for k in range(2):
            y_to = (y + 1 + k) % 2
            dp_to = 2 * f + y_to
            sent.append(
                start_or_local(
                    piece_of_a(c, 2 * y_to + x),
                    rows_for_a(c),
                    in_send.at[c, k],
                    in_recv.at[c],
                    (dp_to, 2 * x),
                    jnp.logical_and(dp_to == p, core == 0),
                )
            )
    for c in range(n_chunks):
        for k in range(2):
            x_to = (x + 1 + k) % 2
            feat_to = 2 * x_to + 1
            sent.append(
                start_or_local(
                    b_ref.at[:, pl.ds(pl.multiple_of(x_to * width + c * chunk, chunk), chunk)],
                    raw.at[
                        pl.ds(pl.multiple_of(f * rows_b, rows_b), rows_b),
                        pl.ds(c * chunk, chunk),
                    ],
                    in_send.at[c, GROUP + k],
                    in_recv.at[c],
                    (p, feat_to),
                    feat_to == f,
                )
            )
    for c in range(n_chunks):
        for ys in range(2):
            crossing[2 * c + ys].wait_recv()
            dp_to = 2 * (2 * (1 - x) + core) + ys
            sent.append(
                start_or_local(
                    relay.at[c, ys],
                    rows_for_a(c),
                    in_send.at[c, 2 + ys],
                    in_recv.at[c],
                    (dp_to, 2 * x),
                    jnp.logical_and(dp_to == p, core == 0),
                )
            )

    eye = jnp.where(
        lax.broadcasted_iota(jnp.int32, (BLK, BLK), 0)
        == lax.broadcasted_iota(jnp.int32, (BLK, BLK), 1),
        jnp.float32(width),
        jnp.float32(0),
    )
    where = {}
    for bi in range(n_blk):
        for bj in range(bi, n_blk):
            where[bi, bj] = len(where)
    swaps = []
    for c in range(n_chunks):
        part = raw.at[:, pl.ds(c * chunk, chunk)]
        pltpu.make_async_copy(part, part, in_recv.at[c]).wait()
        for h in range(c * chunk, (c + 1) * chunk, BLK):
            cols = slice(h, h + BLK)
            values = raw[:, cols].astype(jnp.float32)
            center = jnp.sum(values, axis=0, keepdims=True) / count
            centered = values - center
            spread = jnp.sum(centered * centered, axis=0, keepdims=True) / count
            inverse = lax.rsqrt(spread + EPSILON)
            standardized = centered * inverse
            xhat[:, cols] = standardized
            norm[:, cols] = standardized.astype(jnp.bfloat16)
            inv[0:1, cols] = inverse
        cols = slice(c * chunk, (c + 1) * chunk)
        for bi in range(n_blk):
            share = lax.dot_general(
                norm[bi * BLK : (bi + 1) * BLK, cols],
                norm[bi * BLK :, cols],
                (((1,), (1,)), ((), ())),
                preferred_element_type=jnp.float32,
            )
            for bj in range(bi, n_blk):
                at = slice(where[bi, bj] * BLK, (where[bi, bj] + 1) * BLK)
                block = share[:, (bj - bi) * BLK : (bj - bi + 1) * BLK]
                if bi == bj and c == 0:
                    block = block - eye
                if c > 0:
                    block = block + running[at, :]
                if c < n_chunks - 1:
                    running[at, :] = block
                else:
                    packed[at, :] = block.astype(jnp.bfloat16)
        swap = pltpu.make_async_remote_copy(
            src_ref=norm.at[:, pl.ds(c * chunk, chunk)],
            dst_ref=other.at[:, pl.ds(c * chunk, chunk)],
            send_sem=swap_send.at[c],
            recv_sem=swap_recv.at[c],
            device_id=(p, 2 * x + 1 - core),
            device_id_type=MESH,
        )
        swaps.append(swap)
        if c < n_chunks - 1:
            swap.start()

    copies = []
    arriving = {}
    for kz in range(1, GROUP + 1):
        zt = (z + kz) % GROUP
        for k in range(1, GROUP):
            q = (g + k) % GROUP
            cp = pltpu.make_async_remote_copy(
                src_ref=packed.at[pl.ds(pl.multiple_of(q * seg + zt * unit, unit), unit), :],
                dst_ref=r1.at[kz - 1, k - 1],
                send_sem=rs1_send.at[kz - 1, k - 1],
                recv_sem=rs1_recv.at[kz - 1, k - 1],
                device_id=(2 * z + q // 2, 2 * (q % 2) + core),
                device_id_type=MESH,
            )
            cp.start()
            arriving[kz, k] = cp
            copies.append(cp)
    swaps[-1].start()
    coming = []
    for kz in range(1, GROUP + 1):
        zt = (z + kz) % GROUP
        total = packed[pl.ds(pl.multiple_of(g * seg + zt * unit, unit), unit), :].astype(
            jnp.float32
        )
        for k in range(1, GROUP):
            arriving[kz, k].wait_recv()
            total = total + r1[kz - 1, k - 1].astype(jnp.float32)
        if kz < GROUP:
            s1[kz - 1] = total.astype(jnp.bfloat16)
            cp = pltpu.make_async_remote_copy(
                src_ref=s1.at[kz - 1],
                dst_ref=r2.at[kz - 1],
                send_sem=rs2_send.at[kz - 1],
                recv_sem=rs2_recv.at[kz - 1],
                device_id=(2 * zt + y, f),
                device_id_type=MESH,
            )
            cp.start()
            coming.append(cp)
    for kz in range(1, GROUP):
        coming[kz - 1].wait_recv()
        total = total + r2[kz - 1].astype(jnp.float32)
    copies += coming
    mine = pl.ds(pl.multiple_of(z * unit, unit), unit)
    gathered[mine, :] = total.astype(jnp.bfloat16)

    coming = []
    for kz in range(1, GROUP):
        zt = (z + kz) % GROUP
        cp = pltpu.make_async_remote_copy(
            src_ref=gathered.at[mine, :],
            dst_ref=gathered.at[mine, :],
            send_sem=ag1_send.at[kz - 1],
            recv_sem=ag1_recv.at[kz - 1],
            device_id=(2 * zt + y, f),
            device_id_type=MESH,
        )
        cp.start()
        coming.append(cp)
    last = []
    for kz in range(GROUP):
        if kz > 0:
            coming[kz - 1].wait_recv()
        zs = (z + GROUP - kz) % GROUP
        for k in range(1, GROUP + 1):
            q = (g + k) % GROUP
            cp = pltpu.make_async_remote_copy(
                src_ref=gathered.at[pl.ds(pl.multiple_of(zs * unit, unit), unit), :],
                dst_ref=full_packed.at[
                    pl.ds(pl.multiple_of(g * seg + zs * unit, unit), unit), :
                ],
                send_sem=ag2_send.at[kz, k - 1],
                recv_sem=ag2_recv.at[kz, k - 1],
                device_id=(2 * z + q // 2, 2 * (q % 2) + 1 - core),
                device_id_type=MESH,
            )
            cp.start()
            last.append(cp)
    copies += coming

    scale = 2.0 * OFF_WEIGHT / count
    for c in range(n_chunks):
        swaps[c].wait_recv()
        cols = slice(c * chunk, (c + 1) * chunk)
        own = norm[:, cols].astype(jnp.float32)
        paired = other[:, cols].astype(jnp.float32)
        corr = jnp.sum(own * paired, axis=0, keepdims=True) / count
        diagonal = 2.0 * (corr - 1.0) - 2.0 * OFF_WEIGHT * corr
        base[:, cols] = own * (scale * features) + paired * diagonal
    for cp in last:
        cp.wait_recv()
    for (bi, bj), at in where.items():
        block = full_packed[at * BLK : (at + 1) * BLK, :]
        gram[bi * BLK : (bi + 1) * BLK, bj * BLK : (bj + 1) * BLK] = block
        if bi != bj:
            gram[bj * BLK : (bj + 1) * BLK, bi * BLK : (bi + 1) * BLK] = block.T

    for c in range(n_chunks):
        cols = slice(c * chunk, (c + 1) * chunk)
        dnorm = base[:, cols] + scale * lax.dot_general(
            gram[...], norm[:, cols], (((1,), (0,)), ((), ())), preferred_element_type=jnp.float32
        )
        standardized = xhat[:, cols]
        centering = jnp.sum(dnorm, axis=0, keepdims=True) / count
        projection = jnp.sum(dnorm * standardized, axis=0, keepdims=True) / count
        grad[:, cols] = (
            (dnorm - centering - standardized * projection) * inv[0:1, cols]
        ).astype(jnp.bfloat16)

        @pl.when(core == 0)
        def _():
            place = pl.ds(pl.multiple_of(g * width + c * chunk, chunk), chunk)
            for k in range(1, n_dp + 1):
                to = (p + k) % n_dp
                is_self = jnp.logical_and(to == p, z == f)
                src = grad.at[pl.ds(pl.multiple_of(to * rows_a, rows_a), rows_a), cols]

                start_or_local(
                    src,
                    ga_ref.at[:, place],
                    out_send.at[c, k - 1],
                    out_recv.at[0],
                    (to, z),
                    is_self,
                )

        @pl.when(core == 1)
        def _():
            place = pl.ds(pl.multiple_of(x * width + c * chunk, chunk), chunk)
            for k in range(1, n_feat + 1):
                to = (f + k) % n_feat
                src = grad.at[pl.ds(pl.multiple_of(to * rows_b, rows_b), rows_b), cols]
                if k == n_feat:
                    pltpu.make_async_copy(src, gb_ref.at[:, place], out_recv.at[1]).start()
                else:
                    pltpu.make_async_remote_copy(
                        src_ref=src,
                        dst_ref=gb_ref.at[:, place],
                        send_sem=out_send.at[c, k - 1],
                        recv_sem=out_recv.at[1],
                        device_id=(p, to),
                        device_id_type=MESH,
                    ).start()

    for item in sent:
        wait_sent(item)
    for cp in crossing + swaps + copies + last:
        cp.wait_send()

    @pl.when(core == 0)
    def _():
        for c in range(n_chunks):
            for k in range(1, n_dp + 1):
                to = (p + k) % n_dp
                piece = grad.at[0:rows_a, 0:chunk]

                @pl.when(jnp.logical_not(jnp.logical_and(to == p, z == f)))
                def _():
                    pltpu.make_async_copy(piece, piece, out_send.at[c, k - 1]).wait()

    @pl.when(core == 1)
    def _():
        for c in range(n_chunks):
            for k in range(1, n_feat):
                piece = grad.at[0:rows_b, 0:chunk]
                pltpu.make_async_copy(piece, piece, out_send.at[c, k - 1]).wait()

    pltpu.make_async_copy(ga_ref, ga_ref, out_recv.at[0]).wait()
    pltpu.make_async_copy(gb_ref, gb_ref, out_recv.at[1]).wait()


def hand_out(landed_a, landed_b, ga_ref, gb_ref, stores):
    first = pltpu.make_async_copy(landed_a, ga_ref, stores.at[0])
    second = pltpu.make_async_copy(landed_b, gb_ref, stores.at[1])
    first.start()
    second.start()
    first.wait()
    second.wait()


def owned_shards(first_view_outputs, second_view_outputs):
    count = first_view_outputs.shape[0] * lax.axis_size("dp")
    features = first_view_outputs.shape[1] * lax.axis_size("feat")
    width = first_view_outputs.shape[1] // GROUP
    chunk = 256 if width % 256 == 0 else 128
    chunks = width // chunk
    n_blk = count // BLK
    packed_rows = n_blk * (n_blk + 1) // 2 * BLK
    seg = packed_rows // GROUP
    unit = seg // GROUP
    bf16, f32 = jnp.bfloat16, jnp.float32
    dma = pltpu.SemaphoreType.DMA
    any_spec = pl.BlockSpec(memory_space=pl.ANY)
    landed = pl.pallas_call(
        functools.partial(kernel, float(features), chunk),
        out_shape=[
            pltpu.VMEM(first_view_outputs.shape, bf16),
            pltpu.VMEM(second_view_outputs.shape, bf16),
        ],
        in_specs=[any_spec] * 2,
        out_specs=[pl.BlockSpec(memory_space=pltpu.VMEM)] * 2,
        scratch_shapes=[
            pltpu.VMEM((count, width), bf16),
            pltpu.VMEM((count, width), f32),
            pltpu.VMEM((8, width), f32),
            pltpu.VMEM((count, width), bf16),
            pltpu.VMEM((count, width), bf16),
            pltpu.VMEM((count, width), f32),
            pltpu.VMEM((packed_rows, BLK), f32),
            pltpu.VMEM((packed_rows, BLK), bf16),
            pltpu.VMEM((GROUP, GROUP - 1, unit, BLK), bf16),
            pltpu.VMEM((GROUP - 1, unit, BLK), bf16),
            pltpu.VMEM((GROUP - 1, unit, BLK), bf16),
            pltpu.VMEM((seg, BLK), bf16),
            pltpu.VMEM((packed_rows, BLK), bf16),
            pltpu.VMEM((count, count), bf16),
            pltpu.VMEM((count, width), bf16),
            pltpu.VMEM((chunks, 2, first_view_outputs.shape[0], chunk), bf16),
            dma((chunks, GROUP + 2)),
            dma((chunks,)),
            dma((chunks,)),
            dma((chunks,)),
            dma((GROUP, GROUP - 1)),
            dma((GROUP, GROUP - 1)),
            dma((GROUP - 1,)),
            dma((GROUP - 1,)),
            dma((GROUP - 1,)),
            dma((GROUP - 1,)),
            dma((GROUP, GROUP)),
            dma((GROUP, GROUP)),
            dma((chunks, 8)),
            dma((2,)),
            dma((chunks, 2)),
            dma((chunks, 2)),
        ],
        compiler_params=pltpu.CompilerParams(
            collective_id=0, has_side_effects=True, vmem_limit_bytes=60 * 1024 * 1024
        ),
        name="owned_columns",
    )(first_view_outputs, second_view_outputs)
    return pl.pallas_call(
        hand_out,
        out_shape=[
            jax.ShapeDtypeStruct(first_view_outputs.shape, bf16),
            jax.ShapeDtypeStruct(second_view_outputs.shape, bf16),
        ],
        in_specs=[pl.BlockSpec(memory_space=pltpu.VMEM)] * 2,
        out_specs=[any_spec] * 2,
        scratch_shapes=[dma((2,))],
        compiler_params=pltpu.CompilerParams(vmem_limit_bytes=4 * 1024 * 1024),
        name="hand_out",
    )(*landed)


def shards(first_view_outputs, second_view_outputs):
    rows_a, width_a = first_view_outputs.shape
    rows_b, width_b = second_view_outputs.shape
    fits = (
        lax.axis_size("dp") == 8
        and lax.axis_size("feat") == 4
        and rows_a % 16 == 0
        and rows_b == 2 * rows_a
        and width_a == 2 * width_b
        and width_a % (GROUP * BLK) == 0
        and (8 * rows_a) % (4 * BLK) == 0
        and 8 * rows_a <= 1024
    )
    plan = owned_shards if fits else general_shards
    return plan(first_view_outputs, second_view_outputs)


def solution(mesh):
    placed = (P("dp", "feat"), P("feat", "dp"))
    return jax.shard_map(
        shards,
        mesh=mesh,
        in_specs=placed,
        out_specs=(P("dp", "feat"), P("feat", "dp")),
        check_vma=False,
    )
```

```python
import functools
import jax
import jax.numpy as jnp
from jax import lax
from jax.experimental import pallas as pl
from jax.experimental.pallas import tpu as pltpu
from jax.sharding import PartitionSpec as P

EPSILON = 1e-05
OFF_WEIGHT = 0.0051
MESH = pl.DeviceIdType.MESH
BLK = 128
HOMEWARD = (4, 3, 5, 2, 6, 1, 7, 8)
GROUP = 4


def normalize_backward(
    normalized_gradient, standardized_values, inverse_scale, column_sums, total_count
):
    centering_term = column_sums[0] / total_count
    projection_term = column_sums[1] / total_count
    return (
        (normalized_gradient - centering_term - standardized_values * projection_term)
        * inverse_scale
    ).astype(jnp.bfloat16)


def general_shards(first_view_outputs, second_view_outputs):
    rows_a, width_a = first_view_outputs.shape
    rows_b, width_b = second_view_outputs.shape
    total_count = rows_a * lax.axis_size("dp")

    def standardize(values, axis):
        local = values.astype(jnp.float32)
        center = lax.psum(jnp.sum(local, axis=0), axis) / total_count
        centered = local - center
        spread = lax.psum(jnp.sum(centered * centered, axis=0), axis) / total_count
        inverse = lax.rsqrt(spread + EPSILON)
        standardized = centered * inverse
        gathered = lax.all_gather(standardized.astype(jnp.bfloat16), axis, axis=0, tiled=True)
        return standardized, inverse, gathered

    standardized_first, inverse_first, normalized_first = standardize(first_view_outputs, "dp")
    standardized_second, inverse_second, normalized_second = standardize(
        second_view_outputs, "feat"
    )
    correlation = (
        lax.dot_general(
            normalized_first,
            normalized_second,
            (((0,), (0,)), ((), ())),
            preferred_element_type=jnp.float32,
        )
        / total_count
    )
    row_ids = lax.axis_index("feat") * width_a + lax.broadcasted_iota(
        jnp.int32, (width_a, width_b), 0
    )
    col_ids = lax.axis_index("dp") * width_b + lax.broadcasted_iota(
        jnp.int32, (width_a, width_b), 1
    )
    grad_tile = jnp.where(
        row_ids == col_ids, 2.0 * (correlation - 1.0), 2.0 * OFF_WEIGHT * correlation
    ).astype(jnp.bfloat16)

    def finish(partial, axis, standardized, inverse):
        gradient = lax.psum_scatter(
            partial.astype(jnp.bfloat16), axis, scatter_dimension=0, tiled=True
        ).astype(jnp.float32)
        sums = lax.psum(
            (jnp.sum(gradient, axis=0), jnp.sum(gradient * standardized, axis=0)), axis
        )
        return normalize_backward(gradient, standardized, inverse, sums, total_count)

    partial_first = lax.dot_general(
        normalized_second,
        grad_tile,
        (((1,), (1,)), ((), ())),
        preferred_element_type=jnp.float32,
    )
    partial_second = jnp.dot(normalized_first, grad_tile, preferred_element_type=jnp.float32)
    return (
        finish(partial_first, "dp", standardized_first, inverse_first),
        finish(partial_second, "feat", standardized_second, inverse_second),
    )


def kernel(
    features,
    chunk,
    a_ref,
    b_ref,
    ga_ref,
    gb_ref,
    raw,
    xhat,
    inv,
    norm,
    other,
    base,
    running,
    packed,
    r1,
    s1,
    r2,
    gathered,
    full_packed,
    gram,
    grad,
    relay,
    in_send,
    in_recv,
    swap_send,
    swap_recv,
    rs1_send,
    rs1_recv,
    rs2_send,
    rs2_recv,
    ag1_send,
    ag1_recv,
    ag2_send,
    ag2_recv,
    out_send,
    out_recv,
    relay_send,
    relay_recv,
):
    n_dp, n_feat = 8, 4
    n_dev = n_dp * n_feat
    p = lax.axis_index("dp")
    f = lax.axis_index("feat")
    z, y = p // 2, p % 2
    x, core = f // 2, f % 2
    g = 2 * y + x
    rows_a = a_ref.shape[0]
    rows_b = b_ref.shape[0]
    n_chunks, count, _ = raw.shape
    width = n_chunks * chunk
    n_blk = count // BLK
    seg = packed.shape[0] // GROUP
    unit = seg // GROUP

    barrier = pltpu.get_barrier_semaphore()
    for dp_to in reversed(range(n_dp)):
        for feat_to in range(n_feat):

            @pl.when(jnp.logical_or(p != dp_to, f != feat_to))
            def _():
                pl.semaphore_signal(
                    barrier, inc=1, device_id=(dp_to, feat_to), device_id_type=MESH
                )

    pl.semaphore_wait(barrier, n_dev - 1)

    def start_or_local(src, dst, send_sem, recv_sem, device, is_self):
        cp = pltpu.make_async_remote_copy(
            src_ref=src,
            dst_ref=dst,
            send_sem=send_sem,
            recv_sem=recv_sem,
            device_id=device,
            device_id_type=MESH,
        )

        @pl.when(is_self)
        def _():
            pltpu.make_async_copy(src, dst, recv_sem).start()

        @pl.when(jnp.logical_not(is_self))
        def _():
            cp.start()

        return cp, is_self

    def wait_sent(item):
        cp, is_self = item

        @pl.when(jnp.logical_not(is_self))
        def _():
            cp.wait_send()

    def piece_of_a(c, q):
        return a_ref.at[:, pl.ds(pl.multiple_of(q * width + c * chunk, chunk), chunk)]

    def rows_for_a(c):
        return raw.at[c, pl.ds(pl.multiple_of(p * rows_a, rows_a), rows_a), :]

    sent = []
    crossing = []
    for c in range(n_chunks):
        for ys in range(2):
            cp = pltpu.make_async_remote_copy(
                src_ref=piece_of_a(c, 2 * ys + 1 - x),
                dst_ref=relay.at[c, ys],
                send_sem=relay_send.at[c, ys],
                recv_sem=relay_recv.at[c, ys],
                device_id=(p, 2 * (1 - x) + core),
                device_id_type=MESH,
            )
            cp.start()
            crossing.append(cp)
        for k in range(2):
            y_to = (y + 1 + k) % 2
            dp_to = 2 * f + y_to
            sent.append(
                start_or_local(
                    piece_of_a(c, 2 * y_to + x),
                    rows_for_a(c),
                    in_send.at[c, k],
                    in_recv.at[c],
                    (dp_to, 2 * x),
                    jnp.logical_and(dp_to == p, core == 0),
                )
            )
    for c in range(n_chunks):
        for k in range(2):
            x_to = (x + 1 + k) % 2
            feat_to = 2 * x_to + 1
            sent.append(
                start_or_local(
                    b_ref.at[:, pl.ds(pl.multiple_of(x_to * width + c * chunk, chunk), chunk)],
                    raw.at[c, pl.ds(pl.multiple_of(f * rows_b, rows_b), rows_b), :],
                    in_send.at[c, GROUP + k],
                    in_recv.at[c],
                    (p, feat_to),
                    feat_to == f,
                )
            )
    for c in range(n_chunks):
        for ys in range(2):
            crossing[2 * c + ys].wait_recv()
            dp_to = 2 * (2 * (1 - x) + core) + ys
            sent.append(
                start_or_local(
                    relay.at[c, ys],
                    rows_for_a(c),
                    in_send.at[c, 2 + ys],
                    in_recv.at[c],
                    (dp_to, 2 * x),
                    jnp.logical_and(dp_to == p, core == 0),
                )
            )

    eye = jnp.where(
        lax.broadcasted_iota(jnp.int32, (BLK, BLK), 0)
        == lax.broadcasted_iota(jnp.int32, (BLK, BLK), 1),
        jnp.float32(width),
        jnp.float32(0),
    )
    where = {}
    for bi in range(n_blk):
        for bj in range(bi, n_blk):
            where[bi, bj] = len(where)
    swaps = []
    for c in range(n_chunks):
        pltpu.make_async_copy(raw.at[c], raw.at[c], in_recv.at[c]).wait()
        for h in range(0, chunk, BLK):
            cols = slice(h, h + BLK)
            values = raw[c, :, cols].astype(jnp.float32)
            center = jnp.sum(values, axis=0, keepdims=True) / count
            centered = values - center
            spread = jnp.sum(centered * centered, axis=0, keepdims=True) / count
            inverse = lax.rsqrt(spread + EPSILON)
            standardized = centered * inverse
            xhat[c, :, cols] = standardized
            norm[c, :, cols] = standardized.astype(jnp.bfloat16)
            inv[c, 0:1, cols] = inverse
        for bi in range(n_blk):
            share = lax.dot_general(
                norm[c, bi * BLK : (bi + 1) * BLK, :],
                norm[c, bi * BLK :, :],
                (((1,), (1,)), ((), ())),
                preferred_element_type=jnp.float32,
            )
            for bj in range(bi, n_blk):
                at = slice(where[bi, bj] * BLK, (where[bi, bj] + 1) * BLK)
                block = share[:, (bj - bi) * BLK : (bj - bi + 1) * BLK]
                if bi == bj and c == 0:
                    block = block - eye
                if c > 0:
                    block = block + running[at, :]
                if c < n_chunks - 1:
                    running[at, :] = block
                else:
                    packed[at, :] = block.astype(jnp.bfloat16)
        swap = pltpu.make_async_remote_copy(
            src_ref=norm.at[c],
            dst_ref=other.at[c],
            send_sem=swap_send.at[c],
            recv_sem=swap_recv.at[c],
            device_id=(p, 2 * x + 1 - core),
            device_id_type=MESH,
        )
        swaps.append(swap)
        if c < n_chunks - 1:
            swap.start()

    copies = []
    arriving = {}
    for kz in range(1, GROUP + 1):
        zt = (z + kz) % GROUP
        for k in range(1, GROUP):
            q = (g + k) % GROUP
            cp = pltpu.make_async_remote_copy(
                src_ref=packed.at[pl.ds(pl.multiple_of(q * seg + zt * unit, unit), unit), :],
                dst_ref=r1.at[kz - 1, k - 1],
                send_sem=rs1_send.at[kz - 1, k - 1],
                recv_sem=rs1_recv.at[kz - 1, k - 1],
                device_id=(2 * z + q // 2, 2 * (q % 2) + core),
                device_id_type=MESH,
            )
            cp.start()
            arriving[kz, k] = cp
            copies.append(cp)
    swaps[-1].start()
    coming = []
    for kz in range(1, GROUP + 1):
        zt = (z + kz) % GROUP
        total = packed[pl.ds(pl.multiple_of(g * seg + zt * unit, unit), unit), :].astype(
            jnp.float32
        )
        for k in range(1, GROUP):
            arriving[kz, k].wait_recv()
            total = total + r1[kz - 1, k - 1].astype(jnp.float32)
        if kz < GROUP:
            s1[kz - 1] = total.astype(jnp.bfloat16)
            cp = pltpu.make_async_remote_copy(
                src_ref=s1.at[kz - 1],
                dst_ref=r2.at[kz - 1],
                send_sem=rs2_send.at[kz - 1],
                recv_sem=rs2_recv.at[kz - 1],
                device_id=(2 * zt + y, f),
                device_id_type=MESH,
            )
            cp.start()
            coming.append(cp)
    for kz in range(1, GROUP):
        coming[kz - 1].wait_recv()
        total = total + r2[kz - 1].astype(jnp.float32)
    copies += coming
    mine = pl.ds(pl.multiple_of(z * unit, unit), unit)
    gathered[mine, :] = total.astype(jnp.bfloat16)

    coming = []
    for kz in range(1, GROUP):
        zt = (z + kz) % GROUP
        cp = pltpu.make_async_remote_copy(
            src_ref=gathered.at[mine, :],
            dst_ref=gathered.at[mine, :],
            send_sem=ag1_send.at[kz - 1],
            recv_sem=ag1_recv.at[kz - 1],
            device_id=(2 * zt + y, f),
            device_id_type=MESH,
        )
        cp.start()
        coming.append(cp)
    last = []
    for kz in range(GROUP):
        if kz > 0:
            coming[kz - 1].wait_recv()
        zs = (z + GROUP - kz) % GROUP
        for k in range(1, GROUP + 1):
            q = (g + k) % GROUP
            cp = pltpu.make_async_remote_copy(
                src_ref=gathered.at[pl.ds(pl.multiple_of(zs * unit, unit), unit), :],
                dst_ref=full_packed.at[
                    pl.ds(pl.multiple_of(g * seg + zs * unit, unit), unit), :
                ],
                send_sem=ag2_send.at[kz, k - 1],
                recv_sem=ag2_recv.at[kz, k - 1],
                device_id=(2 * z + q // 2, 2 * (q % 2) + 1 - core),
                device_id_type=MESH,
            )
            cp.start()
            last.append(cp)
    copies += coming

    scale = 2.0 * OFF_WEIGHT / count
    for c in range(n_chunks):
        swaps[c].wait_recv()
        own = norm[c].astype(jnp.float32)
        paired = other[c].astype(jnp.float32)
        corr = jnp.sum(own * paired, axis=0, keepdims=True) / count
        diagonal = 2.0 * (corr - 1.0) - 2.0 * OFF_WEIGHT * corr
        base[c] = own * (scale * features) + paired * diagonal
    for cp in last:
        cp.wait_recv()
    for (bi, bj), at in where.items():
        block = full_packed[at * BLK : (at + 1) * BLK, :]
        gram[bi * BLK : (bi + 1) * BLK, bj * BLK : (bj + 1) * BLK] = block
        if bi != bj:
            gram[bj * BLK : (bj + 1) * BLK, bi * BLK : (bi + 1) * BLK] = block.T

    for c in range(n_chunks):
        dnorm = base[c] + scale * lax.dot_general(
            gram[...], norm[c], (((1,), (0,)), ((), ())), preferred_element_type=jnp.float32
        )
        standardized = xhat[c]
        centering = jnp.sum(dnorm, axis=0, keepdims=True) / count
        projection = jnp.sum(dnorm * standardized, axis=0, keepdims=True) / count
        grad[c] = (
            (dnorm - centering - standardized * projection) * inv[c, 0:1, :]
        ).astype(jnp.bfloat16)

        @pl.when(core == 0)
        def _():
            place = pl.ds(pl.multiple_of(g * width + c * chunk, chunk), chunk)
            for k in HOMEWARD:
                to = (p + k) % n_dp
                is_self = jnp.logical_and(to == p, z == f)
                src = grad.at[c, pl.ds(pl.multiple_of(to * rows_a, rows_a), rows_a), :]

                start_or_local(
                    src,
                    ga_ref.at[:, place],
                    out_send.at[c, k - 1],
                    out_recv.at[0],
                    (to, z),
                    is_self,
                )

        @pl.when(core == 1)
        def _():
            place = pl.ds(pl.multiple_of(x * width + c * chunk, chunk), chunk)
            for k in range(1, n_feat + 1):
                to = (f + k) % n_feat
                src = grad.at[c, pl.ds(pl.multiple_of(to * rows_b, rows_b), rows_b), :]
                if k == n_feat:
                    pltpu.make_async_copy(src, gb_ref.at[:, place], out_recv.at[1]).start()
                else:
                    pltpu.make_async_remote_copy(
                        src_ref=src,
                        dst_ref=gb_ref.at[:, place],
                        send_sem=out_send.at[c, k - 1],
                        recv_sem=out_recv.at[1],
                        device_id=(p, to),
                        device_id_type=MESH,
                    ).start()

    for item in sent:
        wait_sent(item)
    for cp in crossing + swaps + copies + last:
        cp.wait_send()

    @pl.when(core == 0)
    def _():
        for c in range(n_chunks):
            for k in range(1, n_dp + 1):
                to = (p + k) % n_dp
                piece = grad.at[c, 0:rows_a, :]

                @pl.when(jnp.logical_not(jnp.logical_and(to == p, z == f)))
                def _():
                    pltpu.make_async_copy(piece, piece, out_send.at[c, k - 1]).wait()

    @pl.when(core == 1)
    def _():
        for c in range(n_chunks):
            for k in range(1, n_feat):
                piece = grad.at[c, 0:rows_b, :]
                pltpu.make_async_copy(piece, piece, out_send.at[c, k - 1]).wait()

    pltpu.make_async_copy(ga_ref, ga_ref, out_recv.at[0]).wait()
    pltpu.make_async_copy(gb_ref, gb_ref, out_recv.at[1]).wait()


def hand_out(landed_a, landed_b, ga_ref, gb_ref, stores):
    first = pltpu.make_async_copy(landed_a, ga_ref, stores.at[0])
    second = pltpu.make_async_copy(landed_b, gb_ref, stores.at[1])
    first.start()
    second.start()
    first.wait()
    second.wait()


def owned_shards(first_view_outputs, second_view_outputs):
    count = first_view_outputs.shape[0] * lax.axis_size("dp")
    features = first_view_outputs.shape[1] * lax.axis_size("feat")
    width = first_view_outputs.shape[1] // GROUP
    chunk = 256 if width % 256 == 0 else 128
    chunks = width // chunk
    n_blk = count // BLK
    packed_rows = n_blk * (n_blk + 1) // 2 * BLK
    seg = packed_rows // GROUP
    unit = seg // GROUP
    bf16, f32 = jnp.bfloat16, jnp.float32
    dma = pltpu.SemaphoreType.DMA
    any_spec = pl.BlockSpec(memory_space=pl.ANY)
    landed = pl.pallas_call(
        functools.partial(kernel, float(features), chunk),
        out_shape=[
            pltpu.VMEM(first_view_outputs.shape, bf16),
            pltpu.VMEM(second_view_outputs.shape, bf16),
        ],
        in_specs=[any_spec] * 2,
        out_specs=[pl.BlockSpec(memory_space=pltpu.VMEM)] * 2,
        scratch_shapes=[
            pltpu.VMEM((chunks, count, chunk), bf16),
            pltpu.VMEM((chunks, count, chunk), f32),
            pltpu.VMEM((chunks, 8, chunk), f32),
            pltpu.VMEM((chunks, count, chunk), bf16),
            pltpu.VMEM((chunks, count, chunk), bf16),
            pltpu.VMEM((chunks, count, chunk), f32),
            pltpu.VMEM((packed_rows, BLK), f32),
            pltpu.VMEM((packed_rows, BLK), bf16),
            pltpu.VMEM((GROUP, GROUP - 1, unit, BLK), bf16),
            pltpu.VMEM((GROUP - 1, unit, BLK), bf16),
            pltpu.VMEM((GROUP - 1, unit, BLK), bf16),
            pltpu.VMEM((seg, BLK), bf16),
            pltpu.VMEM((packed_rows, BLK), bf16),
            pltpu.VMEM((count, count), bf16),
            pltpu.VMEM((chunks, count, chunk), bf16),
            pltpu.VMEM((chunks, 2, first_view_outputs.shape[0], chunk), bf16),
            dma((chunks, GROUP + 2)),
            dma((chunks,)),
            dma((chunks,)),
            dma((chunks,)),
            dma((GROUP, GROUP - 1)),
            dma((GROUP, GROUP - 1)),
            dma((GROUP - 1,)),
            dma((GROUP - 1,)),
            dma((GROUP - 1,)),
            dma((GROUP - 1,)),
            dma((GROUP, GROUP)),
            dma((GROUP, GROUP)),
            dma((chunks, 8)),
            dma((2,)),
            dma((chunks, 2)),
            dma((chunks, 2)),
        ],
        compiler_params=pltpu.CompilerParams(
            collective_id=0, has_side_effects=True, vmem_limit_bytes=60 * 1024 * 1024
        ),
        name="owned_columns",
    )(first_view_outputs, second_view_outputs)
    return pl.pallas_call(
        hand_out,
        out_shape=[
            jax.ShapeDtypeStruct(first_view_outputs.shape, bf16),
            jax.ShapeDtypeStruct(second_view_outputs.shape, bf16),
        ],
        in_specs=[pl.BlockSpec(memory_space=pltpu.VMEM)] * 2,
        out_specs=[any_spec] * 2,
        scratch_shapes=[dma((2,))],
        compiler_params=pltpu.CompilerParams(vmem_limit_bytes=4 * 1024 * 1024),
        name="hand_out",
    )(*landed)


def shards(first_view_outputs, second_view_outputs):
    rows_a, width_a = first_view_outputs.shape
    rows_b, width_b = second_view_outputs.shape
    fits = (
        lax.axis_size("dp") == 8
        and lax.axis_size("feat") == 4
        and rows_a % 16 == 0
        and rows_b == 2 * rows_a
        and width_a == 2 * width_b
        and width_a % (GROUP * BLK) == 0
        and (8 * rows_a) % (4 * BLK) == 0
        and 8 * rows_a <= 1024
    )
    plan = owned_shards if fits else general_shards
    return plan(first_view_outputs, second_view_outputs)


def solution(mesh):
    placed = (P("dp", "feat"), P("feat", "dp"))
    return jax.shard_map(
        shards,
        mesh=mesh,
        in_specs=placed,
        out_specs=(P("dp", "feat"), P("feat", "dp")),
        check_vma=False,
    )
```

```python
import functools
import jax
import jax.numpy as jnp
from jax import lax
from jax.experimental import pallas as pl
from jax.experimental.pallas import tpu as pltpu
from jax.sharding import PartitionSpec as P

EPSILON = 1e-05
OFF_WEIGHT = 0.0051
MESH = pl.DeviceIdType.MESH
BLK = 128
HOMEWARD = (4, 3, 5, 2, 6, 1, 7, 8)
GROUP = 4


def normalize_backward(
    normalized_gradient, standardized_values, inverse_scale, column_sums, total_count
):
    centering_term = column_sums[0] / total_count
    projection_term = column_sums[1] / total_count
    return (
        (normalized_gradient - centering_term - standardized_values * projection_term)
        * inverse_scale
    ).astype(jnp.bfloat16)


def general_shards(first_view_outputs, second_view_outputs):
    rows_a, width_a = first_view_outputs.shape
    rows_b, width_b = second_view_outputs.shape
    total_count = rows_a * lax.axis_size("dp")

    def standardize(values, axis):
        local = values.astype(jnp.float32)
        center = lax.psum(jnp.sum(local, axis=0), axis) / total_count
        centered = local - center
        spread = lax.psum(jnp.sum(centered * centered, axis=0), axis) / total_count
        inverse = lax.rsqrt(spread + EPSILON)
        standardized = centered * inverse
        gathered = lax.all_gather(standardized.astype(jnp.bfloat16), axis, axis=0, tiled=True)
        return standardized, inverse, gathered

    standardized_first, inverse_first, normalized_first = standardize(first_view_outputs, "dp")
    standardized_second, inverse_second, normalized_second = standardize(
        second_view_outputs, "feat"
    )
    correlation = (
        lax.dot_general(
            normalized_first,
            normalized_second,
            (((0,), (0,)), ((), ())),
            preferred_element_type=jnp.float32,
        )
        / total_count
    )
    row_ids = lax.axis_index("feat") * width_a + lax.broadcasted_iota(
        jnp.int32, (width_a, width_b), 0
    )
    col_ids = lax.axis_index("dp") * width_b + lax.broadcasted_iota(
        jnp.int32, (width_a, width_b), 1
    )
    grad_tile = jnp.where(
        row_ids == col_ids, 2.0 * (correlation - 1.0), 2.0 * OFF_WEIGHT * correlation
    ).astype(jnp.bfloat16)

    def finish(partial, axis, standardized, inverse):
        gradient = lax.psum_scatter(
            partial.astype(jnp.bfloat16), axis, scatter_dimension=0, tiled=True
        ).astype(jnp.float32)
        sums = lax.psum(
            (jnp.sum(gradient, axis=0), jnp.sum(gradient * standardized, axis=0)), axis
        )
        return normalize_backward(gradient, standardized, inverse, sums, total_count)

    partial_first = lax.dot_general(
        normalized_second,
        grad_tile,
        (((1,), (1,)), ((), ())),
        preferred_element_type=jnp.float32,
    )
    partial_second = jnp.dot(normalized_first, grad_tile, preferred_element_type=jnp.float32)
    return (
        finish(partial_first, "dp", standardized_first, inverse_first),
        finish(partial_second, "feat", standardized_second, inverse_second),
    )


def kernel(
    features,
    chunk,
    a_ref,
    b_ref,
    ga_ref,
    gb_ref,
    raw,
    xhat,
    inv,
    norm,
    other,
    base,
    running,
    packed,
    r1,
    s1,
    r2,
    gathered,
    full_packed,
    gram,
    grad,
    relay,
    in_send,
    in_recv,
    swap_send,
    swap_recv,
    rs1_send,
    rs1_recv,
    rs2_send,
    rs2_recv,
    ag1_send,
    ag1_recv,
    ag2_send,
    ag2_recv,
    out_send,
    out_recv,
    relay_send,
    relay_recv,
):
    n_dp, n_feat = 8, 4
    n_dev = n_dp * n_feat
    p = lax.axis_index("dp")
    f = lax.axis_index("feat")
    z, y = p // 2, p % 2
    x, core = f // 2, f % 2
    g = 2 * y + x
    rows_a = a_ref.shape[0]
    rows_b = b_ref.shape[0]
    n_chunks, count, _ = raw.shape
    width = n_chunks * chunk
    n_blk = count // BLK
    seg = packed.shape[0] // GROUP
    unit = seg // GROUP

    barrier = pltpu.get_barrier_semaphore()
    for dp_to in reversed(range(n_dp)):
        for feat_to in range(n_feat):

            @pl.when(jnp.logical_or(p != dp_to, f != feat_to))
            def _():
                pl.semaphore_signal(
                    barrier, inc=1, device_id=(dp_to, feat_to), device_id_type=MESH
                )

    pl.semaphore_wait(barrier, n_dev - 1)

    def start_or_local(src, dst, send_sem, recv_sem, device, is_self):
        cp = pltpu.make_async_remote_copy(
            src_ref=src,
            dst_ref=dst,
            send_sem=send_sem,
            recv_sem=recv_sem,
            device_id=device,
            device_id_type=MESH,
        )

        @pl.when(is_self)
        def _():
            pltpu.make_async_copy(src, dst, recv_sem).start()

        @pl.when(jnp.logical_not(is_self))
        def _():
            cp.start()

        return cp, is_self

    def wait_sent(item):
        cp, is_self = item

        @pl.when(jnp.logical_not(is_self))
        def _():
            cp.wait_send()

    def piece_of_a(c, q):
        return a_ref.at[:, pl.ds(pl.multiple_of(q * width + c * chunk, chunk), chunk)]

    def rows_for_a(c):
        return raw.at[c, pl.ds(pl.multiple_of(p * rows_a, rows_a), rows_a), :]

    sent = []
    crossing = []
    straight = []
    relayed = [2] * (n_chunks - 1) + [1]
    for c in range(n_chunks):
        for k in range(relayed[c]):
            cp = pltpu.make_async_remote_copy(
                src_ref=piece_of_a(c, 2 * ((y + 1 + k) % 2) + 1 - x),
                dst_ref=relay.at[c, k],
                send_sem=relay_send.at[c, k],
                recv_sem=relay_recv.at[c, k],
                device_id=(p, 2 * (1 - x) + core),
                device_id_type=MESH,
            )
            cp.start()
            crossing.append(cp)
        for k in range(2):
            y_to = (y + 1 + k) % 2
            dp_to = 2 * f + y_to
            sent.append(
                start_or_local(
                    piece_of_a(c, 2 * y_to + x),
                    rows_for_a(c),
                    in_send.at[c, k],
                    in_recv.at[c],
                    (dp_to, 2 * x),
                    jnp.logical_and(dp_to == p, core == 0),
                )
            )
        for k in range(relayed[c], 2):
            y_to = (y + 1 + k) % 2
            cp = pltpu.make_async_remote_copy(
                src_ref=piece_of_a(c, 2 * y_to + 1 - x),
                dst_ref=rows_for_a(c),
                send_sem=in_send.at[c, 2 + k],
                recv_sem=in_recv.at[c],
                device_id=(2 * f + y_to, 2 * (1 - x)),
                device_id_type=MESH,
            )
            cp.start()
            straight.append(cp)
    for c in range(n_chunks):
        for k in range(2):
            x_to = (x + 1 + k) % 2
            feat_to = 2 * x_to + 1
            sent.append(
                start_or_local(
                    b_ref.at[:, pl.ds(pl.multiple_of(x_to * width + c * chunk, chunk), chunk)],
                    raw.at[c, pl.ds(pl.multiple_of(f * rows_b, rows_b), rows_b), :],
                    in_send.at[c, GROUP + k],
                    in_recv.at[c],
                    (p, feat_to),
                    feat_to == f,
                )
            )
    for c in range(n_chunks):
        for k in range(relayed[c]):
            crossing[sum(relayed[:c]) + k].wait_recv()
            dp_to = 2 * (2 * (1 - x) + core) + (y + 1 + k) % 2
            sent.append(
                start_or_local(
                    relay.at[c, k],
                    rows_for_a(c),
                    in_send.at[c, 2 + k],
                    in_recv.at[c],
                    (dp_to, 2 * x),
                    jnp.logical_and(dp_to == p, core == 0),
                )
            )

    eye = jnp.where(
        lax.broadcasted_iota(jnp.int32, (BLK, BLK), 0)
        == lax.broadcasted_iota(jnp.int32, (BLK, BLK), 1),
        jnp.float32(width),
        jnp.float32(0),
    )
    where = {}
    for bi in range(n_blk):
        for bj in range(bi, n_blk):
            where[bi, bj] = len(where)
    swaps = []
    for c in range(n_chunks):
        pltpu.make_async_copy(raw.at[c], raw.at[c], in_recv.at[c]).wait()
        for h in range(0, chunk, BLK):
            cols = slice(h, h + BLK)
            values = raw[c, :, cols].astype(jnp.float32)
            center = jnp.sum(values, axis=0, keepdims=True) / count
            centered = values - center
            spread = jnp.sum(centered * centered, axis=0, keepdims=True) / count
            inverse = lax.rsqrt(spread + EPSILON)
            standardized = centered * inverse
            xhat[c, :, cols] = standardized
            norm[c, :, cols] = standardized.astype(jnp.bfloat16)
            inv[c, 0:1, cols] = inverse
        for bi in range(n_blk):
            share = lax.dot_general(
                norm[c, bi * BLK : (bi + 1) * BLK, :],
                norm[c, bi * BLK :, :],
                (((1,), (1,)), ((), ())),
                preferred_element_type=jnp.float32,
            )
            for bj in range(bi, n_blk):
                at = slice(where[bi, bj] * BLK, (where[bi, bj] + 1) * BLK)
                block = share[:, (bj - bi) * BLK : (bj - bi + 1) * BLK]
                if bi == bj and c == 0:
                    block = block - eye
                if c > 0:
                    block = block + running[at, :]
                if c < n_chunks - 1:
                    running[at, :] = block
                else:
                    packed[at, :] = block.astype(jnp.bfloat16)
        swap = pltpu.make_async_remote_copy(
            src_ref=norm.at[c],
            dst_ref=other.at[c],
            send_sem=swap_send.at[c],
            recv_sem=swap_recv.at[c],
            device_id=(p, 2 * x + 1 - core),
            device_id_type=MESH,
        )
        swaps.append(swap)
        if c < n_chunks - 1:
            swap.start()

    copies = []
    arriving = {}
    for kz in range(1, GROUP + 1):
        zt = (z + kz) % GROUP
        for k in range(1, GROUP):
            q = (g + k) % GROUP
            cp = pltpu.make_async_remote_copy(
                src_ref=packed.at[pl.ds(pl.multiple_of(q * seg + zt * unit, unit), unit), :],
                dst_ref=r1.at[kz - 1, k - 1],
                send_sem=rs1_send.at[kz - 1, k - 1],
                recv_sem=rs1_recv.at[kz - 1, k - 1],
                device_id=(2 * z + q // 2, 2 * (q % 2) + core),
                device_id_type=MESH,
            )
            cp.start()
            arriving[kz, k] = cp
            copies.append(cp)
    swaps[-1].start()
    coming = []
    for kz in range(1, GROUP + 1):
        zt = (z + kz) % GROUP
        total = packed[pl.ds(pl.multiple_of(g * seg + zt * unit, unit), unit), :].astype(
            jnp.float32
        )
        for k in range(1, GROUP):
            arriving[kz, k].wait_recv()
            total = total + r1[kz - 1, k - 1].astype(jnp.float32)
        if kz < GROUP:
            s1[kz - 1] = total.astype(jnp.bfloat16)
            cp = pltpu.make_async_remote_copy(
                src_ref=s1.at[kz - 1],
                dst_ref=r2.at[kz - 1],
                send_sem=rs2_send.at[kz - 1],
                recv_sem=rs2_recv.at[kz - 1],
                device_id=(2 * zt + y, f),
                device_id_type=MESH,
            )
            cp.start()
            coming.append(cp)
    for kz in range(1, GROUP):
        coming[kz - 1].wait_recv()
        total = total + r2[kz - 1].astype(jnp.float32)
    copies += coming
    mine = pl.ds(pl.multiple_of(z * unit, unit), unit)
    gathered[mine, :] = total.astype(jnp.bfloat16)

    coming = []
    for kz in range(1, GROUP):
        zt = (z + kz) % GROUP
        cp = pltpu.make_async_remote_copy(
            src_ref=gathered.at[mine, :],
            dst_ref=gathered.at[mine, :],
            send_sem=ag1_send.at[kz - 1],
            recv_sem=ag1_recv.at[kz - 1],
            device_id=(2 * zt + y, f),
            device_id_type=MESH,
        )
        cp.start()
        coming.append(cp)
    last = []
    for kz in range(GROUP):
        if kz > 0:
            coming[kz - 1].wait_recv()
        zs = (z + GROUP - kz) % GROUP
        for k in range(1, GROUP + 1):
            q = (g + k) % GROUP
            cp = pltpu.make_async_remote_copy(
                src_ref=gathered.at[pl.ds(pl.multiple_of(zs * unit, unit), unit), :],
                dst_ref=full_packed.at[
                    pl.ds(pl.multiple_of(g * seg + zs * unit, unit), unit), :
                ],
                send_sem=ag2_send.at[kz, k - 1],
                recv_sem=ag2_recv.at[kz, k - 1],
                device_id=(2 * z + q // 2, 2 * (q % 2) + 1 - core),
                device_id_type=MESH,
            )
            cp.start()
            last.append(cp)
    copies += coming

    scale = 2.0 * OFF_WEIGHT / count
    for c in range(n_chunks):
        swaps[c].wait_recv()
        own = norm[c].astype(jnp.float32)
        paired = other[c].astype(jnp.float32)
        corr = jnp.sum(own * paired, axis=0, keepdims=True) / count
        diagonal = 2.0 * (corr - 1.0) - 2.0 * OFF_WEIGHT * corr
        base[c] = own * (scale * features) + paired * diagonal
    for cp in last:
        cp.wait_recv()
    for (bi, bj), at in where.items():
        block = full_packed[at * BLK : (at + 1) * BLK, :]
        gram[bi * BLK : (bi + 1) * BLK, bj * BLK : (bj + 1) * BLK] = block
        if bi != bj:
            gram[bj * BLK : (bj + 1) * BLK, bi * BLK : (bi + 1) * BLK] = block.T

    for c in range(n_chunks):
        dnorm = base[c] + scale * lax.dot_general(
            gram[...], norm[c], (((1,), (0,)), ((), ())), preferred_element_type=jnp.float32
        )
        standardized = xhat[c]
        centering = jnp.sum(dnorm, axis=0, keepdims=True) / count
        projection = jnp.sum(dnorm * standardized, axis=0, keepdims=True) / count
        grad[c] = (
            (dnorm - centering - standardized * projection) * inv[c, 0:1, :]
        ).astype(jnp.bfloat16)

        @pl.when(core == 0)
        def _():
            place = pl.ds(pl.multiple_of(g * width + c * chunk, chunk), chunk)
            for k in HOMEWARD:
                to = (p + k) % n_dp
                is_self = jnp.logical_and(to == p, z == f)
                src = grad.at[c, pl.ds(pl.multiple_of(to * rows_a, rows_a), rows_a), :]

                start_or_local(
                    src,
                    ga_ref.at[:, place],
                    out_send.at[c, k - 1],
                    out_recv.at[0],
                    (to, z),
                    is_self,
                )

        @pl.when(core == 1)
        def _():
            place = pl.ds(pl.multiple_of(x * width + c * chunk, chunk), chunk)
            for k in range(1, n_feat + 1):
                to = (f + k) % n_feat
                src = grad.at[c, pl.ds(pl.multiple_of(to * rows_b, rows_b), rows_b), :]
                if k == n_feat:
                    pltpu.make_async_copy(src, gb_ref.at[:, place], out_recv.at[1]).start()
                else:
                    pltpu.make_async_remote_copy(
                        src_ref=src,
                        dst_ref=gb_ref.at[:, place],
                        send_sem=out_send.at[c, k - 1],
                        recv_sem=out_recv.at[1],
                        device_id=(p, to),
                        device_id_type=MESH,
                    ).start()

    for item in sent:
        wait_sent(item)
    for cp in crossing + straight + swaps + copies + last:
        cp.wait_send()

    @pl.when(core == 0)
    def _():
        for c in range(n_chunks):
            for k in range(1, n_dp + 1):
                to = (p + k) % n_dp
                piece = grad.at[c, 0:rows_a, :]

                @pl.when(jnp.logical_not(jnp.logical_and(to == p, z == f)))
                def _():
                    pltpu.make_async_copy(piece, piece, out_send.at[c, k - 1]).wait()

    @pl.when(core == 1)
    def _():
        for c in range(n_chunks):
            for k in range(1, n_feat):
                piece = grad.at[c, 0:rows_b, :]
                pltpu.make_async_copy(piece, piece, out_send.at[c, k - 1]).wait()

    pltpu.make_async_copy(ga_ref, ga_ref, out_recv.at[0]).wait()
    pltpu.make_async_copy(gb_ref, gb_ref, out_recv.at[1]).wait()


def hand_out(landed_a, landed_b, ga_ref, gb_ref, stores):
    first = pltpu.make_async_copy(landed_a, ga_ref, stores.at[0])
    second = pltpu.make_async_copy(landed_b, gb_ref, stores.at[1])
    first.start()
    second.start()
    first.wait()
    second.wait()


def owned_shards(first_view_outputs, second_view_outputs):
    count = first_view_outputs.shape[0] * lax.axis_size("dp")
    features = first_view_outputs.shape[1] * lax.axis_size("feat")
    width = first_view_outputs.shape[1] // GROUP
    chunk = 256 if width % 256 == 0 else 128
    chunks = width // chunk
    n_blk = count // BLK
    packed_rows = n_blk * (n_blk + 1) // 2 * BLK
    seg = packed_rows // GROUP
    unit = seg // GROUP
    bf16, f32 = jnp.bfloat16, jnp.float32
    dma = pltpu.SemaphoreType.DMA
    any_spec = pl.BlockSpec(memory_space=pl.ANY)
    landed = pl.pallas_call(
        functools.partial(kernel, float(features), chunk),
        out_shape=[
            pltpu.VMEM(first_view_outputs.shape, bf16),
            pltpu.VMEM(second_view_outputs.shape, bf16),
        ],
        in_specs=[any_spec] * 2,
        out_specs=[pl.BlockSpec(memory_space=pltpu.VMEM)] * 2,
        scratch_shapes=[
            pltpu.VMEM((chunks, count, chunk), bf16),
            pltpu.VMEM((chunks, count, chunk), f32),
            pltpu.VMEM((chunks, 8, chunk), f32),
            pltpu.VMEM((chunks, count, chunk), bf16),
            pltpu.VMEM((chunks, count, chunk), bf16),
            pltpu.VMEM((chunks, count, chunk), f32),
            pltpu.VMEM((packed_rows, BLK), f32),
            pltpu.VMEM((packed_rows, BLK), bf16),
            pltpu.VMEM((GROUP, GROUP - 1, unit, BLK), bf16),
            pltpu.VMEM((GROUP - 1, unit, BLK), bf16),
            pltpu.VMEM((GROUP - 1, unit, BLK), bf16),
            pltpu.VMEM((seg, BLK), bf16),
            pltpu.VMEM((packed_rows, BLK), bf16),
            pltpu.VMEM((count, count), bf16),
            pltpu.VMEM((chunks, count, chunk), bf16),
            pltpu.VMEM((chunks, 2, first_view_outputs.shape[0], chunk), bf16),
            dma((chunks, GROUP + 2)),
            dma((chunks,)),
            dma((chunks,)),
            dma((chunks,)),
            dma((GROUP, GROUP - 1)),
            dma((GROUP, GROUP - 1)),
            dma((GROUP - 1,)),
            dma((GROUP - 1,)),
            dma((GROUP - 1,)),
            dma((GROUP - 1,)),
            dma((GROUP, GROUP)),
            dma((GROUP, GROUP)),
            dma((chunks, 8)),
            dma((2,)),
            dma((chunks, 2)),
            dma((chunks, 2)),
        ],
        compiler_params=pltpu.CompilerParams(
            collective_id=0, has_side_effects=True, vmem_limit_bytes=60 * 1024 * 1024
        ),
        name="owned_columns",
    )(first_view_outputs, second_view_outputs)
    return pl.pallas_call(
        hand_out,
        out_shape=[
            jax.ShapeDtypeStruct(first_view_outputs.shape, bf16),
            jax.ShapeDtypeStruct(second_view_outputs.shape, bf16),
        ],
        in_specs=[pl.BlockSpec(memory_space=pltpu.VMEM)] * 2,
        out_specs=[any_spec] * 2,
        scratch_shapes=[dma((2,))],
        compiler_params=pltpu.CompilerParams(vmem_limit_bytes=4 * 1024 * 1024),
        name="hand_out",
    )(*landed)


def shards(first_view_outputs, second_view_outputs):
    rows_a, width_a = first_view_outputs.shape
    rows_b, width_b = second_view_outputs.shape
    fits = (
        lax.axis_size("dp") == 8
        and lax.axis_size("feat") == 4
        and rows_a % 16 == 0
        and rows_b == 2 * rows_a
        and width_a == 2 * width_b
        and width_a % (GROUP * BLK) == 0
        and (8 * rows_a) % (4 * BLK) == 0
        and 8 * rows_a <= 1024
    )
    plan = owned_shards if fits else general_shards
    return plan(first_view_outputs, second_view_outputs)


def solution(mesh):
    placed = (P("dp", "feat"), P("feat", "dp"))
    return jax.shard_map(
        shards,
        mesh=mesh,
        in_specs=placed,
        out_specs=(P("dp", "feat"), P("feat", "dp")),
        check_vma=False,
    )
```

```python
import functools
import jax
import jax.numpy as jnp
from jax import lax
from jax.experimental import pallas as pl
from jax.experimental.pallas import tpu as pltpu
from jax.sharding import PartitionSpec as P

EPSILON = 1e-05
OFF_WEIGHT = 0.0051
MESH = pl.DeviceIdType.MESH
BLK = 128
HOMEWARD = (4, 3, 5, 2, 6, 1, 7, 8)
GROUP = 4


def normalize_backward(
    normalized_gradient, standardized_values, inverse_scale, column_sums, total_count
):
    centering_term = column_sums[0] / total_count
    projection_term = column_sums[1] / total_count
    return (
        (normalized_gradient - centering_term - standardized_values * projection_term)
        * inverse_scale
    ).astype(jnp.bfloat16)


def general_shards(first_view_outputs, second_view_outputs):
    rows_a, width_a = first_view_outputs.shape
    rows_b, width_b = second_view_outputs.shape
    total_count = rows_a * lax.axis_size("dp")

    def standardize(values, axis):
        local = values.astype(jnp.float32)
        center = lax.psum(jnp.sum(local, axis=0), axis) / total_count
        centered = local - center
        spread = lax.psum(jnp.sum(centered * centered, axis=0), axis) / total_count
        inverse = lax.rsqrt(spread + EPSILON)
        standardized = centered * inverse
        gathered = lax.all_gather(standardized.astype(jnp.bfloat16), axis, axis=0, tiled=True)
        return standardized, inverse, gathered

    standardized_first, inverse_first, normalized_first = standardize(first_view_outputs, "dp")
    standardized_second, inverse_second, normalized_second = standardize(
        second_view_outputs, "feat"
    )
    correlation = (
        lax.dot_general(
            normalized_first,
            normalized_second,
            (((0,), (0,)), ((), ())),
            preferred_element_type=jnp.float32,
        )
        / total_count
    )
    row_ids = lax.axis_index("feat") * width_a + lax.broadcasted_iota(
        jnp.int32, (width_a, width_b), 0
    )
    col_ids = lax.axis_index("dp") * width_b + lax.broadcasted_iota(
        jnp.int32, (width_a, width_b), 1
    )
    grad_tile = jnp.where(
        row_ids == col_ids, 2.0 * (correlation - 1.0), 2.0 * OFF_WEIGHT * correlation
    ).astype(jnp.bfloat16)

    def finish(partial, axis, standardized, inverse):
        gradient = lax.psum_scatter(
            partial.astype(jnp.bfloat16), axis, scatter_dimension=0, tiled=True
        ).astype(jnp.float32)
        sums = lax.psum(
            (jnp.sum(gradient, axis=0), jnp.sum(gradient * standardized, axis=0)), axis
        )
        return normalize_backward(gradient, standardized, inverse, sums, total_count)

    partial_first = lax.dot_general(
        normalized_second,
        grad_tile,
        (((1,), (1,)), ((), ())),
        preferred_element_type=jnp.float32,
    )
    partial_second = jnp.dot(normalized_first, grad_tile, preferred_element_type=jnp.float32)
    return (
        finish(partial_first, "dp", standardized_first, inverse_first),
        finish(partial_second, "feat", standardized_second, inverse_second),
    )


def kernel(
    features,
    chunk,
    a_ref,
    b_ref,
    ga_ref,
    gb_ref,
    raw,
    xhat,
    inv,
    norm,
    other,
    base,
    running,
    packed,
    r1,
    s1,
    r2,
    gathered,
    full_packed,
    gram,
    grad,
    relay,
    in_send,
    in_recv,
    swap_send,
    swap_recv,
    rs1_send,
    rs1_recv,
    rs2_send,
    rs2_recv,
    ag1_send,
    ag1_recv,
    ag2_send,
    ag2_recv,
    out_send,
    out_recv,
    relay_send,
    relay_recv,
):
    n_dp, n_feat = 8, 4
    n_dev = n_dp * n_feat
    p = lax.axis_index("dp")
    f = lax.axis_index("feat")
    z, y = p // 2, p % 2
    x, core = f // 2, f % 2
    g = 2 * y + x
    rows_a = a_ref.shape[0]
    rows_b = b_ref.shape[0]
    n_chunks, count, _ = raw.shape
    width = n_chunks * chunk
    n_blk = count // BLK
    seg = packed.shape[0] // GROUP
    unit = seg // GROUP

    barrier = pltpu.get_barrier_semaphore()
    for dp_to in reversed(range(n_dp)):
        for feat_to in range(n_feat):

            @pl.when(jnp.logical_or(p != dp_to, f != feat_to))
            def _():
                pl.semaphore_signal(
                    barrier, inc=1, device_id=(dp_to, feat_to), device_id_type=MESH
                )

    pl.semaphore_wait(barrier, n_dev - 1)

    def start_or_local(src, dst, send_sem, recv_sem, device, is_self):
        cp = pltpu.make_async_remote_copy(
            src_ref=src,
            dst_ref=dst,
            send_sem=send_sem,
            recv_sem=recv_sem,
            device_id=device,
            device_id_type=MESH,
        )

        @pl.when(is_self)
        def _():
            pltpu.make_async_copy(src, dst, recv_sem).start()

        @pl.when(jnp.logical_not(is_self))
        def _():
            cp.start()

        return cp, is_self

    def wait_sent(item):
        cp, is_self = item

        @pl.when(jnp.logical_not(is_self))
        def _():
            cp.wait_send()

    def piece_of_a(c, q):
        return a_ref.at[:, pl.ds(pl.multiple_of(q * width + c * chunk, chunk), chunk)]

    def rows_for_a(c):
        return raw.at[c, pl.ds(pl.multiple_of(p * rows_a, rows_a), rows_a), :]

    sent = []
    crossing = []
    straight = []
    relayed = [2] * (n_chunks - n_chunks // 2) + [1] * (n_chunks // 2)
    for c in range(n_chunks):
        for k in range(relayed[c]):
            cp = pltpu.make_async_remote_copy(
                src_ref=piece_of_a(c, 2 * ((y + 1 + k) % 2) + 1 - x),
                dst_ref=relay.at[c, k],
                send_sem=relay_send.at[c, k],
                recv_sem=relay_recv.at[c, k],
                device_id=(p, 2 * (1 - x) + core),
                device_id_type=MESH,
            )
            cp.start()
            crossing.append(cp)
        for k in range(2):
            y_to = (y + 1 + k) % 2
            dp_to = 2 * f + y_to
            sent.append(
                start_or_local(
                    piece_of_a(c, 2 * y_to + x),
                    rows_for_a(c),
                    in_send.at[c, k],
                    in_recv.at[c],
                    (dp_to, 2 * x),
                    jnp.logical_and(dp_to == p, core == 0),
                )
            )
        for k in range(relayed[c], 2):
            y_to = (y + 1 + k) % 2
            cp = pltpu.make_async_remote_copy(
                src_ref=piece_of_a(c, 2 * y_to + 1 - x),
                dst_ref=rows_for_a(c),
                send_sem=in_send.at[c, 2 + k],
                recv_sem=in_recv.at[c],
                device_id=(2 * f + y_to, 2 * (1 - x)),
                device_id_type=MESH,
            )
            cp.start()
            straight.append(cp)
    for c in range(n_chunks):
        for k in range(2):
            x_to = (x + 1 + k) % 2
            feat_to = 2 * x_to + 1
            sent.append(
                start_or_local(
                    b_ref.at[:, pl.ds(pl.multiple_of(x_to * width + c * chunk, chunk), chunk)],
                    raw.at[c, pl.ds(pl.multiple_of(f * rows_b, rows_b), rows_b), :],
                    in_send.at[c, GROUP + k],
                    in_recv.at[c],
                    (p, feat_to),
                    feat_to == f,
                )
            )
    for c in range(n_chunks):
        for k in range(relayed[c]):
            crossing[sum(relayed[:c]) + k].wait_recv()
            dp_to = 2 * (2 * (1 - x) + core) + (y + 1 + k) % 2
            sent.append(
                start_or_local(
                    relay.at[c, k],
                    rows_for_a(c),
                    in_send.at[c, 2 + k],
                    in_recv.at[c],
                    (dp_to, 2 * x),
                    jnp.logical_and(dp_to == p, core == 0),
                )
            )

    eye = jnp.where(
        lax.broadcasted_iota(jnp.int32, (BLK, BLK), 0)
        == lax.broadcasted_iota(jnp.int32, (BLK, BLK), 1),
        jnp.float32(width),
        jnp.float32(0),
    )
    where = {}
    for bi in range(n_blk):
        for bj in range(bi, n_blk):
            where[bi, bj] = len(where)
    swaps = []
    for c in range(n_chunks):
        pltpu.make_async_copy(raw.at[c], raw.at[c], in_recv.at[c]).wait()
        for h in range(0, chunk, BLK):
            cols = slice(h, h + BLK)
            values = raw[c, :, cols].astype(jnp.float32)
            center = jnp.sum(values, axis=0, keepdims=True) / count
            centered = values - center
            spread = jnp.sum(centered * centered, axis=0, keepdims=True) / count
            inverse = lax.rsqrt(spread + EPSILON)
            standardized = centered * inverse
            xhat[c, :, cols] = standardized
            norm[c, :, cols] = standardized.astype(jnp.bfloat16)
            inv[c, 0:1, cols] = inverse
        for bi in range(n_blk):
            share = lax.dot_general(
                norm[c, bi * BLK : (bi + 1) * BLK, :],
                norm[c, bi * BLK :, :],
                (((1,), (1,)), ((), ())),
                preferred_element_type=jnp.float32,
            )
            for bj in range(bi, n_blk):
                at = slice(where[bi, bj] * BLK, (where[bi, bj] + 1) * BLK)
                block = share[:, (bj - bi) * BLK : (bj - bi + 1) * BLK]
                if bi == bj and c == 0:
                    block = block - eye
                if c > 0:
                    block = block + running[at, :]
                if c < n_chunks - 1:
                    running[at, :] = block
                else:
                    packed[at, :] = block.astype(jnp.bfloat16)
        swap = pltpu.make_async_remote_copy(
            src_ref=norm.at[c],
            dst_ref=other.at[c],
            send_sem=swap_send.at[c],
            recv_sem=swap_recv.at[c],
            device_id=(p, 2 * x + 1 - core),
            device_id_type=MESH,
        )
        swaps.append(swap)
        if c < n_chunks - 1:
            swap.start()

    copies = []
    arriving = {}
    for kz in range(1, GROUP + 1):
        zt = (z + kz) % GROUP
        for k in range(1, GROUP):
            q = (g + k) % GROUP
            cp = pltpu.make_async_remote_copy(
                src_ref=packed.at[pl.ds(pl.multiple_of(q * seg + zt * unit, unit), unit), :],
                dst_ref=r1.at[kz - 1, k - 1],
                send_sem=rs1_send.at[kz - 1, k - 1],
                recv_sem=rs1_recv.at[kz - 1, k - 1],
                device_id=(2 * z + q // 2, 2 * (q % 2) + core),
                device_id_type=MESH,
            )
            cp.start()
            arriving[kz, k] = cp
            copies.append(cp)
    swaps[-1].start()
    coming = []
    for kz in range(1, GROUP + 1):
        zt = (z + kz) % GROUP
        total = packed[pl.ds(pl.multiple_of(g * seg + zt * unit, unit), unit), :].astype(
            jnp.float32
        )
        for k in range(1, GROUP):
            arriving[kz, k].wait_recv()
            total = total + r1[kz - 1, k - 1].astype(jnp.float32)
        if kz < GROUP:
            s1[kz - 1] = total.astype(jnp.bfloat16)
            cp = pltpu.make_async_remote_copy(
                src_ref=s1.at[kz - 1],
                dst_ref=r2.at[kz - 1],
                send_sem=rs2_send.at[kz - 1],
                recv_sem=rs2_recv.at[kz - 1],
                device_id=(2 * zt + y, f),
                device_id_type=MESH,
            )
            cp.start()
            coming.append(cp)
    for kz in range(1, GROUP):
        coming[kz - 1].wait_recv()
        total = total + r2[kz - 1].astype(jnp.float32)
    copies += coming
    mine = pl.ds(pl.multiple_of(z * unit, unit), unit)
    gathered[mine, :] = total.astype(jnp.bfloat16)

    coming = []
    for kz in range(1, GROUP):
        zt = (z + kz) % GROUP
        cp = pltpu.make_async_remote_copy(
            src_ref=gathered.at[mine, :],
            dst_ref=gathered.at[mine, :],
            send_sem=ag1_send.at[kz - 1],
            recv_sem=ag1_recv.at[kz - 1],
            device_id=(2 * zt + y, f),
            device_id_type=MESH,
        )
        cp.start()
        coming.append(cp)
    last = []
    for kz in range(GROUP):
        if kz > 0:
            coming[kz - 1].wait_recv()
        zs = (z + GROUP - kz) % GROUP
        for k in range(1, GROUP + 1):
            q = (g + k) % GROUP
            cp = pltpu.make_async_remote_copy(
                src_ref=gathered.at[pl.ds(pl.multiple_of(zs * unit, unit), unit), :],
                dst_ref=full_packed.at[
                    pl.ds(pl.multiple_of(g * seg + zs * unit, unit), unit), :
                ],
                send_sem=ag2_send.at[kz, k - 1],
                recv_sem=ag2_recv.at[kz, k - 1],
                device_id=(2 * z + q // 2, 2 * (q % 2) + 1 - core),
                device_id_type=MESH,
            )
            cp.start()
            last.append(cp)
    copies += coming

    scale = 2.0 * OFF_WEIGHT / count
    for c in range(n_chunks):
        swaps[c].wait_recv()
        own = norm[c].astype(jnp.float32)
        paired = other[c].astype(jnp.float32)
        corr = jnp.sum(own * paired, axis=0, keepdims=True) / count
        diagonal = 2.0 * (corr - 1.0) - 2.0 * OFF_WEIGHT * corr
        base[c] = own * (scale * features) + paired * diagonal
    for cp in last:
        cp.wait_recv()
    for (bi, bj), at in where.items():
        block = full_packed[at * BLK : (at + 1) * BLK, :]
        gram[bi * BLK : (bi + 1) * BLK, bj * BLK : (bj + 1) * BLK] = block
        if bi != bj:
            gram[bj * BLK : (bj + 1) * BLK, bi * BLK : (bi + 1) * BLK] = block.T

    for c in range(n_chunks):
        dnorm = base[c] + scale * lax.dot_general(
            gram[...], norm[c], (((1,), (0,)), ((), ())), preferred_element_type=jnp.float32
        )
        standardized = xhat[c]
        centering = jnp.sum(dnorm, axis=0, keepdims=True) / count
        projection = jnp.sum(dnorm * standardized, axis=0, keepdims=True) / count
        grad[c] = (
            (dnorm - centering - standardized * projection) * inv[c, 0:1, :]
        ).astype(jnp.bfloat16)

        @pl.when(core == 0)
        def _():
            place = pl.ds(pl.multiple_of(g * width + c * chunk, chunk), chunk)
            for k in HOMEWARD:
                to = (p + k) % n_dp
                is_self = jnp.logical_and(to == p, z == f)
                src = grad.at[c, pl.ds(pl.multiple_of(to * rows_a, rows_a), rows_a), :]

                start_or_local(
                    src,
                    ga_ref.at[:, place],
                    out_send.at[c, k - 1],
                    out_recv.at[0],
                    (to, z),
                    is_self,
                )

        @pl.when(core == 1)
        def _():
            place = pl.ds(pl.multiple_of(x * width + c * chunk, chunk), chunk)
            for k in range(1, n_feat + 1):
                to = (f + k) % n_feat
                src = grad.at[c, pl.ds(pl.multiple_of(to * rows_b, rows_b), rows_b), :]
                if k == n_feat:
                    pltpu.make_async_copy(src, gb_ref.at[:, place], out_recv.at[1]).start()
                else:
                    pltpu.make_async_remote_copy(
                        src_ref=src,
                        dst_ref=gb_ref.at[:, place],
                        send_sem=out_send.at[c, k - 1],
                        recv_sem=out_recv.at[1],
                        device_id=(p, to),
                        device_id_type=MESH,
                    ).start()

    for item in sent:
        wait_sent(item)
    for cp in crossing + straight + swaps + copies + last:
        cp.wait_send()

    @pl.when(core == 0)
    def _():
        for c in range(n_chunks):
            for k in range(1, n_dp + 1):
                to = (p + k) % n_dp
                piece = grad.at[c, 0:rows_a, :]

                @pl.when(jnp.logical_not(jnp.logical_and(to == p, z == f)))
                def _():
                    pltpu.make_async_copy(piece, piece, out_send.at[c, k - 1]).wait()

    @pl.when(core == 1)
    def _():
        for c in range(n_chunks):
            for k in range(1, n_feat):
                piece = grad.at[c, 0:rows_b, :]
                pltpu.make_async_copy(piece, piece, out_send.at[c, k - 1]).wait()

    pltpu.make_async_copy(ga_ref, ga_ref, out_recv.at[0]).wait()
    pltpu.make_async_copy(gb_ref, gb_ref, out_recv.at[1]).wait()


def hand_out(landed_a, landed_b, ga_ref, gb_ref, stores):
    first = pltpu.make_async_copy(landed_a, ga_ref, stores.at[0])
    second = pltpu.make_async_copy(landed_b, gb_ref, stores.at[1])
    first.start()
    second.start()
    first.wait()
    second.wait()


def owned_shards(first_view_outputs, second_view_outputs):
    count = first_view_outputs.shape[0] * lax.axis_size("dp")
    features = first_view_outputs.shape[1] * lax.axis_size("feat")
    width = first_view_outputs.shape[1] // GROUP
    chunk = BLK
    chunks = width // chunk
    n_blk = count // BLK
    packed_rows = n_blk * (n_blk + 1) // 2 * BLK
    seg = packed_rows // GROUP
    unit = seg // GROUP
    bf16, f32 = jnp.bfloat16, jnp.float32
    dma = pltpu.SemaphoreType.DMA
    any_spec = pl.BlockSpec(memory_space=pl.ANY)
    landed = pl.pallas_call(
        functools.partial(kernel, float(features), chunk),
        out_shape=[
            pltpu.VMEM(first_view_outputs.shape, bf16),
            pltpu.VMEM(second_view_outputs.shape, bf16),
        ],
        in_specs=[any_spec] * 2,
        out_specs=[pl.BlockSpec(memory_space=pltpu.VMEM)] * 2,
        scratch_shapes=[
            pltpu.VMEM((chunks, count, chunk), bf16),
            pltpu.VMEM((chunks, count, chunk), f32),
            pltpu.VMEM((chunks, 8, chunk), f32),
            pltpu.VMEM((chunks, count, chunk), bf16),
            pltpu.VMEM((chunks, count, chunk), bf16),
            pltpu.VMEM((chunks, count, chunk), f32),
            pltpu.VMEM((packed_rows, BLK), f32),
            pltpu.VMEM((packed_rows, BLK), bf16),
            pltpu.VMEM((GROUP, GROUP - 1, unit, BLK), bf16),
            pltpu.VMEM((GROUP - 1, unit, BLK), bf16),
            pltpu.VMEM((GROUP - 1, unit, BLK), bf16),
            pltpu.VMEM((seg, BLK), bf16),
            pltpu.VMEM((packed_rows, BLK), bf16),
            pltpu.VMEM((count, count), bf16),
            pltpu.VMEM((chunks, count, chunk), bf16),
            pltpu.VMEM((chunks, 2, first_view_outputs.shape[0], chunk), bf16),
            dma((chunks, GROUP + 2)),
            dma((chunks,)),
            dma((chunks,)),
            dma((chunks,)),
            dma((GROUP, GROUP - 1)),
            dma((GROUP, GROUP - 1)),
            dma((GROUP - 1,)),
            dma((GROUP - 1,)),
            dma((GROUP - 1,)),
            dma((GROUP - 1,)),
            dma((GROUP, GROUP)),
            dma((GROUP, GROUP)),
            dma((chunks, 8)),
            dma((2,)),
            dma((chunks, 2)),
            dma((chunks, 2)),
        ],
        compiler_params=pltpu.CompilerParams(
            collective_id=0, has_side_effects=True, vmem_limit_bytes=60 * 1024 * 1024
        ),
        name="owned_columns",
    )(first_view_outputs, second_view_outputs)
    return pl.pallas_call(
        hand_out,
        out_shape=[
            jax.ShapeDtypeStruct(first_view_outputs.shape, bf16),
            jax.ShapeDtypeStruct(second_view_outputs.shape, bf16),
        ],
        in_specs=[pl.BlockSpec(memory_space=pltpu.VMEM)] * 2,
        out_specs=[any_spec] * 2,
        scratch_shapes=[dma((2,))],
        compiler_params=pltpu.CompilerParams(vmem_limit_bytes=4 * 1024 * 1024),
        name="hand_out",
    )(*landed)


def shards(first_view_outputs, second_view_outputs):
    rows_a, width_a = first_view_outputs.shape
    rows_b, width_b = second_view_outputs.shape
    fits = (
        lax.axis_size("dp") == 8
        and lax.axis_size("feat") == 4
        and rows_a % 16 == 0
        and rows_b == 2 * rows_a
        and width_a == 2 * width_b
        and width_a % (GROUP * BLK) == 0
        and (8 * rows_a) % (4 * BLK) == 0
        and 8 * rows_a <= 1024
    )
    plan = owned_shards if fits else general_shards
    return plan(first_view_outputs, second_view_outputs)


def solution(mesh):
    placed = (P("dp", "feat"), P("feat", "dp"))
    return jax.shard_map(
        shards,
        mesh=mesh,
        in_specs=placed,
        out_specs=(P("dp", "feat"), P("feat", "dp")),
        check_vma=False,
    )
```
